32 devices in a mesh: section: 4 (over y, x), shard: 8 (over z, core).
Axes of the slice: x: 2, y: 2, z: 4, core: 2. Of those that a mesh axis runs over, the one named last changes fastest.
Arguments:
- features: bfloat16 [512, 768], P('shard'), may hold values from -6 to 6
- tile_cols: int32 [4, 4, 16], P('section'), may hold values from 0 to 3
- live_tiles: int32 [4, 4], P('section'), may hold values from 1 to 16, 32 in all within a row
- tile_values: bfloat16 [4, 512, 16, 128], P('section', 'shard'), may hold values from -0.375 to 0.375
- degrees: int32 [4, 512], P('section', 'shard'), may hold values from 1 to 8
Outputs:
- hops: bfloat16 [4, 512, 768], P('section', 'shard')
The draws below stay inside these ranges and needn't reach their ends.
Inputs may be any that keep to these rules, and one draw needn't show every extreme that they name: `live_tiles`: every row block has at least one live tile slot; the live counts of one relation sum to 32.
All inputs are finite; a program needn't handle non-finite values.
Results may differ from the reference program's by a relative error of at most 0.0056.
Values may be sent and summed in bfloat16 or wider, within the bound.
No kernel may reach another device: no remote copies, remote signals or barrier semaphores. Data moves between devices by JAX's collectives and lax.ppermute only.
A program may use at most 64 MiB of HBM per device.

```python
import math
import jax
import jax.numpy as jnp
import numpy as np
from jax import lax

D = 768
TILE = 128
K = 16
NODES = 512
ROW_BLOCKS = 4
N_SECTION = 4


def with_ends(drawn, stream_key, low, top_value):
    extent = drawn.shape
    spot = [jax.random.randint(jax.random.fold_in(stream_key, axis), (), 0, extent[axis]) for axis in range(len(extent))]
    drawn = drawn.at[tuple(spot)].set(low)
    longest = extent.index(max(extent))
    spot[longest] = (spot[longest] + 1) % extent[longest]
    return drawn.at[tuple(spot)].set(top_value)


def levels(rng, extent, split, least, largest):
    loudness, own = 1.0, jax.random.fold_in(rng, 6)
    for axis_at, shards_of in split:
        heights = jnp.exp(jax.random.uniform(jax.random.fold_in(own, axis_at), (shards_of,), jnp.float32, least / len(split), largest / len(split)))
        loudness = loudness * jnp.repeat(heights, extent[axis_at] // shards_of).reshape([-1 if axis == axis_at else 1 for axis in range(len(extent))])
    return loudness


def profile(amount, total, limit, lean):
    loads = [(1 << 20) // math.isqrt(grade ** lean) + 1 for grade in range(2, amount + 1)]
    surplus, given = total - limit - (amount - 1), [1] * (amount - 1)
    while surplus > 0:
        free = [i for i in range(amount - 1) if given[i] < limit]
        mass, budget = sum([loads[i] for i in free]), surplus
        for i in free:
            addition = min(limit - given[i], max(1, budget * loads[i] // mass), surplus)
            given[i] = given[i] + addition
            surplus = surplus - addition
    return np.array([limit] + given)


def ragged_sizes(own_key, count, total, bound, skew):
    if count == 2:
        one = jax.random.randint(own_key, (), max(1, total - bound), min(bound, total - 1) + 1)
        return jnp.stack([one, total - one])
    sizes = jnp.asarray(profile(count, total, bound, skew), jnp.int32)
    pairs = (count - 1) // 2
    giver, taker = sizes[1:1 + 2 * pairs:2], sizes[2:2 + 2 * pairs:2]
    room = jnp.minimum(giver - 1, bound - taker)
    moved = jax.random.randint(jax.random.fold_in(own_key, 1), (pairs,), 0, 1 << 20) % (room + 1)
    sizes = sizes.at[1:1 + 2 * pairs:2].set(giver - moved).at[2:2 + 2 * pairs:2].set(taker + moved)
    return sizes[jax.random.permutation(jax.random.fold_in(own_key, 2), count)]


def noise(stream_key, shape, width, bound, pieces=(), held_as=jnp.bfloat16):
    values = width * jax.random.normal(stream_key, shape, jnp.float32)
    if pieces:
        values = values * levels(stream_key, shape, pieces, -0.22, 0.18)
    return jnp.clip(values, -bound, bound).astype(held_as)


def setup_inputs(seed: int = 0) -> dict:
    key_list = jax.random.split(jax.random.key(seed), 6)
    features = noise(key_list[0], (NODES, D), 1.0, 6.0, ((0, 8),))
    tile_cols = with_ends(jax.random.randint(key_list[1], (N_SECTION, ROW_BLOCKS, K), 0, ROW_BLOCKS), jax.random.fold_in(key_list[1], 1), 0, ROW_BLOCKS - 1).astype(jnp.int32)
    live_tiles = jax.vmap(lambda own: ragged_sizes(own, ROW_BLOCKS, ROW_BLOCKS * K // 2, K, 2))(jax.random.split(key_list[2], N_SECTION)).reshape((N_SECTION, ROW_BLOCKS)).astype(jnp.int32)
    tile_values = noise(key_list[3], (N_SECTION, NODES, K, TILE), (K * TILE // 8) ** -0.5, 0.375, ((0, 4), (1, 8)))
    degrees = with_ends(jax.random.randint(key_list[4], (N_SECTION, NODES), 1, 9), jax.random.fold_in(key_list[4], 1), 1, 8).astype(jnp.int32)
    return {"features": features, "tile_cols": tile_cols, "live_tiles": live_tiles, "tile_values": tile_values, "degrees": degrees}


def reference(features, tile_cols, live_tiles, tile_values, degrees):
    previous = features
    collected = []
    for section in range(N_SECTION):
        blocks = previous.reshape(ROW_BLOCKS, TILE, D)

        def one_block(block_row):
            block_ids = tile_cols[section, block_row]
            source = blocks[block_ids].astype(jnp.float32)
            tile_rows = lax.dynamic_slice_in_dim(tile_values[section], block_row * TILE, TILE, 0).astype(jnp.float32)
            live_mask = (jnp.arange(K, dtype=jnp.int32) < live_tiles[section, block_row]).astype(jnp.float32)
            return jnp.einsum('rkc,kcd->rd', tile_rows * live_mask[None, :, None], source)
        summed = lax.map(one_block, jnp.arange(ROW_BLOCKS, dtype=jnp.int32)).reshape(NODES, D)
        row_scale = lax.rsqrt(degrees[section].astype(jnp.float32))
        previous = (summed * row_scale[:, None]).astype(jnp.bfloat16)
        collected.append(previous)
    return jnp.stack(collected)
```

```python
import jax
import jax.numpy as jnp
from jax import lax
from jax.experimental import pallas as pl
from jax.experimental.pallas import tpu as pltpu
from jax.sharding import PartitionSpec as P


def dense_rows_kernel(cols_ref, live_ref, tiles_ref, degrees_ref, rows_ref):
    row_count, slots, tile_size = tiles_ref.shape
    blocks = rows_ref.shape[1] // tile_size
    block_row = lax.axis_index("shard") * row_count // tile_size
    live = live_ref[0, block_row]
    wide = row_count * slots
    place = lax.broadcasted_iota(jnp.int32, (row_count, wide), 1)
    slot = lax.rem(place, slots)
    mine = lax.broadcasted_iota(jnp.int32, (row_count, wide), 0) == lax.div(place, slots)
    column = jnp.full((row_count, wide), -1, jnp.int32)
    for k in range(slots):
        column = jnp.where((slot == k) & mine & (k < live), cols_ref[0, block_row, k], column)
    tiles = tiles_ref[...].reshape(wide, tile_size)
    degree = jnp.broadcast_to(degrees_ref[...].astype(jnp.float32), (row_count, row_count))
    diagonal = lax.broadcasted_iota(jnp.int32, (row_count, row_count), 0) == lax.broadcasted_iota(
        jnp.int32, (row_count, row_count), 1
    )
    scale = lax.rsqrt(jnp.sum(jnp.where(diagonal, degree, 0.0), axis=1, keepdims=True))
    for b in range(blocks):
        pick = (column == b).astype(jnp.bfloat16)
        summed = jnp.dot(pick, tiles, preferred_element_type=jnp.float32)
        rows_ref[:, b * tile_size : (b + 1) * tile_size] = (summed * scale).astype(jnp.bfloat16)


def dense_rows(tile_cols, live_tiles, tile_rows, degrees, nodes):
    row_count = tile_rows.shape[0]
    return pl.pallas_call(
        dense_rows_kernel,
        out_shape=jax.ShapeDtypeStruct((row_count, nodes), jnp.bfloat16),
        in_specs=[
            pl.BlockSpec(memory_space=pltpu.SMEM),
            pl.BlockSpec(memory_space=pltpu.SMEM),
            pl.BlockSpec(memory_space=pltpu.VMEM),
            pl.BlockSpec(memory_space=pltpu.VMEM),
        ],
        out_specs=pl.BlockSpec(memory_space=pltpu.VMEM),
        name="dense_rows",
    )(tile_cols, live_tiles, tile_rows, degrees)


def chain_kernel(own_ref, relations_ref, slab_ref, out_ref, halves):
    row_count = own_ref.shape[0]
    section = lax.axis_index("section")
    halves[:row_count] = own_ref[...]
    halves[row_count:] = jnp.zeros_like(own_ref)

    def times(i, carry):
        both = jnp.dot(halves[...], relations_ref[section - 1 - i], preferred_element_type=jnp.float32)
        product = both[:row_count] + both[row_count:]
        high = product.astype(jnp.bfloat16)
        halves[:row_count] = high
        halves[row_count:] = (product - high.astype(jnp.float32)).astype(jnp.bfloat16)
        return carry

    lax.fori_loop(0, section, times, 0)
    both = jnp.dot(halves[...], slab_ref[...], preferred_element_type=jnp.float32)
    out_ref[...] = (both[:row_count] + both[row_count:]).astype(jnp.bfloat16)


def chain(own, relations, slab):
    row_count, nodes = own.shape
    return pl.pallas_call(
        chain_kernel,
        out_shape=jax.ShapeDtypeStruct((row_count, slab.shape[1]), jnp.bfloat16),
        in_specs=[pl.BlockSpec(memory_space=pltpu.VMEM)] * 3,
        out_specs=pl.BlockSpec(memory_space=pltpu.VMEM),
        scratch_shapes=[pltpu.VMEM((2 * row_count, nodes), jnp.bfloat16)],
        compiler_params=pltpu.CompilerParams(vmem_limit_bytes=32 * 1024 * 1024),
        name="chain",
    )(own, relations, slab)


def by_products(features, own):
    sections = lax.axis_size("section")
    nodes = own.shape[1]
    slab = lax.all_gather(features, "shard", axis=0, tiled=True)
    relations = lax.all_gather(own, ("section", "shard"), axis=0, tiled=True)
    return chain(own, relations.reshape(sections, nodes, nodes), slab)


def by_hops(features, own):
    sections = lax.axis_size("section")
    section = lax.axis_index("section")
    step = [(i, i + 1) for i in range(sections - 1)]
    result = jnp.zeros_like(features)
    arrived = features
    for hop in range(sections):
        slab = lax.all_gather(arrived, "shard", axis=0, tiled=True)
        output = jnp.dot(own, slab, preferred_element_type=jnp.float32).astype(jnp.bfloat16)
        result = jnp.where(section == hop, output, result)
        arrived = lax.ppermute(output, "section", step)
    return result


def per_device(features, tile_cols, live_tiles, tile_values, degrees):
    nodes = features.shape[0] * lax.axis_size("shard")
    own = dense_rows(tile_cols, live_tiles, tile_values[0], degrees, nodes)
    plan = by_products if nodes <= features.shape[1] else by_hops
    return plan(features, own)[None]


def solution(mesh):
    in_specs = (
        P("shard", None),
        P("section", None, None),
        P("section", None),
        P("section", "shard", None, None),
        P("section", "shard"),
    )
    out_specs = P("section", "shard", None)
    return jax.shard_map(
        per_device, mesh=mesh, in_specs=in_specs, out_specs=out_specs, check_vma=False
    )
```

```python
import jax
import jax.numpy as jnp
from jax import lax
from jax.experimental import pallas as pl
from jax.experimental.pallas import tpu as pltpu
from jax.sharding import PartitionSpec as P


def dense_rows_kernel(cols_ref, live_ref, tiles_ref, degrees_ref, rows_ref):
    row_count, slots, tile_size = tiles_ref.shape
    blocks = rows_ref.shape[1] // tile_size
    block_row = lax.axis_index("shard") * row_count // tile_size
    live = live_ref[0, block_row]
    wide = row_count * slots
    place = lax.broadcasted_iota(jnp.int32, (row_count, wide), 1)
    slot = lax.rem(place, slots)
    mine = lax.broadcasted_iota(jnp.int32, (row_count, wide), 0) == lax.div(place, slots)
    column = jnp.full((row_count, wide), -1, jnp.int32)
    for k in range(slots):
        column = jnp.where((slot == k) & mine & (k < live), cols_ref[0, block_row, k], column)
    tiles = tiles_ref[...].reshape(wide, tile_size)
    degree = jnp.broadcast_to(degrees_ref[...].astype(jnp.float32), (row_count, row_count))
    diagonal = lax.broadcasted_iota(jnp.int32, (row_count, row_count), 0) == lax.broadcasted_iota(
        jnp.int32, (row_count, row_count), 1
    )
    scale = lax.rsqrt(jnp.sum(jnp.where(diagonal, degree, 0.0), axis=1, keepdims=True))
    for b in range(blocks):
        pick = (column == b).astype(jnp.bfloat16)
        summed = jnp.dot(pick, tiles, preferred_element_type=jnp.float32)
        rows_ref[:, b * tile_size : (b + 1) * tile_size] = (summed * scale).astype(jnp.bfloat16)


def dense_rows(tile_cols, live_tiles, tile_rows, degrees, nodes):
    row_count = tile_rows.shape[0]
    return pl.pallas_call(
        dense_rows_kernel,
        out_shape=jax.ShapeDtypeStruct((row_count, nodes), jnp.bfloat16),
        in_specs=[
            pl.BlockSpec(memory_space=pltpu.SMEM),
            pl.BlockSpec(memory_space=pltpu.SMEM),
            pl.BlockSpec(memory_space=pltpu.VMEM),
            pl.BlockSpec(memory_space=pltpu.VMEM),
        ],
        out_specs=pl.BlockSpec(memory_space=pltpu.VMEM),
        name="dense_rows",
    )(tile_cols, live_tiles, tile_rows, degrees)


def per_device(features, tile_cols, live_tiles, tile_values, degrees):
    sections = lax.axis_size("section")
    part = features.shape[1] // sections
    row_count = features.shape[0]
    nodes = row_count * lax.axis_size("shard")
    piece = lax.dynamic_slice_in_dim(features, lax.axis_index("section") * part, part, axis=1)
    own = dense_rows(tile_cols, live_tiles, tile_values[0], degrees, nodes)
    relations = lax.all_gather(own, "section", axis=0, tiled=False)
    pieces = []
    for hop in range(sections):
        slab = lax.all_gather(piece, "shard", axis=0, tiled=True)
        piece = jnp.dot(relations[hop], slab, preferred_element_type=jnp.float32).astype(jnp.bfloat16)
        pieces.append(piece)
    mine = lax.all_to_all(jnp.stack(pieces), "section", split_axis=0, concat_axis=0, tiled=True)
    return jnp.swapaxes(mine, 0, 1).reshape(row_count, sections * part)[None]


def solution(mesh):
    in_specs = (
        P("shard", None),
        P("section", None, None),
        P("section", None),
        P("section", "shard", None, None),
        P("section", "shard"),
    )
    out_specs = P("section", "shard", None)
    return jax.shard_map(
        per_device, mesh=mesh, in_specs=in_specs, out_specs=out_specs, check_vma=False
    )
```

```python
import jax
import jax.numpy as jnp
from jax import lax
from jax.experimental import pallas as pl
from jax.experimental.pallas import tpu as pltpu
from jax.sharding import PartitionSpec as P


def dense_rows_kernel(cols_ref, live_ref, tiles_ref, degrees_ref, rows_ref):
    row_count, slots, tile_size = tiles_ref.shape
    blocks = rows_ref.shape[1] // tile_size
    block_row = lax.axis_index("shard") * row_count // tile_size
    live = live_ref[0, block_row]
    wide = row_count * slots
    place = lax.broadcasted_iota(jnp.int32, (row_count, wide), 1)
    slot = lax.rem(place, slots)
    mine = lax.broadcasted_iota(jnp.int32, (row_count, wide), 0) == lax.div(place, slots)
    column = jnp.full((row_count, wide), -1, jnp.int32)
    for k in range(slots):
        column = jnp.where((slot == k) & mine & (k < live), cols_ref[0, block_row, k], column)
    tiles = tiles_ref[...].reshape(wide, tile_size)
    degree = jnp.broadcast_to(degrees_ref[...].astype(jnp.float32), (row_count, row_count))
    diagonal = lax.broadcasted_iota(jnp.int32, (row_count, row_count), 0) == lax.broadcasted_iota(
        jnp.int32, (row_count, row_count), 1
    )
    scale = lax.rsqrt(jnp.sum(jnp.where(diagonal, degree, 0.0), axis=1, keepdims=True))
    for b in range(blocks):
        pick = (column == b).astype(jnp.bfloat16)
        summed = jnp.dot(pick, tiles, preferred_element_type=jnp.float32)
        rows_ref[:, b * tile_size : (b + 1) * tile_size] = (summed * scale).astype(jnp.bfloat16)


def dense_rows(tile_cols, live_tiles, tile_rows, degrees, nodes):
    row_count = tile_rows.shape[0]
    return pl.pallas_call(
        dense_rows_kernel,
        out_shape=jax.ShapeDtypeStruct((row_count, nodes), jnp.bfloat16),
        in_specs=[
            pl.BlockSpec(memory_space=pltpu.SMEM),
            pl.BlockSpec(memory_space=pltpu.SMEM),
            pl.BlockSpec(memory_space=pltpu.VMEM),
            pl.BlockSpec(memory_space=pltpu.VMEM),
        ],
        out_specs=pl.BlockSpec(memory_space=pltpu.VMEM),
        name="dense_rows",
    )(tile_cols, live_tiles, tile_rows, degrees)


def chain_kernel(own_ref, gathered_ref, out_ref, halves):
    row_count, nodes = own_ref.shape
    width = out_ref.shape[1]
    section = lax.axis_index("section")
    halves[:row_count] = own_ref[...]
    halves[row_count:] = jnp.zeros_like(own_ref)

    def times(i, carry):
        columns = pl.ds(pl.multiple_of((section - 1 - i) * nodes, 128), nodes)
        both = jnp.dot(halves[...], gathered_ref[:, columns], preferred_element_type=jnp.float32)
        product = both[:row_count] + both[row_count:]
        high = product.astype(jnp.bfloat16)
        halves[:row_count] = high
        halves[row_count:] = (product - high.astype(jnp.float32)).astype(jnp.bfloat16)
        return carry

    lax.fori_loop(0, section, times, 0)
    slab = gathered_ref[:, gathered_ref.shape[1] - width :]
    both = jnp.dot(halves[...], slab, preferred_element_type=jnp.float32)
    out_ref[...] = (both[:row_count] + both[row_count:]).astype(jnp.bfloat16)


def chain(own, gathered, width):
    row_count, nodes = own.shape
    return pl.pallas_call(
        chain_kernel,
        out_shape=jax.ShapeDtypeStruct((row_count, width), jnp.bfloat16),
        in_specs=[pl.BlockSpec(memory_space=pltpu.VMEM)] * 2,
        out_specs=pl.BlockSpec(memory_space=pltpu.VMEM),
        scratch_shapes=[pltpu.VMEM((2 * row_count, nodes), jnp.bfloat16)],
        compiler_params=pltpu.CompilerParams(vmem_limit_bytes=32 * 1024 * 1024),
        name="chain",
    )(own, gathered)


def by_products(features, own):
    sections = lax.axis_size("section")
    relations = lax.all_gather(own, "section", axis=0, tiled=False)
    payload = jnp.concatenate([relations[s] for s in range(sections - 1)] + [features], axis=1)
    gathered = lax.all_gather(payload, "shard", axis=0, tiled=True)
    return chain(own, gathered, features.shape[1])


def by_hops(features, own):
    sections = lax.axis_size("section")
    part = features.shape[1] // sections
    piece = lax.dynamic_slice_in_dim(features, lax.axis_index("section") * part, part, axis=1)
    relations = lax.all_gather(own, "section", axis=0, tiled=False)
    pieces = []
    for hop in range(sections):
        slab = lax.all_gather(piece, "shard", axis=0, tiled=True)
        piece = jnp.dot(relations[hop], slab, preferred_element_type=jnp.float32).astype(jnp.bfloat16)
        pieces.append(piece)
    mine = lax.all_to_all(jnp.stack(pieces), "section", split_axis=0, concat_axis=0, tiled=True)
    return jnp.swapaxes(mine, 0, 1).reshape(features.shape)


def per_device(features, tile_cols, live_tiles, tile_values, degrees):
    nodes = features.shape[0] * lax.axis_size("shard")
    own = dense_rows(tile_cols, live_tiles, tile_values[0], degrees, nodes)
    plan = by_products if nodes <= features.shape[1] else by_hops
    return plan(features, own)[None]


def solution(mesh):
    in_specs = (
        P("shard", None),
        P("section", None, None),
        P("section", None),
        P("section", "shard", None, None),
        P("section", "shard"),
    )
    out_specs = P("section", "shard", None)
    return jax.shard_map(
        per_device, mesh=mesh, in_specs=in_specs, out_specs=out_specs, check_vma=False
    )
```

```python
import jax
import jax.numpy as jnp
from jax import lax
from jax.experimental import pallas as pl
from jax.experimental.pallas import tpu as pltpu
from jax.sharding import PartitionSpec as P


def dense_rows_kernel(cols_ref, live_ref, tiles_ref, degrees_ref, features_ref, rows_ref):
    row_count, slots, tile_size = tiles_ref.shape
    nodes = row_count * lax.axis_size("shard")
    blocks = nodes // tile_size
    share = rows_ref.shape[1] - nodes
    block_row = lax.axis_index("shard") * row_count // tile_size
    live = live_ref[0, block_row]
    wide = row_count * slots
    place = lax.broadcasted_iota(jnp.int32, (row_count, wide), 1)
    slot = lax.rem(place, slots)
    mine = lax.broadcasted_iota(jnp.int32, (row_count, wide), 0) == lax.div(place, slots)
    column = jnp.full((row_count, wide), -1, jnp.int32)
    for k in range(slots):
        column = jnp.where((slot == k) & mine & (k < live), cols_ref[0, block_row, k], column)
    tiles = tiles_ref[...].reshape(wide, tile_size)
    degree = jnp.broadcast_to(degrees_ref[...].astype(jnp.float32), (row_count, row_count))
    diagonal = lax.broadcasted_iota(jnp.int32, (row_count, row_count), 0) == lax.broadcasted_iota(
        jnp.int32, (row_count, row_count), 1
    )
    scale = lax.rsqrt(jnp.sum(jnp.where(diagonal, degree, 0.0), axis=1, keepdims=True))
    for b in range(blocks):
        pick = (column == b).astype(jnp.bfloat16)
        summed = jnp.dot(pick, tiles, preferred_element_type=jnp.float32)
        rows_ref[:, b * tile_size : (b + 1) * tile_size] = (summed * scale).astype(jnp.bfloat16)
    if share:
        shares = features_ref.shape[1] // share
        first = pl.multiple_of(lax.rem(lax.axis_index("section"), shares) * share, 128)
        rows_ref[:, nodes:] = features_ref[:, pl.ds(first, share)]


def dense_rows(tile_cols, live_tiles, tile_rows, degrees, features, share):
    row_count = tile_rows.shape[0]
    nodes = row_count * lax.axis_size("shard")
    return pl.pallas_call(
        dense_rows_kernel,
        out_shape=jax.ShapeDtypeStruct((row_count, nodes + share), jnp.bfloat16),
        in_specs=[pl.BlockSpec(memory_space=pltpu.SMEM)] * 2 + [pl.BlockSpec(memory_space=pltpu.VMEM)] * 3,
        out_specs=pl.BlockSpec(memory_space=pltpu.VMEM),
        name="dense_rows",
    )(tile_cols, live_tiles, tile_rows, degrees, features)


def chain_kernel(own_ref, here_ref, there_ref, out_ref, halves):
    chips, relations, row_count, both_widths = here_ref.shape
    nodes = 2 * chips * row_count
    share = both_widths - nodes
    section = lax.axis_index("section")

    def run(even_ref, odd_ref):
        def rows_of(relation, columns):
            parts = []
            for chip in range(chips):
                parts += [even_ref[chip, relation, :, columns], odd_ref[chip, relation, :, columns]]
            return jnp.concatenate(parts, axis=0)

        halves[:row_count] = own_ref[:, :nodes]
        halves[row_count:] = jnp.zeros((row_count, nodes), jnp.bfloat16)

        def times(i, carry):
            matrix = rows_of(section - 1 - i, slice(0, nodes))
            both = jnp.dot(halves[...], matrix, preferred_element_type=jnp.float32)
            product = both[:row_count] + both[row_count:]
            high = product.astype(jnp.bfloat16)
            halves[:row_count] = high
            halves[row_count:] = (product - high.astype(jnp.float32)).astype(jnp.bfloat16)
            return carry

        lax.fori_loop(0, section, times, 0)
        for part in range(relations):
            slab = rows_of(part, slice(nodes, both_widths))
            both = jnp.dot(halves[...], slab, preferred_element_type=jnp.float32)
            out_ref[:, part * share : (part + 1) * share] = (both[:row_count] + both[row_count:]).astype(jnp.bfloat16)

    core = lax.rem(lax.axis_index("shard"), 2)
    pl.when(core == 0)(lambda: run(here_ref, there_ref))
    pl.when(core == 1)(lambda: run(there_ref, here_ref))


def chain(own, here, there, width):
    row_count = own.shape[0]
    nodes = row_count * lax.axis_size("shard")
    return pl.pallas_call(
        chain_kernel,
        out_shape=jax.ShapeDtypeStruct((row_count, width), jnp.bfloat16),
        in_specs=[pl.BlockSpec(memory_space=pltpu.VMEM)] * 3,
        out_specs=pl.BlockSpec(memory_space=pltpu.VMEM),
        scratch_shapes=[pltpu.VMEM((2 * row_count, nodes), jnp.bfloat16)],
        compiler_params=pltpu.CompilerParams(vmem_limit_bytes=32 * 1024 * 1024),
        name="chain",
    )(own, here, there)


def by_products(own, width):
    sections, shards = lax.axis_size("section"), lax.axis_size("shard")
    relations = lax.all_gather(own, "section", axis=0, tiled=False)[: sections - 1]
    same_core = [list(range(core, shards, 2)) for core in range(2)]
    here = lax.all_gather(relations, "shard", axis=0, tiled=False, axis_index_groups=same_core)
    there = lax.ppermute(here, "shard", [(i, i ^ 1) for i in range(shards)])
    return chain(own, here, there, width)


def by_hops(features, own):
    sections = lax.axis_size("section")
    part = features.shape[1] // sections
    piece = lax.dynamic_slice_in_dim(features, lax.axis_index("section") * part, part, axis=1)
    relations = lax.all_gather(own, "section", axis=0, tiled=False)
    pieces = []
    for hop in range(sections):
        slab = lax.all_gather(piece, "shard", axis=0, tiled=True)
        piece = jnp.dot(relations[hop], slab, preferred_element_type=jnp.float32).astype(jnp.bfloat16)
        pieces.append(piece)
    mine = lax.all_to_all(jnp.stack(pieces), "section", split_axis=0, concat_axis=0, tiled=True)
    return jnp.swapaxes(mine, 0, 1).reshape(features.shape)


def per_device(features, tile_cols, live_tiles, tile_values, degrees):
    row_count, width = features.shape
    sections = lax.axis_size("section")
    products = row_count * lax.axis_size("shard") <= width and width % (sections - 1) == 0
    share = width // (sections - 1) if products else 0
    own = dense_rows(tile_cols, live_tiles, tile_values[0], degrees, features, share)
    out = by_products(own, width) if products else by_hops(features, own)
    return out[None]


def solution(mesh):
    in_specs = (
        P("shard", None),
        P("section", None, None),
        P("section", None),
        P("section", "shard", None, None),
        P("section", "shard"),
    )
    out_specs = P("section", "shard", None)
    return jax.shard_map(
        per_device, mesh=mesh, in_specs=in_specs, out_specs=out_specs, check_vma=False
    )
```

```python
import jax
import jax.numpy as jnp
from jax import lax
from jax.experimental import pallas as pl
from jax.experimental.pallas import tpu as pltpu
from jax.sharding import PartitionSpec as P


def dense_rows_kernel(cols_ref, live_ref, tiles_ref, degrees_ref, rows_ref):
    row_count, slots, tile_size = tiles_ref.shape
    blocks = rows_ref.shape[1] // tile_size
    block_row = lax.axis_index("shard") * row_count // tile_size
    live = live_ref[0, block_row]
    wide = row_count * slots
    place = lax.broadcasted_iota(jnp.int32, (row_count, wide), 1)
    slot = lax.rem(place, slots)
    mine = lax.broadcasted_iota(jnp.int32, (row_count, wide), 0) == lax.div(place, slots)
    column = jnp.full((row_count, wide), -1, jnp.int32)
    for k in range(slots):
        column = jnp.where((slot == k) & mine & (k < live), cols_ref[0, block_row, k], column)
    tiles = tiles_ref[...].reshape(wide, tile_size)
    degree = jnp.broadcast_to(degrees_ref[...].astype(jnp.float32), (row_count, row_count))
    diagonal = lax.broadcasted_iota(jnp.int32, (row_count, row_count), 0) == lax.broadcasted_iota(
        jnp.int32, (row_count, row_count), 1
    )
    scale = lax.rsqrt(jnp.sum(jnp.where(diagonal, degree, 0.0), axis=1, keepdims=True))
    for b in range(blocks):
        pick = (column == b).astype(jnp.bfloat16)
        summed = jnp.dot(pick, tiles, preferred_element_type=jnp.float32)
        rows_ref[:, b * tile_size : (b + 1) * tile_size] = (summed * scale).astype(jnp.bfloat16)


def dense_rows(tile_cols, live_tiles, tile_rows, degrees, nodes):
    row_count = tile_rows.shape[0]
    return pl.pallas_call(
        dense_rows_kernel,
        out_shape=jax.ShapeDtypeStruct((row_count, nodes), jnp.bfloat16),
        in_specs=[
            pl.BlockSpec(memory_space=pltpu.SMEM),
            pl.BlockSpec(memory_space=pltpu.SMEM),
            pl.BlockSpec(memory_space=pltpu.VMEM),
            pl.BlockSpec(memory_space=pltpu.VMEM),
        ],
        out_specs=pl.BlockSpec(memory_space=pltpu.VMEM),
        name="dense_rows",
    )(tile_cols, live_tiles, tile_rows, degrees)


def chain_kernel(own_ref, here_ref, there_ref, slab_here_ref, slab_there_ref, out_ref, halves):
    chips, _, row_count, nodes = here_ref.shape
    section, shard = lax.axis_index("section"), lax.axis_index("shard")
    chip, core = lax.div(shard, 2), lax.rem(shard, 2)

    def run(even_ref, odd_ref, slab_even_ref, slab_odd_ref):
        halves[:row_count] = own_ref[...]
        halves[row_count:] = jnp.zeros((row_count, nodes), jnp.bfloat16)

        def times(i, carry):
            parts = []
            for at in range(chips):
                parts += [even_ref[at, section - 1 - i], odd_ref[at, section - 1 - i]]
            both = jnp.dot(halves[...], jnp.concatenate(parts, axis=0), preferred_element_type=jnp.float32)
            product = both[:row_count] + both[row_count:]
            high = product.astype(jnp.bfloat16)
            halves[:row_count] = high
            halves[row_count:] = (product - high.astype(jnp.float32)).astype(jnp.bfloat16)
            return carry

        lax.fori_loop(0, section, times, 0)
        parts = []
        for at in range(chips):
            back = lax.rem(chip - at + chips, chips)
            parts += [slab_even_ref[back], slab_odd_ref[back]]
        both = jnp.dot(halves[...], jnp.concatenate(parts, axis=0), preferred_element_type=jnp.float32)
        out_ref[...] = (both[:row_count] + both[row_count:]).astype(jnp.bfloat16)

    pl.when(core == 0)(lambda: run(here_ref, there_ref, slab_here_ref, slab_there_ref))
    pl.when(core == 1)(lambda: run(there_ref, here_ref, slab_there_ref, slab_here_ref))


def chain(own, here, there, slab_here, slab_there):
    row_count, nodes = own.shape
    return pl.pallas_call(
        chain_kernel,
        out_shape=jax.ShapeDtypeStruct((row_count, slab_here.shape[2]), jnp.bfloat16),
        in_specs=[pl.BlockSpec(memory_space=pltpu.VMEM)] * 5,
        out_specs=pl.BlockSpec(memory_space=pltpu.VMEM),
        scratch_shapes=[pltpu.VMEM((2 * row_count, nodes), jnp.bfloat16)],
        compiler_params=pltpu.CompilerParams(vmem_limit_bytes=32 * 1024 * 1024),
        name="chain",
    )(own, here, there, slab_here, slab_there)


def by_products(features, own):
    sections, shards = lax.axis_size("section"), lax.axis_size("shard")
    chips = shards // 2
    slabs = [features]
    for back in range(1, chips):
        slabs.append(lax.ppermute(features, "shard", [(i, (i + 2 * back) % shards) for i in range(shards)]))
    relations = lax.all_gather(own, "section", axis=0, tiled=False)[: sections - 1]
    same_core = [list(range(core, shards, 2)) for core in range(2)]
    here = lax.all_gather(relations, "shard", axis=0, tiled=False, axis_index_groups=same_core)
    swap = [(i, i ^ 1) for i in range(shards)]
    slab_here = jnp.stack(slabs)
    slab_there = lax.ppermute(slab_here, "shard", swap)
    there = lax.ppermute(here, "shard", swap)
    return chain(own, here, there, slab_here, slab_there)


def by_hops(features, own):
    sections = lax.axis_size("section")
    part = features.shape[1] // sections
    piece = lax.dynamic_slice_in_dim(features, lax.axis_index("section") * part, part, axis=1)
    relations = lax.all_gather(own, "section", axis=0, tiled=False)
    pieces = []
    for hop in range(sections):
        slab = lax.all_gather(piece, "shard", axis=0, tiled=True)
        piece = jnp.dot(relations[hop], slab, preferred_element_type=jnp.float32).astype(jnp.bfloat16)
        pieces.append(piece)
    mine = lax.all_to_all(jnp.stack(pieces), "section", split_axis=0, concat_axis=0, tiled=True)
    return jnp.swapaxes(mine, 0, 1).reshape(features.shape)


def per_device(features, tile_cols, live_tiles, tile_values, degrees):
    nodes = features.shape[0] * lax.axis_size("shard")
    own = dense_rows(tile_cols, live_tiles, tile_values[0], degrees, nodes)
    plan = by_products if nodes <= features.shape[1] else by_hops
    return plan(features, own)[None]


def solution(mesh):
    in_specs = (
        P("shard", None),
        P("section", None, None),
        P("section", None),
        P("section", "shard", None, None),
        P("section", "shard"),
    )
    out_specs = P("section", "shard", None)
    return jax.shard_map(
        per_device, mesh=mesh, in_specs=in_specs, out_specs=out_specs, check_vma=False
    )
```

```python
import jax
import jax.numpy as jnp
from jax import lax
from jax.experimental import pallas as pl
from jax.experimental.pallas import tpu as pltpu
from jax.sharding import PartitionSpec as P


def dense_rows_kernel(cols_ref, live_ref, tiles_ref, degrees_ref, rows_ref):
    row_count, slots, tile_size = tiles_ref.shape
    blocks = rows_ref.shape[1] // tile_size
    block_row = lax.axis_index("shard") * row_count // tile_size
    live = live_ref[0, block_row]
    wide = row_count * slots
    place = lax.broadcasted_iota(jnp.int32, (row_count, wide), 1)
    slot = lax.rem(place, slots)
    mine = lax.broadcasted_iota(jnp.int32, (row_count, wide), 0) == lax.div(place, slots)
    column = jnp.full((row_count, wide), -1, jnp.int32)
    for k in range(slots):
        column = jnp.where((slot == k) & mine & (k < live), cols_ref[0, block_row, k], column)
    tiles = tiles_ref[...].reshape(wide, tile_size)
    degree = jnp.broadcast_to(degrees_ref[...].astype(jnp.float32), (row_count, row_count))
    diagonal = lax.broadcasted_iota(jnp.int32, (row_count, row_count), 0) == lax.broadcasted_iota(
        jnp.int32, (row_count, row_count), 1
    )
    scale = lax.rsqrt(jnp.sum(jnp.where(diagonal, degree, 0.0), axis=1, keepdims=True))
    for b in range(blocks):
        pick = (column == b).astype(jnp.bfloat16)
        summed = jnp.dot(pick, tiles, preferred_element_type=jnp.float32)
        rows_ref[:, b * tile_size : (b + 1) * tile_size] = (summed * scale).astype(jnp.bfloat16)


def dense_rows(tile_cols, live_tiles, tile_rows, degrees, nodes):
    row_count = tile_rows.shape[0]
    return pl.pallas_call(
        dense_rows_kernel,
        out_shape=jax.ShapeDtypeStruct((row_count, nodes), jnp.bfloat16),
        in_specs=[
            pl.BlockSpec(memory_space=pltpu.SMEM),
            pl.BlockSpec(memory_space=pltpu.SMEM),
            pl.BlockSpec(memory_space=pltpu.VMEM),
            pl.BlockSpec(memory_space=pltpu.VMEM),
        ],
        out_specs=pl.BlockSpec(memory_space=pltpu.VMEM),
        name="dense_rows",
    )(tile_cols, live_tiles, tile_rows, degrees)


def chain_kernel(own_ref, here_ref, there_ref, slab_here_ref, slab_there_ref, out_ref, halves):
    chips, _, row_count, nodes = here_ref.shape
    section, shard = lax.axis_index("section"), lax.axis_index("shard")
    chip, core = lax.div(shard, 2), lax.rem(shard, 2)

    def run(even_ref, odd_ref, slab_even_ref, slab_odd_ref):
        halves[:row_count] = own_ref[...]
        halves[row_count:] = jnp.zeros((row_count, nodes), jnp.bfloat16)

        def times(i, carry):
            parts = []
            for at in range(chips):
                parts += [even_ref[at, section - 1 - i], odd_ref[at, section - 1 - i]]
            both = jnp.dot(halves[...], jnp.concatenate(parts, axis=0), preferred_element_type=jnp.float32)
            product = both[:row_count] + both[row_count:]
            high = product.astype(jnp.bfloat16)
            halves[:row_count] = high
            halves[row_count:] = (product - high.astype(jnp.float32)).astype(jnp.bfloat16)
            return carry

        lax.fori_loop(0, section, times, 0)
        parts = []
        for at in range(chips):
            back = lax.rem(chip - at + chips, chips)
            parts += [slab_even_ref[back], slab_odd_ref[back]]
        both = jnp.dot(halves[...], jnp.concatenate(parts, axis=0), preferred_element_type=jnp.float32)
        out_ref[...] = (both[:row_count] + both[row_count:]).astype(jnp.bfloat16)

    pl.when(core == 0)(lambda: run(here_ref, there_ref, slab_here_ref, slab_there_ref))
    pl.when(core == 1)(lambda: run(there_ref, here_ref, slab_there_ref, slab_here_ref))


def chain(own, here, there, slab_here, slab_there):
    row_count, nodes = own.shape
    return pl.pallas_call(
        chain_kernel,
        out_shape=jax.ShapeDtypeStruct((row_count, slab_here.shape[2]), jnp.bfloat16),
        in_specs=[pl.BlockSpec(memory_space=pltpu.VMEM)] * 5,
        out_specs=pl.BlockSpec(memory_space=pltpu.VMEM),
        scratch_shapes=[pltpu.VMEM((2 * row_count, nodes), jnp.bfloat16)],
        compiler_params=pltpu.CompilerParams(vmem_limit_bytes=32 * 1024 * 1024),
        name="chain",
    )(own, here, there, slab_here, slab_there)


def by_products(features, own):
    sections, shards = lax.axis_size("section"), lax.axis_size("shard")
    chips = shards // 2
    slabs = [features]
    for back in range(1, chips):
        slabs.append(lax.ppermute(features, "shard", [(i, (i + 2 * back) % shards) for i in range(shards)]))
    relations = lax.all_gather(own, "section", axis=0, tiled=False)[: sections - 1]
    relations, slabs = lax.optimization_barrier((relations, slabs))
    same_core = [list(range(core, shards, 2)) for core in range(2)]
    here = lax.all_gather(relations, "shard", axis=0, tiled=False, axis_index_groups=same_core)
    swap = [(i, i ^ 1) for i in range(shards)]
    slab_here = jnp.stack(slabs)
    slab_there = lax.ppermute(slab_here, "shard", swap)
    there = lax.ppermute(here, "shard", swap)
    return chain(own, here, there, slab_here, slab_there)


def by_hops(features, own):
    sections = lax.axis_size("section")
    part = features.shape[1] // sections
    piece = lax.dynamic_slice_in_dim(features, lax.axis_index("section") * part, part, axis=1)
    relations = lax.all_gather(own, "section", axis=0, tiled=False)
    pieces = []
    for hop in range(sections):
        slab = lax.all_gather(piece, "shard", axis=0, tiled=True)
        piece = jnp.dot(relations[hop], slab, preferred_element_type=jnp.float32).astype(jnp.bfloat16)
        pieces.append(piece)
    mine = lax.all_to_all(jnp.stack(pieces), "section", split_axis=0, concat_axis=0, tiled=True)
    return jnp.swapaxes(mine, 0, 1).reshape(features.shape)


def per_device(features, tile_cols, live_tiles, tile_values, degrees):
    nodes = features.shape[0] * lax.axis_size("shard")
    own = dense_rows(tile_cols, live_tiles, tile_values[0], degrees, nodes)
    plan = by_products if nodes <= features.shape[1] else by_hops
    return plan(features, own)[None]


def solution(mesh):
    in_specs = (
        P("shard", None),
        P("section", None, None),
        P("section", None),
        P("section", "shard", None, None),
        P("section", "shard"),
    )
    out_specs = P("section", "shard", None)
    return jax.shard_map(
        per_device, mesh=mesh, in_specs=in_specs, out_specs=out_specs, check_vma=False
    )
```

```python
import jax
import jax.numpy as jnp
from jax import lax
from jax.experimental import pallas as pl
from jax.experimental.pallas import tpu as pltpu
from jax.sharding import PartitionSpec as P


def dense_rows_kernel(cols_ref, live_ref, tiles_ref, degrees_ref, rows_ref):
    row_count, slots, tile_size = tiles_ref.shape
    blocks = rows_ref.shape[1] // tile_size
    block_row = lax.axis_index("shard") * row_count // tile_size
    live = live_ref[0, block_row]
    wide = row_count * slots
    place = lax.broadcasted_iota(jnp.int32, (row_count, wide), 1)
    slot = lax.rem(place, slots)
    mine = lax.broadcasted_iota(jnp.int32, (row_count, wide), 0) == lax.div(place, slots)
    column = jnp.full((row_count, wide), -1, jnp.int32)
    for k in range(slots):
        column = jnp.where((slot == k) & mine & (k < live), cols_ref[0, block_row, k], column)
    tiles = tiles_ref[...].reshape(wide, tile_size)
    degree = jnp.broadcast_to(degrees_ref[...].astype(jnp.float32), (row_count, row_count))
    diagonal = lax.broadcasted_iota(jnp.int32, (row_count, row_count), 0) == lax.broadcasted_iota(
        jnp.int32, (row_count, row_count), 1
    )
    scale = lax.rsqrt(jnp.sum(jnp.where(diagonal, degree, 0.0), axis=1, keepdims=True))
    for b in range(blocks):
        pick = (column == b).astype(jnp.bfloat16)
        summed = jnp.dot(pick, tiles, preferred_element_type=jnp.float32)
        rows_ref[:, b * tile_size : (b + 1) * tile_size] = (summed * scale).astype(jnp.bfloat16)


def dense_rows(tile_cols, live_tiles, tile_rows, degrees, nodes):
    row_count = tile_rows.shape[0]
    return pl.pallas_call(
        dense_rows_kernel,
        out_shape=jax.ShapeDtypeStruct((row_count, nodes), jnp.bfloat16),
        in_specs=[
            pl.BlockSpec(memory_space=pltpu.SMEM),
            pl.BlockSpec(memory_space=pltpu.SMEM),
            pl.BlockSpec(memory_space=pltpu.VMEM),
            pl.BlockSpec(memory_space=pltpu.VMEM),
        ],
        out_specs=pl.BlockSpec(memory_space=pltpu.VMEM),
        name="dense_rows",
    )(tile_cols, live_tiles, tile_rows, degrees)


def chain_kernel(own_ref, slab_here_ref, slab_there_ref, *refs):
    relation_refs, out_ref, halves = refs[:-2], refs[-2], refs[-1]
    row_count, nodes = own_ref.shape
    chips = slab_here_ref.shape[0]
    section, shard = lax.axis_index("section"), lax.axis_index("shard")
    chip, first_core = lax.div(shard, 2), lax.rem(shard, 2) == 0

    def in_order(pairs):
        parts = []
        for here, there in pairs:
            parts += [jnp.where(first_core, here, there), jnp.where(first_core, there, here)]
        return jnp.concatenate(parts, axis=0)

    halves[:row_count] = own_ref[...]
    halves[row_count:] = jnp.zeros((row_count, nodes), jnp.bfloat16)
    for back in range(len(relation_refs) // 2):

        @pl.when(section > back)
        def _(here_ref=relation_refs[2 * back], there_ref=relation_refs[2 * back + 1]):
            rows = [slice(at * row_count, (at + 1) * row_count) for at in range(chips)]
            matrix = in_order([(here_ref[at], there_ref[at]) for at in rows])
            both = jnp.dot(halves[...], matrix, preferred_element_type=jnp.float32)
            product = both[:row_count] + both[row_count:]
            high = product.astype(jnp.bfloat16)
            halves[:row_count] = high
            halves[row_count:] = (product - high.astype(jnp.float32)).astype(jnp.bfloat16)

    at = [lax.rem(chip - place + chips, chips) for place in range(chips)]
    slab = in_order([(slab_here_ref[back], slab_there_ref[back]) for back in at])
    both = jnp.dot(halves[...], slab, preferred_element_type=jnp.float32)
    out_ref[...] = (both[:row_count] + both[row_count:]).astype(jnp.bfloat16)


def chain(own, slab_here, slab_there, relations):
    row_count, nodes = own.shape
    return pl.pallas_call(
        chain_kernel,
        out_shape=jax.ShapeDtypeStruct((row_count, slab_here.shape[2]), jnp.bfloat16),
        in_specs=[pl.BlockSpec(memory_space=pltpu.VMEM)] * (3 + len(relations)),
        out_specs=pl.BlockSpec(memory_space=pltpu.VMEM),
        scratch_shapes=[pltpu.VMEM((2 * row_count, nodes), jnp.bfloat16)],
        compiler_params=pltpu.CompilerParams(vmem_limit_bytes=32 * 1024 * 1024),
        name="chain",
    )(own, slab_here, slab_there, *relations)


def by_products(features, own):
    sections, shards = lax.axis_size("section"), lax.axis_size("shard")
    chips = shards // 2
    swap = [(i, i ^ 1) for i in range(shards)]
    same_core = [list(range(core, shards, 2)) for core in range(2)]
    mine = lax.all_gather(own, "shard", axis=0, tiled=True, axis_index_groups=same_core)
    mine, features = lax.optimization_barrier((mine, features))
    relations = []
    for back in range(1, sections):
        here = lax.ppermute(mine, "section", [(i, i + back) for i in range(sections - back)])
        relations += [here, lax.ppermute(here, "shard", swap)]
    slabs = [features]
    for back in range(1, chips):
        slabs.append(lax.ppermute(features, "shard", [(i, (i + 2 * back) % shards) for i in range(shards)]))
    slab_here = jnp.stack(slabs)
    slab_there = lax.ppermute(slab_here, "shard", swap)
    return chain(own, slab_here, slab_there, relations)


def by_hops(features, own):
    sections = lax.axis_size("section")
    part = features.shape[1] // sections
    piece = lax.dynamic_slice_in_dim(features, lax.axis_index("section") * part, part, axis=1)
    relations = lax.all_gather(own, "section", axis=0, tiled=False)
    pieces = []
    for hop in range(sections):
        slab = lax.all_gather(piece, "shard", axis=0, tiled=True)
        piece = jnp.dot(relations[hop], slab, preferred_element_type=jnp.float32).astype(jnp.bfloat16)
        pieces.append(piece)
    mine = lax.all_to_all(jnp.stack(pieces), "section", split_axis=0, concat_axis=0, tiled=True)
    return jnp.swapaxes(mine, 0, 1).reshape(features.shape)


def per_device(features, tile_cols, live_tiles, tile_values, degrees):
    nodes = features.shape[0] * lax.axis_size("shard")
    own = dense_rows(tile_cols, live_tiles, tile_values[0], degrees, nodes)
    plan = by_products if nodes <= features.shape[1] else by_hops
    return plan(features, own)[None]


def solution(mesh):
    in_specs = (
        P("shard", None),
        P("section", None, None),
        P("section", None),
        P("section", "shard", None, None),
        P("section", "shard"),
    )
    out_specs = P("section", "shard", None)
    return jax.shard_map(
        per_device, mesh=mesh, in_specs=in_specs, out_specs=out_specs, check_vma=False
    )
```

```python
import jax
import jax.numpy as jnp
from jax import lax
from jax.experimental import pallas as pl
from jax.experimental.pallas import tpu as pltpu
from jax.sharding import PartitionSpec as P


def dense_rows_kernel(cols_ref, live_ref, tiles_ref, degrees_ref, rows_ref):
    row_count, slots, tile_size = tiles_ref.shape
    blocks = rows_ref.shape[1] // tile_size
    block_row = lax.axis_index("shard") * row_count // tile_size
    live = live_ref[0, block_row]
    wide = row_count * slots
    place = lax.broadcasted_iota(jnp.int32, (row_count, wide), 1)
    slot = lax.rem(place, slots)
    mine = lax.broadcasted_iota(jnp.int32, (row_count, wide), 0) == lax.div(place, slots)
    column = jnp.full((row_count, wide), -1, jnp.int32)
    for k in range(slots):
        column = jnp.where((slot == k) & mine & (k < live), cols_ref[0, block_row, k], column)
    tiles = tiles_ref[...].reshape(wide, tile_size)
    degree = jnp.broadcast_to(degrees_ref[...].astype(jnp.float32), (row_count, row_count))
    diagonal = lax.broadcasted_iota(jnp.int32, (row_count, row_count), 0) == lax.broadcasted_iota(
        jnp.int32, (row_count, row_count), 1
    )
    scale = lax.rsqrt(jnp.sum(jnp.where(diagonal, degree, 0.0), axis=1, keepdims=True))
    for b in range(blocks):
        pick = (column == b).astype(jnp.bfloat16)
        summed = jnp.dot(pick, tiles, preferred_element_type=jnp.float32)
        rows_ref[:, b * tile_size : (b + 1) * tile_size] = (summed * scale).astype(jnp.bfloat16)


def dense_rows(tile_cols, live_tiles, tile_rows, degrees, nodes):
    row_count = tile_rows.shape[0]
    return pl.pallas_call(
        dense_rows_kernel,
        out_shape=jax.ShapeDtypeStruct((row_count, nodes), jnp.bfloat16),
        in_specs=[
            pl.BlockSpec(memory_space=pltpu.SMEM),
            pl.BlockSpec(memory_space=pltpu.SMEM),
            pl.BlockSpec(memory_space=pltpu.VMEM),
            pl.BlockSpec(memory_space=pltpu.VMEM),
        ],
        out_specs=pl.BlockSpec(memory_space=pltpu.VMEM),
        name="dense_rows",
    )(tile_cols, live_tiles, tile_rows, degrees)


def chain_kernel(own_ref, slab_here_ref, slab_there_ref, *refs):
    relation_refs, out_ref, halves = refs[:-2], refs[-2], refs[-1]
    row_count, nodes = own_ref.shape
    chips = slab_here_ref.shape[0]
    section, shard = lax.axis_index("section"), lax.axis_index("shard")
    chip, first_core = lax.div(shard, 2), lax.rem(shard, 2) == 0
    backs = [lax.rem(chip - place + chips, chips) for place in range(chips)]

    def in_order(pairs):
        parts = []
        for here, there in pairs:
            parts += [jnp.where(first_core, here, there), jnp.where(first_core, there, here)]
        return jnp.concatenate(parts, axis=0)

    halves[:row_count] = own_ref[...]
    halves[row_count:] = jnp.zeros((row_count, nodes), jnp.bfloat16)
    for back in range(len(relation_refs) // 2):

        @pl.when(section > back)
        def _(here_ref=relation_refs[2 * back], there_ref=relation_refs[2 * back + 1]):
            matrix = in_order([(here_ref[at], there_ref[at]) for at in backs])
            both = jnp.dot(halves[...], matrix, preferred_element_type=jnp.float32)
            product = both[:row_count] + both[row_count:]
            high = product.astype(jnp.bfloat16)
            halves[:row_count] = high
            halves[row_count:] = (product - high.astype(jnp.float32)).astype(jnp.bfloat16)

    slab = in_order([(slab_here_ref[at], slab_there_ref[at]) for at in backs])
    both = jnp.dot(halves[...], slab, preferred_element_type=jnp.float32)
    out_ref[...] = (both[:row_count] + both[row_count:]).astype(jnp.bfloat16)


def chain(own, slab_here, slab_there, relations):
    row_count, nodes = own.shape
    return pl.pallas_call(
        chain_kernel,
        out_shape=jax.ShapeDtypeStruct((row_count, slab_here.shape[2]), jnp.bfloat16),
        in_specs=[pl.BlockSpec(memory_space=pltpu.VMEM)] * (3 + len(relations)),
        out_specs=pl.BlockSpec(memory_space=pltpu.VMEM),
        scratch_shapes=[pltpu.VMEM((2 * row_count, nodes), jnp.bfloat16)],
        compiler_params=pltpu.CompilerParams(vmem_limit_bytes=32 * 1024 * 1024),
        name="chain",
    )(own, slab_here, slab_there, *relations)


def by_products(features, own):
    sections, shards = lax.axis_size("section"), lax.axis_size("shard")
    chips = shards // 2
    swap = [(i, i ^ 1) for i in range(shards)]

    def along_z(value, back):
        return lax.ppermute(value, "shard", [(i, (i + 2 * back) % shards) for i in range(shards)])

    rows = [own] + [along_z(own, back) for back in range(1, chips)]
    rows[1], features = lax.optimization_barrier((rows[1], features))
    slab_here = jnp.stack([features] + [along_z(features, back) for back in range(1, chips)])
    slab_there = lax.ppermute(slab_here, "shard", swap)
    mine = jnp.stack(rows)
    relations = []
    for back in range(1, sections):
        here = lax.ppermute(mine, "section", [(i, i + back) for i in range(sections - back)])
        relations += [here, lax.ppermute(here, "shard", swap)]
    return chain(own, slab_here, slab_there, relations)


def by_hops(features, own):
    sections = lax.axis_size("section")
    part = features.shape[1] // sections
    piece = lax.dynamic_slice_in_dim(features, lax.axis_index("section") * part, part, axis=1)
    relations = lax.all_gather(own, "section", axis=0, tiled=False)
    pieces = []
    for hop in range(sections):
        slab = lax.all_gather(piece, "shard", axis=0, tiled=True)
        piece = jnp.dot(relations[hop], slab, preferred_element_type=jnp.float32).astype(jnp.bfloat16)
        pieces.append(piece)
    mine = lax.all_to_all(jnp.stack(pieces), "section", split_axis=0, concat_axis=0, tiled=True)
    return jnp.swapaxes(mine, 0, 1).reshape(features.shape)


def per_device(features, tile_cols, live_tiles, tile_values, degrees):
    nodes = features.shape[0] * lax.axis_size("shard")
    own = dense_rows(tile_cols, live_tiles, tile_values[0], degrees, nodes)
    plan = by_products if nodes <= features.shape[1] else by_hops
    return plan(features, own)[None]


def solution(mesh):
    in_specs = (
        P("shard", None),
        P("section", None, None),
        P("section", None),
        P("section", "shard", None, None),
        P("section", "shard"),
    )
    out_specs = P("section", "shard", None)
    return jax.shard_map(
        per_device, mesh=mesh, in_specs=in_specs, out_specs=out_specs, check_vma=False
    )
```

```python
import jax
import jax.numpy as jnp
from jax import lax
from jax.experimental import pallas as pl
from jax.experimental.pallas import tpu as pltpu
from jax.sharding import PartitionSpec as P


def dense_rows_kernel(cols_ref, live_ref, tiles_ref, degrees_ref, rows_ref):
    row_count, slots, tile_size = tiles_ref.shape
    blocks = rows_ref.shape[1] // tile_size
    block_row = lax.axis_index("shard") * row_count // tile_size
    live = live_ref[0, block_row]
    wide = row_count * slots
    slot = lax.rem(lax.broadcasted_iota(jnp.int32, (1, wide), 1), slots)
    column = jnp.full((1, wide), -1, jnp.int32)
    for k in range(slots):
        column = jnp.where(slot == k, jnp.where(k < live, cols_ref[0, block_row, k], -1), column)
    owner = lax.div(lax.broadcasted_iota(jnp.int32, (row_count, wide), 1), slots)
    mine = lax.broadcasted_iota(jnp.int32, (row_count, wide), 0) == owner
    column = jnp.where(mine, jnp.broadcast_to(column, (row_count, wide)), -1)
    tiles = tiles_ref[...].reshape(wide, tile_size)
    degree = jnp.broadcast_to(degrees_ref[...].astype(jnp.float32), (row_count, row_count))
    diagonal = lax.broadcasted_iota(jnp.int32, (row_count, row_count), 0) == lax.broadcasted_iota(
        jnp.int32, (row_count, row_count), 1
    )
    scale = lax.rsqrt(jnp.sum(jnp.where(diagonal, degree, 0.0), axis=1, keepdims=True))
    for b in range(blocks):
        pick = (column == b).astype(jnp.bfloat16)
        summed = jnp.dot(pick, tiles, preferred_element_type=jnp.float32)
        rows_ref[:, b * tile_size : (b + 1) * tile_size] = (summed * scale).astype(jnp.bfloat16)


def dense_rows(tile_cols, live_tiles, tile_rows, degrees, nodes):
    row_count = tile_rows.shape[0]
    return pl.pallas_call(
        dense_rows_kernel,
        out_shape=pltpu.VMEM((row_count, nodes), jnp.bfloat16),
        in_specs=[
            pl.BlockSpec(memory_space=pltpu.SMEM),
            pl.BlockSpec(memory_space=pltpu.SMEM),
            pl.BlockSpec(memory_space=pltpu.VMEM),
            pl.BlockSpec(memory_space=pltpu.VMEM),
        ],
        out_specs=pl.BlockSpec(memory_space=pltpu.VMEM),
        name="dense_rows",
    )(tile_cols, live_tiles, tile_rows, degrees)


def chain_kernel(own_ref, *refs):
    slab_refs, relation_refs, out_ref, halves = refs[:4], refs[4:-2], refs[-2], refs[-1]
    row_count, nodes = own_ref.shape
    section, shard = lax.axis_index("section"), lax.axis_index("shard")
    chip, first_core = lax.div(shard, 2), lax.rem(shard, 2) == 0

    def times(*matrix_refs):
        left, right = [], []
        for here_ref, there_ref in zip(matrix_refs[::2], matrix_refs[1::2]):
            for piece in range(here_ref.shape[0]):
                source = lax.bitwise_xor(chip, len(left))
                left.append(halves[:, pl.ds(pl.multiple_of(source * 2 * row_count, 128), 2 * row_count)])
                here, there = here_ref[piece], there_ref[piece]
                right += [jnp.where(first_core, here, there), jnp.where(first_core, there, here)]
        left, right = jnp.concatenate(left, axis=1), jnp.concatenate(right, axis=0)
        both = jnp.dot(left, right, preferred_element_type=jnp.float32)
        return both[:row_count] + both[row_count:]

    halves[:row_count] = own_ref[...]
    halves[row_count:] = jnp.zeros((row_count, nodes), jnp.bfloat16)
    for back in range(len(relation_refs) // 2):

        @pl.when(section > back)
        def _(here_ref=relation_refs[2 * back], there_ref=relation_refs[2 * back + 1]):
            product = times(here_ref, there_ref)
            high = product.astype(jnp.bfloat16)
            halves[:row_count] = high
            halves[row_count:] = (product - high.astype(jnp.float32)).astype(jnp.bfloat16)

    out_ref[...] = times(*slab_refs).astype(jnp.bfloat16)


def chain(own, slab, relations):
    row_count, nodes = own.shape
    return pl.pallas_call(
        chain_kernel,
        out_shape=jax.ShapeDtypeStruct((row_count, slab[0].shape[2]), jnp.bfloat16),
        in_specs=[pl.BlockSpec(memory_space=pltpu.VMEM)] * (1 + len(slab) + len(relations)),
        out_specs=pl.BlockSpec(memory_space=pltpu.VMEM),
        scratch_shapes=[pltpu.VMEM((2 * row_count, nodes), jnp.bfloat16)],
        compiler_params=pltpu.CompilerParams(vmem_limit_bytes=32 * 1024 * 1024),
        name="chain",
    )(own, *slab, *relations)


def by_products(features, own):
    sections, shards = lax.axis_size("section"), lax.axis_size("shard")
    chips = shards // 2

    def swap(value, mask):
        return lax.ppermute(value, "shard", [(i, i ^ mask) for i in range(shards)])

    own, features = lax.optimization_barrier((own, features))
    rows = [own] + [swap(own, 2 * step) for step in range(1, chips)]
    held, step = features[None], 1
    while 2 * step < chips:
        held = jnp.concatenate([held, swap(held, 2 * step)])
        step *= 2
    mine = jnp.stack(rows)
    mine, held = lax.optimization_barrier((mine, held))
    came = swap(held, 2 * step)
    slab = [held, swap(held, 1), came, swap(came, 1)]
    relations = []
    for back in range(1, sections):
        here = lax.ppermute(mine, "section", [(i, i + back) for i in range(sections - back)])
        relations += [here, swap(here, 1)]
    return chain(own, slab, relations)


def by_hops(features, own):
    sections = lax.axis_size("section")
    part = features.shape[1] // sections
    piece = lax.dynamic_slice_in_dim(features, lax.axis_index("section") * part, part, axis=1)
    relations = lax.all_gather(own, "section", axis=0, tiled=False)
    pieces = []
    for hop in range(sections):
        slab = lax.all_gather(piece, "shard", axis=0, tiled=True)
        piece = jnp.dot(relations[hop], slab, preferred_element_type=jnp.float32).astype(jnp.bfloat16)
        pieces.append(piece)
    mine = lax.all_to_all(jnp.stack(pieces), "section", split_axis=0, concat_axis=0, tiled=True)
    return jnp.swapaxes(mine, 0, 1).reshape(features.shape)


def per_device(features, tile_cols, live_tiles, tile_values, degrees):
    nodes = features.shape[0] * lax.axis_size("shard")
    own = dense_rows(tile_cols, live_tiles, tile_values[0], degrees, nodes)
    shards = lax.axis_size("shard")
    doubles = shards >= 4 and shards & (shards - 1) == 0
    plan = by_products if doubles and nodes <= features.shape[1] else by_hops
    return plan(features, own)[None]


def solution(mesh):
    in_specs = (
        P("shard", None),
        P("section", None, None),
        P("section", None),
        P("section", "shard", None, None),
        P("section", "shard"),
    )
    out_specs = P("section", "shard", None)
    return jax.shard_map(
        per_device, mesh=mesh, in_specs=in_specs, out_specs=out_specs, check_vma=False
    )
```

```python
import functools

import jax
import jax.numpy as jnp
from jax import lax
from jax.experimental import pallas as pl
from jax.experimental.pallas import tpu as pltpu
from jax.sharding import PartitionSpec as P


def dense_rows_kernel(cols_ref, live_ref, tiles_ref, degrees_ref, rows_ref):
    row_count, slots, tile_size = tiles_ref.shape
    blocks = rows_ref.shape[1] // tile_size
    block_row = lax.axis_index("shard") * row_count // tile_size
    live = live_ref[0, block_row]
    wide = row_count * slots
    slot = lax.rem(lax.broadcasted_iota(jnp.int32, (1, wide), 1), slots)
    column = jnp.full((1, wide), -1, jnp.int32)
    for k in range(slots):
        column = jnp.where(slot == k, jnp.where(k < live, cols_ref[0, block_row, k], -1), column)
    owner = lax.div(lax.broadcasted_iota(jnp.int32, (row_count, wide), 1), slots)
    mine = lax.broadcasted_iota(jnp.int32, (row_count, wide), 0) == owner
    column = jnp.where(mine, jnp.broadcast_to(column, (row_count, wide)), -1)
    tiles = tiles_ref[...].reshape(wide, tile_size)
    degree = jnp.broadcast_to(degrees_ref[...].astype(jnp.float32), (row_count, row_count))
    diagonal = lax.broadcasted_iota(jnp.int32, (row_count, row_count), 0) == lax.broadcasted_iota(
        jnp.int32, (row_count, row_count), 1
    )
    scale = lax.rsqrt(jnp.sum(jnp.where(diagonal, degree, 0.0), axis=1, keepdims=True))
    for b in range(blocks):
        pick = (column == b).astype(jnp.bfloat16)
        summed = jnp.dot(pick, tiles, preferred_element_type=jnp.float32)
        rows_ref[:, b * tile_size : (b + 1) * tile_size] = (summed * scale).astype(jnp.bfloat16)


def dense_rows(tile_cols, live_tiles, tile_rows, degrees, nodes):
    row_count = tile_rows.shape[0]
    return pl.pallas_call(
        dense_rows_kernel,
        out_shape=pltpu.VMEM((row_count, nodes), jnp.bfloat16),
        in_specs=[
            pl.BlockSpec(memory_space=pltpu.SMEM),
            pl.BlockSpec(memory_space=pltpu.SMEM),
            pl.BlockSpec(memory_space=pltpu.VMEM),
            pl.BlockSpec(memory_space=pltpu.VMEM),
        ],
        out_specs=pl.BlockSpec(memory_space=pltpu.VMEM),
        name="dense_rows",
    )(tile_cols, live_tiles, tile_rows, degrees)


def chain_kernel(slab_masks, own_ref, *refs):
    slab_refs, relation_refs, out_ref, halves = refs[:4], refs[4:-2], refs[-2], refs[-1]
    row_count, nodes = own_ref.shape
    section, shard = lax.axis_index("section"), lax.axis_index("shard")
    chip, first_core = lax.div(shard, 2), lax.rem(shard, 2) == 0

    def times(pairs):
        left, right = [], []
        for here_ref, there_ref, masks in pairs:
            for piece, mask in enumerate(masks):
                source = lax.bitwise_xor(chip, mask)
                left.append(halves[:, pl.ds(pl.multiple_of(source * 2 * row_count, 128), 2 * row_count)])
                here, there = here_ref[piece], there_ref[piece]
                right += [jnp.where(first_core, here, there), jnp.where(first_core, there, here)]
        left, right = jnp.concatenate(left, axis=1), jnp.concatenate(right, axis=0)
        both = jnp.dot(left, right, preferred_element_type=jnp.float32)
        return both[:row_count] + both[row_count:]

    halves[:row_count] = own_ref[...]
    halves[row_count:] = jnp.zeros((row_count, nodes), jnp.bfloat16)
    for at in range(1, len(relation_refs) // 2 + 1):

        @pl.when(section == at)
        def _(at=at):
            for earlier in reversed(range(at)):
                other = 2 * ((at ^ earlier) - 1)
                here_ref, there_ref = relation_refs[other], relation_refs[other + 1]
                product = times([(here_ref, there_ref, range(here_ref.shape[0]))])
                high = product.astype(jnp.bfloat16)
                halves[:row_count] = high
                halves[row_count:] = (product - high.astype(jnp.float32)).astype(jnp.bfloat16)

    slab = [(slab_refs[0], slab_refs[1], slab_masks[0]), (slab_refs[2], slab_refs[3], slab_masks[1])]
    out_ref[...] = times(slab).astype(jnp.bfloat16)


def chain(own, slab, slab_masks, relations):
    row_count, nodes = own.shape
    return pl.pallas_call(
        functools.partial(chain_kernel, slab_masks),
        out_shape=jax.ShapeDtypeStruct((row_count, slab[0].shape[2]), jnp.bfloat16),
        in_specs=[pl.BlockSpec(memory_space=pltpu.VMEM)] * (1 + len(slab) + len(relations)),
        out_specs=pl.BlockSpec(memory_space=pltpu.VMEM),
        scratch_shapes=[pltpu.VMEM((2 * row_count, nodes), jnp.bfloat16)],
        compiler_params=pltpu.CompilerParams(vmem_limit_bytes=32 * 1024 * 1024),
        name="chain",
    )(own, *slab, *relations)


def by_products(features, own):
    sections, shards = lax.axis_size("section"), lax.axis_size("shard")
    chips = shards // 2

    def swap(value, mask):
        return lax.ppermute(value, "shard", [(i, i ^ mask) for i in range(shards)])

    def later(value, mask):
        return lax.ppermute(value, "section", [(i, i ^ mask) for i in range(sections) if i ^ mask > i])

    def along_z(value):
        return jnp.stack([value] + [swap(value, 2 * mask) for mask in range(1, chips)])

    held, masks, step = features[None], [0], chips // 2
    while step > 1:
        held, masks, step = jnp.concatenate([held, swap(held, 2 * step)]), masks + [m ^ step for m in masks], step // 2
    crossing = {mask: later(own, mask) for mask in range(1, sections) if mask & (mask - 1)}
    mine = along_z(own)
    mine, held = lax.optimization_barrier((mine, held))
    came = swap(held, 2)
    slab = [held, swap(held, 1), came, swap(came, 1)]
    relations = []
    for mask in range(1, sections):
        here = along_z(crossing[mask]) if mask in crossing else later(mine, mask)
        relations += [here, swap(here, 1)]
    return chain(own, slab, (masks, [m ^ 1 for m in masks]), relations)


def by_hops(features, own):
    sections = lax.axis_size("section")
    part = features.shape[1] // sections
    piece = lax.dynamic_slice_in_dim(features, lax.axis_index("section") * part, part, axis=1)
    relations = lax.all_gather(own, "section", axis=0, tiled=False)
    pieces = []
    for hop in range(sections):
        slab = lax.all_gather(piece, "shard", axis=0, tiled=True)
        piece = jnp.dot(relations[hop], slab, preferred_element_type=jnp.float32).astype(jnp.bfloat16)
        pieces.append(piece)
    mine = lax.all_to_all(jnp.stack(pieces), "section", split_axis=0, concat_axis=0, tiled=True)
    return jnp.swapaxes(mine, 0, 1).reshape(features.shape)


def per_device(features, tile_cols, live_tiles, tile_values, degrees):
    nodes = features.shape[0] * lax.axis_size("shard")
    own = dense_rows(tile_cols, live_tiles, tile_values[0], degrees, nodes)
    sections, shards = lax.axis_size("section"), lax.axis_size("shard")
    doubles = shards >= 4 and shards & (shards - 1) == 0 and sections & (sections - 1) == 0
    plan = by_products if doubles and nodes <= features.shape[1] else by_hops
    return plan(features, own)[None]


def solution(mesh):
    in_specs = (
        P("shard", None),
        P("section", None, None),
        P("section", None),
        P("section", "shard", None, None),
        P("section", "shard"),
    )
    out_specs = P("section", "shard", None)
    return jax.shard_map(
        per_device, mesh=mesh, in_specs=in_specs, out_specs=out_specs, check_vma=False
    )
```

```python
import functools

import jax
import jax.numpy as jnp
from jax import lax
from jax.experimental import pallas as pl
from jax.experimental.pallas import tpu as pltpu
from jax.sharding import PartitionSpec as P


def dense_rows_kernel(cols_ref, live_ref, tiles_ref, degrees_ref, features_ref, rows_ref):
    row_count, slots, tile_size = tiles_ref.shape
    nodes = row_count * lax.axis_size("shard")
    blocks = nodes // tile_size
    share = rows_ref.shape[1] - nodes
    if share:
        shares = features_ref.shape[1] // share
        first = pl.multiple_of(lax.rem(lax.axis_index("section"), shares) * share, 128)
        rows_ref[:, nodes:] = features_ref[:, pl.ds(first, share)]
    block_row = lax.axis_index("shard") * row_count // tile_size
    live = live_ref[0, block_row]
    wide = row_count * slots
    slot = lax.rem(lax.broadcasted_iota(jnp.int32, (1, wide), 1), slots)
    column = jnp.full((1, wide), -1, jnp.int32)
    for k in range(slots):
        column = jnp.where(slot == k, jnp.where(k < live, cols_ref[0, block_row, k], -1), column)
    owner = lax.div(lax.broadcasted_iota(jnp.int32, (row_count, wide), 1), slots)
    mine = lax.broadcasted_iota(jnp.int32, (row_count, wide), 0) == owner
    column = jnp.where(mine, jnp.broadcast_to(column, (row_count, wide)), -1)
    tiles = tiles_ref[...].reshape(wide, tile_size)
    degree = jnp.broadcast_to(degrees_ref[...].astype(jnp.float32), (row_count, row_count))
    diagonal = lax.broadcasted_iota(jnp.int32, (row_count, row_count), 0) == lax.broadcasted_iota(
        jnp.int32, (row_count, row_count), 1
    )
    scale = lax.rsqrt(jnp.sum(jnp.where(diagonal, degree, 0.0), axis=1, keepdims=True))
    for b in range(blocks):
        pick = (column == b).astype(jnp.bfloat16)
        summed = jnp.dot(pick, tiles, preferred_element_type=jnp.float32)
        rows_ref[:, b * tile_size : (b + 1) * tile_size] = (summed * scale).astype(jnp.bfloat16)


def dense_rows(tile_cols, live_tiles, tile_rows, degrees, features, share):
    row_count = tile_rows.shape[0]
    nodes = row_count * lax.axis_size("shard")
    return pl.pallas_call(
        dense_rows_kernel,
        out_shape=pltpu.VMEM((row_count, nodes + share), jnp.bfloat16),
        in_specs=[
            pl.BlockSpec(memory_space=pltpu.SMEM),
            pl.BlockSpec(memory_space=pltpu.SMEM),
            pl.BlockSpec(memory_space=pltpu.VMEM),
            pl.BlockSpec(memory_space=pltpu.VMEM),
            pl.BlockSpec(memory_space=pltpu.VMEM),
        ],
        out_specs=pl.BlockSpec(memory_space=pltpu.VMEM),
        name="dense_rows",
    )(tile_cols, live_tiles, tile_rows, degrees, features)


def chain_kernel(nodes, own_ref, *refs):
    pair_refs, out_ref, halves = refs[:-2], refs[-2], refs[-1]
    row_count = own_ref.shape[0]
    share = own_ref.shape[1] - nodes
    sections, chips = len(pair_refs) // 2, pair_refs[0].shape[0]
    section, shard = lax.axis_index("section"), lax.axis_index("shard")
    chip, first_core = lax.div(shard, 2), lax.rem(shard, 2) == 0

    def times(mask, columns):
        left, right = [], []
        for piece in range(chips):
            source = lax.bitwise_xor(chip, piece)
            left.append(halves[:, pl.ds(pl.multiple_of(source * 2 * row_count, 128), 2 * row_count)])
            here, there = pair_refs[2 * mask][piece, :, columns], pair_refs[2 * mask + 1][piece, :, columns]
            right += [jnp.where(first_core, here, there), jnp.where(first_core, there, here)]
        left, right = jnp.concatenate(left, axis=1), jnp.concatenate(right, axis=0)
        both = jnp.dot(left, right, preferred_element_type=jnp.float32)
        return both[:row_count] + both[row_count:]

    halves[:row_count] = own_ref[:, :nodes]
    halves[row_count:] = jnp.zeros((row_count, nodes), jnp.bfloat16)
    for at in range(sections):

        @pl.when(section == at)
        def _(at=at):
            for earlier in reversed(range(at)):
                product = times(at ^ earlier, slice(0, nodes))
                high = product.astype(jnp.bfloat16)
                halves[:row_count] = high
                halves[row_count:] = (product - high.astype(jnp.float32)).astype(jnp.bfloat16)
            for giver in range(out_ref.shape[1] // share):
                product = times(at ^ giver, slice(nodes, nodes + share))
                out_ref[:, giver * share : (giver + 1) * share] = product.astype(jnp.bfloat16)


def chain(own, pairs, nodes, width):
    row_count = own.shape[0]
    return pl.pallas_call(
        functools.partial(chain_kernel, nodes),
        out_shape=jax.ShapeDtypeStruct((row_count, width), jnp.bfloat16),
        in_specs=[pl.BlockSpec(memory_space=pltpu.VMEM)] * (1 + len(pairs)),
        out_specs=pl.BlockSpec(memory_space=pltpu.VMEM),
        scratch_shapes=[pltpu.VMEM((2 * row_count, nodes), jnp.bfloat16)],
        compiler_params=pltpu.CompilerParams(vmem_limit_bytes=32 * 1024 * 1024),
        name="chain",
    )(own, *pairs)


def by_products(own, nodes, width):
    sections, shards = lax.axis_size("section"), lax.axis_size("shard")

    def along_shard(value, mask):
        return lax.ppermute(value, "shard", [(i, i ^ mask) for i in range(shards)])

    def along_section(value, mask):
        return lax.ppermute(value, "section", [(i, i ^ mask) for i in range(sections)])

    def along_z(value):
        return jnp.stack([value] + [along_shard(value, 2 * mask) for mask in range(1, shards // 2)])

    ahead = {mask: along_section(own, mask) for mask in range(1, sections) if mask & (mask - 1)}
    mine, ahead = lax.optimization_barrier((along_z(own), ahead))
    gathered = [mine]
    for mask in range(1, sections):
        gathered.append(along_z(ahead[mask]) if mask in ahead else along_section(mine, mask))
    pairs = []
    for here in gathered:
        pairs += [here, along_shard(here, 1)]
    return chain(own, pairs, nodes, width)


def by_hops(features, own):
    sections = lax.axis_size("section")
    part = features.shape[1] // sections
    piece = lax.dynamic_slice_in_dim(features, lax.axis_index("section") * part, part, axis=1)
    relations = lax.all_gather(own, "section", axis=0, tiled=False)
    pieces = []
    for hop in range(sections):
        slab = lax.all_gather(piece, "shard", axis=0, tiled=True)
        piece = jnp.dot(relations[hop], slab, preferred_element_type=jnp.float32).astype(jnp.bfloat16)
        pieces.append(piece)
    mine = lax.all_to_all(jnp.stack(pieces), "section", split_axis=0, concat_axis=0, tiled=True)
    return jnp.swapaxes(mine, 0, 1).reshape(features.shape)


def per_device(features, tile_cols, live_tiles, tile_values, degrees):
    row_count, width = features.shape
    sections, shards = lax.axis_size("section"), lax.axis_size("shard")
    nodes = row_count * shards
    doubles = shards >= 2 and shards & (shards - 1) == 0 and sections & (sections - 1) == 0
    products = doubles and nodes <= width and width % (sections - 1) == 0
    share = width // (sections - 1) if products else 0
    own = dense_rows(tile_cols, live_tiles, tile_values[0], degrees, features, share)
    out = by_products(own, nodes, width) if products else by_hops(features, own)
    return out[None]


def solution(mesh):
    in_specs = (
        P("shard", None),
        P("section", None, None),
        P("section", None),
        P("section", "shard", None, None),
        P("section", "shard"),
    )
    out_specs = P("section", "shard", None)
    return jax.shard_map(
        per_device, mesh=mesh, in_specs=in_specs, out_specs=out_specs, check_vma=False
    )
```

```python
import functools

import jax
import jax.numpy as jnp
from jax import lax
from jax.experimental import pallas as pl
from jax.experimental.pallas import tpu as pltpu
from jax.sharding import PartitionSpec as P


def dense_rows_kernel(cols_ref, live_ref, tiles_ref, degrees_ref, features_ref, rows_ref):
    row_count, slots, tile_size = tiles_ref.shape
    nodes = row_count * lax.axis_size("shard")
    blocks = nodes // tile_size
    share = rows_ref.shape[1] - nodes
    if share:
        shares = features_ref.shape[1] // share
        first = pl.multiple_of(lax.rem(lax.axis_index("section"), shares) * share, 128)
        rows_ref[:, nodes:] = features_ref[:, pl.ds(first, share)]
    block_row = lax.axis_index("shard") * row_count // tile_size
    live = live_ref[0, block_row]
    wide = row_count * slots
    slot = lax.rem(lax.broadcasted_iota(jnp.int32, (1, wide), 1), slots)
    column = jnp.full((1, wide), -1, jnp.int32)
    for k in range(slots):
        column = jnp.where(slot == k, jnp.where(k < live, cols_ref[0, block_row, k], -1), column)
    owner = lax.div(lax.broadcasted_iota(jnp.int32, (row_count, wide), 1), slots)
    mine = lax.broadcasted_iota(jnp.int32, (row_count, wide), 0) == owner
    column = jnp.where(mine, jnp.broadcast_to(column, (row_count, wide)), -1)
    tiles = tiles_ref[...].reshape(wide, tile_size)
    degree = jnp.broadcast_to(degrees_ref[...].astype(jnp.float32), (row_count, row_count))
    diagonal = lax.broadcasted_iota(jnp.int32, (row_count, row_count), 0) == lax.broadcasted_iota(
        jnp.int32, (row_count, row_count), 1
    )
    scale = lax.rsqrt(jnp.sum(jnp.where(diagonal, degree, 0.0), axis=1, keepdims=True))
    for b in range(blocks):
        pick = (column == b).astype(jnp.bfloat16)
        summed = jnp.dot(pick, tiles, preferred_element_type=jnp.float32)
        rows_ref[:, b * tile_size : (b + 1) * tile_size] = (summed * scale).astype(jnp.bfloat16)


def dense_rows(tile_cols, live_tiles, tile_rows, degrees, features, share):
    row_count = tile_rows.shape[0]
    nodes = row_count * lax.axis_size("shard")
    return pl.pallas_call(
        dense_rows_kernel,
        out_shape=pltpu.VMEM((row_count, nodes + share), jnp.bfloat16),
        in_specs=[
            pl.BlockSpec(memory_space=pltpu.SMEM),
            pl.BlockSpec(memory_space=pltpu.SMEM),
            pl.BlockSpec(memory_space=pltpu.VMEM),
            pl.BlockSpec(memory_space=pltpu.VMEM),
            pl.BlockSpec(memory_space=pltpu.VMEM),
        ],
        out_specs=pl.BlockSpec(memory_space=pltpu.VMEM),
        name="dense_rows",
    )(tile_cols, live_tiles, tile_rows, degrees, features)


def split_chain(section):
    masks = [section ^ earlier for earlier in reversed(range(section))]
    count = next((i for i, mask in enumerate(masks) if mask & (mask - 1)), len(masks))
    return masks[:count], masks[count:]


def times(halves, pair_refs, mask, columns):
    row_count = halves.shape[0] // 2
    shard = lax.axis_index("shard")
    chip, first_core = lax.div(shard, 2), lax.rem(shard, 2) == 0
    here_ref, there_ref = pair_refs[mask]
    left, right = [], []
    for piece in range(here_ref.shape[0]):
        source = lax.bitwise_xor(chip, piece)
        left.append(halves[:, pl.ds(pl.multiple_of(source * 2 * row_count, 128), 2 * row_count)])
        here, there = here_ref[piece, :, columns], there_ref[piece, :, columns]
        right += [jnp.where(first_core, here, there), jnp.where(first_core, there, here)]
    left, right = jnp.concatenate(left, axis=1), jnp.concatenate(right, axis=0)
    both = jnp.dot(left, right, preferred_element_type=jnp.float32)
    return both[:row_count] + both[row_count:]


def multiply_through(halves, pair_refs, masks):
    row_count, nodes = halves.shape[0] // 2, halves.shape[1]
    for mask in masks:
        product = times(halves, pair_refs, mask, slice(0, nodes))
        high = product.astype(jnp.bfloat16)
        halves[:row_count] = high
        halves[row_count:] = (product - high.astype(jnp.float32)).astype(jnp.bfloat16)


def first_kernel(masks, sections, own_ref, *refs):
    pair_refs, halves = dict(zip(masks, zip(refs[:-1:2], refs[1:-1:2]))), refs[-1]
    row_count, nodes = own_ref.shape[0], halves.shape[1]
    halves[:row_count] = own_ref[:, :nodes]
    halves[row_count:] = jnp.zeros((row_count, nodes), jnp.bfloat16)
    for at in range(sections):
        near, _ = split_chain(at)
        if near:
            pl.when(lax.axis_index("section") == at)(functools.partial(multiply_through, halves, pair_refs, near))


def second_kernel(sections, first_ref, *refs):
    pair_refs, out_ref, halves = list(zip(refs[:-2:2], refs[1:-2:2])), refs[-2], refs[-1]
    nodes = halves.shape[1]
    share = pair_refs[0][0].shape[2] - nodes
    halves[...] = first_ref[...]
    for at in range(sections):

        @pl.when(lax.axis_index("section") == at)
        def _(at=at):
            multiply_through(halves, pair_refs, split_chain(at)[1])
            for giver in range(out_ref.shape[1] // share):
                product = times(halves, pair_refs, at ^ giver, slice(nodes, nodes + share))
                out_ref[:, giver * share : (giver + 1) * share] = product.astype(jnp.bfloat16)


def first_products(own, pairs, nodes, sections):
    masks = [mask for mask in range(1, sections) if not mask & (mask - 1)]
    operands = [array for mask in masks for array in pairs[mask]]
    return pl.pallas_call(
        functools.partial(first_kernel, masks, sections),
        out_shape=pltpu.VMEM((2 * own.shape[0], nodes), jnp.bfloat16),
        in_specs=[pl.BlockSpec(memory_space=pltpu.VMEM)] * (1 + len(operands)),
        out_specs=pl.BlockSpec(memory_space=pltpu.VMEM),
        compiler_params=pltpu.CompilerParams(vmem_limit_bytes=32 * 1024 * 1024),
        name="first_products",
    )(own, *operands)


def second_products(first, pairs, width, sections):
    operands = [array for pair in pairs for array in pair]
    return pl.pallas_call(
        functools.partial(second_kernel, sections),
        out_shape=jax.ShapeDtypeStruct((first.shape[0] // 2, width), jnp.bfloat16),
        in_specs=[pl.BlockSpec(memory_space=pltpu.VMEM)] * (1 + len(operands)),
        out_specs=pl.BlockSpec(memory_space=pltpu.VMEM),
        scratch_shapes=[pltpu.VMEM(first.shape, jnp.bfloat16)],
        compiler_params=pltpu.CompilerParams(vmem_limit_bytes=32 * 1024 * 1024),
        name="second_products",
    )(first, *operands)


def by_products(own, nodes, width):
    sections, shards = lax.axis_size("section"), lax.axis_size("shard")

    def along_shard(value, mask):
        return lax.ppermute(value, "shard", [(i, i ^ mask) for i in range(shards)])

    def along_section(value, mask):
        return lax.ppermute(value, "section", [(i, i ^ mask) for i in range(sections)])

    def along_z(value):
        return jnp.stack([value] + [along_shard(value, 2 * mask) for mask in range(1, shards // 2)])

    ahead = {mask: along_section(own, mask) for mask in range(1, sections) if mask & (mask - 1)}
    mine, ahead = lax.optimization_barrier((along_z(own), ahead))
    gathered = [mine]
    for mask in range(1, sections):
        gathered.append(along_z(ahead[mask]) if mask in ahead else along_section(mine, mask))
    pairs = [(here, along_shard(here, 1)) for here in gathered]
    first = first_products(own, pairs, nodes, sections)
    return second_products(first, pairs, width, sections)


def by_hops(features, own):
    sections = lax.axis_size("section")
    part = features.shape[1] // sections
    piece = lax.dynamic_slice_in_dim(features, lax.axis_index("section") * part, part, axis=1)
    relations = lax.all_gather(own, "section", axis=0, tiled=False)
    pieces = []
    for hop in range(sections):
        slab = lax.all_gather(piece, "shard", axis=0, tiled=True)
        piece = jnp.dot(relations[hop], slab, preferred_element_type=jnp.float32).astype(jnp.bfloat16)
        pieces.append(piece)
    mine = lax.all_to_all(jnp.stack(pieces), "section", split_axis=0, concat_axis=0, tiled=True)
    return jnp.swapaxes(mine, 0, 1).reshape(features.shape)


def per_device(features, tile_cols, live_tiles, tile_values, degrees):
    row_count, width = features.shape
    sections, shards = lax.axis_size("section"), lax.axis_size("shard")
    nodes = row_count * shards
    doubles = shards >= 2 and shards & (shards - 1) == 0 and sections & (sections - 1) == 0
    products = doubles and nodes <= width and width % (sections - 1) == 0
    share = width // (sections - 1) if products else 0
    own = dense_rows(tile_cols, live_tiles, tile_values[0], degrees, features, share)
    out = by_products(own, nodes, width) if products else by_hops(features, own)
    return out[None]


def solution(mesh):
    in_specs = (
        P("shard", None),
        P("section", None, None),
        P("section", None),
        P("section", "shard", None, None),
        P("section", "shard"),
    )
    out_specs = P("section", "shard", None)
    return jax.shard_map(
        per_device, mesh=mesh, in_specs=in_specs, out_specs=out_specs, check_vma=False
    )
```

```python
import functools

import jax
import jax.numpy as jnp
from jax import lax
from jax.experimental import pallas as pl
from jax.experimental.pallas import tpu as pltpu
from jax.sharding import PartitionSpec as P


def dense_rows_kernel(cols_ref, live_ref, tiles_ref, degrees_ref, features_ref, rows_ref):
    row_count, slots, tile_size = tiles_ref.shape
    nodes = row_count * lax.axis_size("shard")
    blocks = nodes // tile_size
    share = rows_ref.shape[1] - nodes
    if share:
        shares = features_ref.shape[1] // share
        first = pl.multiple_of(lax.rem(lax.axis_index("section"), shares) * share, 128)
        rows_ref[:, nodes:] = features_ref[:, pl.ds(first, share)]
    block_row = lax.axis_index("shard") * row_count // tile_size
    live = live_ref[0, block_row]
    wide = row_count * slots
    slot = lax.rem(lax.broadcasted_iota(jnp.int32, (1, wide), 1), slots)
    column = jnp.full((1, wide), -1, jnp.int32)
    for k in range(slots):
        column = jnp.where(slot == k, jnp.where(k < live, cols_ref[0, block_row, k], -1), column)
    owner = lax.div(lax.broadcasted_iota(jnp.int32, (row_count, wide), 1), slots)
    mine = lax.broadcasted_iota(jnp.int32, (row_count, wide), 0) == owner
    column = jnp.where(mine, jnp.broadcast_to(column, (row_count, wide)), -1)
    tiles = tiles_ref[...].reshape(wide, tile_size)
    degree = jnp.broadcast_to(degrees_ref[...].astype(jnp.float32), (row_count, row_count))
    diagonal = lax.broadcasted_iota(jnp.int32, (row_count, row_count), 0) == lax.broadcasted_iota(
        jnp.int32, (row_count, row_count), 1
    )
    scale = lax.rsqrt(jnp.sum(jnp.where(diagonal, degree, 0.0), axis=1, keepdims=True))
    for b in range(blocks):
        pick = (column == b).astype(jnp.bfloat16)
        summed = jnp.dot(pick, tiles, preferred_element_type=jnp.float32)
        rows_ref[:, b * tile_size : (b + 1) * tile_size] = (summed * scale).astype(jnp.bfloat16)


def dense_rows(tile_cols, live_tiles, tile_rows, degrees, features, share):
    row_count = tile_rows.shape[0]
    nodes = row_count * lax.axis_size("shard")
    return pl.pallas_call(
        dense_rows_kernel,
        out_shape=pltpu.VMEM((row_count, nodes + share), jnp.bfloat16),
        in_specs=[
            pl.BlockSpec(memory_space=pltpu.SMEM),
            pl.BlockSpec(memory_space=pltpu.SMEM),
            pl.BlockSpec(memory_space=pltpu.VMEM),
            pl.BlockSpec(memory_space=pltpu.VMEM),
            pl.BlockSpec(memory_space=pltpu.VMEM),
        ],
        out_specs=pl.BlockSpec(memory_space=pltpu.VMEM),
        name="dense_rows",
    )(tile_cols, live_tiles, tile_rows, degrees, features)


def split_chain(section):
    masks = [section ^ earlier for earlier in reversed(range(section))]
    count = next((i for i, mask in enumerate(masks) if mask & (mask - 1)), len(masks))
    return masks[:count], masks[count:]


def times(halves, pair_refs, mask, columns):
    row_count = halves.shape[0] // 2
    shard = lax.axis_index("shard")
    chip, first_core = lax.div(shard, 2), lax.rem(shard, 2) == 0
    here_ref, there_ref = pair_refs[mask]
    left, right = [], []
    chips = here_ref.shape[0]
    for piece in range(chips):
        source = lax.rem(chip - piece + chips, chips)
        left.append(halves[:, pl.ds(pl.multiple_of(source * 2 * row_count, 128), 2 * row_count)])
        here, there = here_ref[piece, :, columns], there_ref[piece, :, columns]
        right += [jnp.where(first_core, here, there), jnp.where(first_core, there, here)]
    left, right = jnp.concatenate(left, axis=1), jnp.concatenate(right, axis=0)
    both = jnp.dot(left, right, preferred_element_type=jnp.float32)
    return both[:row_count] + both[row_count:]


def multiply_through(halves, pair_refs, masks):
    row_count, nodes = halves.shape[0] // 2, halves.shape[1]
    for mask in masks:
        product = times(halves, pair_refs, mask, slice(0, nodes))
        high = product.astype(jnp.bfloat16)
        halves[:row_count] = high
        halves[row_count:] = (product - high.astype(jnp.float32)).astype(jnp.bfloat16)


def first_kernel(masks, sections, own_ref, *refs):
    pair_refs, halves = dict(zip(masks, zip(refs[:-1:2], refs[1:-1:2]))), refs[-1]
    row_count, nodes = own_ref.shape[0], halves.shape[1]
    halves[:row_count] = own_ref[:, :nodes]
    halves[row_count:] = jnp.zeros((row_count, nodes), jnp.bfloat16)
    for at in range(sections):
        near, _ = split_chain(at)
        if near:
            pl.when(lax.axis_index("section") == at)(functools.partial(multiply_through, halves, pair_refs, near))


def second_kernel(sections, first_ref, *refs):
    pair_refs, out_ref, halves = list(zip(refs[:-2:2], refs[1:-2:2])), refs[-2], refs[-1]
    nodes = halves.shape[1]
    share = pair_refs[0][0].shape[2] - nodes
    halves[...] = first_ref[...]
    for at in range(sections):

        @pl.when(lax.axis_index("section") == at)
        def _(at=at):
            multiply_through(halves, pair_refs, split_chain(at)[1])
            for giver in range(out_ref.shape[1] // share):
                product = times(halves, pair_refs, at ^ giver, slice(nodes, nodes + share))
                out_ref[:, giver * share : (giver + 1) * share] = product.astype(jnp.bfloat16)


def first_products(own, pairs, nodes, sections):
    masks = [mask for mask in range(1, sections) if not mask & (mask - 1)]
    operands = [array for mask in masks for array in pairs[mask]]
    return pl.pallas_call(
        functools.partial(first_kernel, masks, sections),
        out_shape=pltpu.VMEM((2 * own.shape[0], nodes), jnp.bfloat16),
        in_specs=[pl.BlockSpec(memory_space=pltpu.VMEM)] * (1 + len(operands)),
        out_specs=pl.BlockSpec(memory_space=pltpu.VMEM),
        compiler_params=pltpu.CompilerParams(vmem_limit_bytes=32 * 1024 * 1024),
        name="first_products",
    )(own, *operands)


def second_products(first, pairs, width, sections):
    operands = [array for pair in pairs for array in pair]
    return pl.pallas_call(
        functools.partial(second_kernel, sections),
        out_shape=jax.ShapeDtypeStruct((first.shape[0] // 2, width), jnp.bfloat16),
        in_specs=[pl.BlockSpec(memory_space=pltpu.VMEM)] * (1 + len(operands)),
        out_specs=pl.BlockSpec(memory_space=pltpu.VMEM),
        scratch_shapes=[pltpu.VMEM(first.shape, jnp.bfloat16)],
        compiler_params=pltpu.CompilerParams(vmem_limit_bytes=32 * 1024 * 1024),
        name="second_products",
    )(first, *operands)


def by_products(own, nodes, width):
    sections, shards = lax.axis_size("section"), lax.axis_size("shard")

    def across_cores(value):
        return lax.ppermute(value, "shard", [(i, i ^ 1) for i in range(shards)])

    def along_section(value, mask):
        return lax.ppermute(value, "section", [(i, i ^ mask) for i in range(sections)])

    def along_z(value):
        turns = [[(i, (i + 2 * back) % shards) for i in range(shards)] for back in range(1, shards // 2)]
        return jnp.stack([value] + [lax.ppermute(value, "shard", turn) for turn in turns])

    ahead = {mask: along_section(own, mask) for mask in range(1, sections) if mask & (mask - 1)}
    mine, ahead = lax.optimization_barrier((along_z(own), ahead))
    gathered = [mine]
    for mask in range(1, sections):
        gathered.append(along_z(ahead[mask]) if mask in ahead else along_section(mine, mask))
    pairs = [(here, across_cores(here)) for here in gathered]
    first = first_products(own, pairs, nodes, sections)
    return second_products(first, pairs, width, sections)


def by_hops(features, own):
    sections = lax.axis_size("section")
    part = features.shape[1] // sections
    piece = lax.dynamic_slice_in_dim(features, lax.axis_index("section") * part, part, axis=1)
    relations = lax.all_gather(own, "section", axis=0, tiled=False)
    pieces = []
    for hop in range(sections):
        slab = lax.all_gather(piece, "shard", axis=0, tiled=True)
        piece = jnp.dot(relations[hop], slab, preferred_element_type=jnp.float32).astype(jnp.bfloat16)
        pieces.append(piece)
    mine = lax.all_to_all(jnp.stack(pieces), "section", split_axis=0, concat_axis=0, tiled=True)
    return jnp.swapaxes(mine, 0, 1).reshape(features.shape)


def per_device(features, tile_cols, live_tiles, tile_values, degrees):
    row_count, width = features.shape
    sections, shards = lax.axis_size("section"), lax.axis_size("shard")
    nodes = row_count * shards
    pairs = shards % 2 == 0 and sections > 1 and sections & (sections - 1) == 0
    products = pairs and nodes <= width and width % (sections - 1) == 0
    share = width // (sections - 1) if products else 0
    own = dense_rows(tile_cols, live_tiles, tile_values[0], degrees, features, share)
    out = by_products(own, nodes, width) if products else by_hops(features, own)
    return out[None]


def solution(mesh):
    in_specs = (
        P("shard", None),
        P("section", None, None),
        P("section", None),
        P("section", "shard", None, None),
        P("section", "shard"),
    )
    out_specs = P("section", "shard", None)
    return jax.shard_map(
        per_device, mesh=mesh, in_specs=in_specs, out_specs=out_specs, check_vma=False
    )
```

```python
import functools

import jax
import jax.numpy as jnp
from jax import lax
from jax.experimental import pallas as pl
from jax.experimental.pallas import tpu as pltpu
from jax.sharding import PartitionSpec as P


def dense_rows_kernel(cols_ref, live_ref, tiles_ref, degrees_ref, features_ref, rows_ref):
    row_count, slots, tile_size = tiles_ref.shape
    nodes = row_count * lax.axis_size("shard")
    blocks = nodes // tile_size
    share = rows_ref.shape[1] - nodes
    if share:
        shares = features_ref.shape[1] // share
        first = pl.multiple_of(lax.rem(lax.axis_index("section"), shares) * share, 128)
        rows_ref[:, nodes:] = features_ref[:, pl.ds(first, share)]
    block_row = lax.axis_index("shard") * row_count // tile_size
    live = live_ref[0, block_row]
    wide = row_count * slots
    slot = lax.rem(lax.broadcasted_iota(jnp.int32, (1, wide), 1), slots)
    column = jnp.full((1, wide), -1, jnp.int32)
    for k in range(slots):
        column = jnp.where(slot == k, jnp.where(k < live, cols_ref[0, block_row, k], -1), column)
    owner = lax.div(lax.broadcasted_iota(jnp.int32, (row_count, wide), 1), slots)
    mine = lax.broadcasted_iota(jnp.int32, (row_count, wide), 0) == owner
    column = jnp.where(mine, jnp.broadcast_to(column, (row_count, wide)), -1)
    tiles = tiles_ref[...].reshape(wide, tile_size)
    degree = jnp.broadcast_to(degrees_ref[...].astype(jnp.float32), (row_count, row_count))
    diagonal = lax.broadcasted_iota(jnp.int32, (row_count, row_count), 0) == lax.broadcasted_iota(
        jnp.int32, (row_count, row_count), 1
    )
    scale = lax.rsqrt(jnp.sum(jnp.where(diagonal, degree, 0.0), axis=1, keepdims=True))
    for b in range(blocks):
        pick = (column == b).astype(jnp.bfloat16)
        summed = jnp.dot(pick, tiles, preferred_element_type=jnp.float32)
        rows_ref[:, b * tile_size : (b + 1) * tile_size] = (summed * scale).astype(jnp.bfloat16)


def dense_rows(tile_cols, live_tiles, tile_rows, degrees, features, share):
    row_count = tile_rows.shape[0]
    nodes = row_count * lax.axis_size("shard")
    return pl.pallas_call(
        dense_rows_kernel,
        out_shape=pltpu.VMEM((row_count, nodes + share), jnp.bfloat16),
        in_specs=[
            pl.BlockSpec(memory_space=pltpu.SMEM),
            pl.BlockSpec(memory_space=pltpu.SMEM),
            pl.BlockSpec(memory_space=pltpu.VMEM),
            pl.BlockSpec(memory_space=pltpu.VMEM),
            pl.BlockSpec(memory_space=pltpu.VMEM),
        ],
        out_specs=pl.BlockSpec(memory_space=pltpu.VMEM),
        name="dense_rows",
    )(tile_cols, live_tiles, tile_rows, degrees, features)


def split_chain(section):
    masks = [section ^ earlier for earlier in reversed(range(section))]
    count = next((i for i, mask in enumerate(masks) if mask & (mask - 1)), len(masks))
    return masks[:count], masks[count:]


def times(halves, pair_refs, mask, columns):
    row_count = halves.shape[0] // 2
    shard = lax.axis_index("shard")
    chip, first_core = lax.div(shard, 2), lax.rem(shard, 2) == 0
    here_ref, there_ref = pair_refs[mask]
    left, right = [], []
    for piece in range(here_ref.shape[0]):
        source = lax.bitwise_xor(chip, piece)
        left.append(halves[:, pl.ds(pl.multiple_of(source * 2 * row_count, 128), 2 * row_count)])
        here, there = here_ref[piece, :, columns], there_ref[piece, :, columns]
        right += [jnp.where(first_core, here, there), jnp.where(first_core, there, here)]
    left, right = jnp.concatenate(left, axis=1), jnp.concatenate(right, axis=0)
    both = jnp.dot(left, right, preferred_element_type=jnp.float32)
    return both[:row_count] + both[row_count:]


def multiply_through(halves, pair_refs, masks):
    row_count, nodes = halves.shape[0] // 2, halves.shape[1]
    for mask in masks:
        product = times(halves, pair_refs, mask, slice(0, nodes))
        high = product.astype(jnp.bfloat16)
        halves[:row_count] = high
        halves[row_count:] = (product - high.astype(jnp.float32)).astype(jnp.bfloat16)


def first_kernel(masks, sections, own_ref, *refs):
    pair_refs, halves = dict(zip(masks, zip(refs[:-1:2], refs[1:-1:2]))), refs[-1]
    row_count, nodes = own_ref.shape[0], halves.shape[1]
    halves[:row_count] = own_ref[:, :nodes]
    halves[row_count:] = jnp.zeros((row_count, nodes), jnp.bfloat16)
    for at in range(sections):
        near, _ = split_chain(at)
        if near:
            pl.when(lax.axis_index("section") == at)(functools.partial(multiply_through, halves, pair_refs, near))


def second_kernel(sections, first_ref, *refs):
    pair_refs, out_ref, halves = list(zip(refs[:-2:2], refs[1:-2:2])), refs[-2], refs[-1]
    nodes = halves.shape[1]
    share = pair_refs[0][0].shape[2] - nodes
    halves[...] = first_ref[...]
    for at in range(sections):

        @pl.when(lax.axis_index("section") == at)
        def _(at=at):
            multiply_through(halves, pair_refs, split_chain(at)[1])
            for giver in range(out_ref.shape[1] // share):
                product = times(halves, pair_refs, at ^ giver, slice(nodes, nodes + share))
                out_ref[:, giver * share : (giver + 1) * share] = product.astype(jnp.bfloat16)


def first_products(own, pairs, nodes, sections):
    masks = [mask for mask in range(1, sections) if not mask & (mask - 1)]
    operands = [array for mask in masks for array in pairs[mask]]
    return pl.pallas_call(
        functools.partial(first_kernel, masks, sections),
        out_shape=pltpu.VMEM((2 * own.shape[0], nodes), jnp.bfloat16),
        in_specs=[pl.BlockSpec(memory_space=pltpu.VMEM)] * (1 + len(operands)),
        out_specs=pl.BlockSpec(memory_space=pltpu.VMEM),
        compiler_params=pltpu.CompilerParams(vmem_limit_bytes=32 * 1024 * 1024),
        name="first_products",
    )(own, *operands)


def second_products(first, pairs, width, sections):
    operands = [array for pair in pairs for array in pair]
    return pl.pallas_call(
        functools.partial(second_kernel, sections),
        out_shape=jax.ShapeDtypeStruct((first.shape[0] // 2, width), jnp.bfloat16),
        in_specs=[pl.BlockSpec(memory_space=pltpu.VMEM)] * (1 + len(operands)),
        out_specs=pl.BlockSpec(memory_space=pltpu.VMEM),
        scratch_shapes=[pltpu.VMEM(first.shape, jnp.bfloat16)],
        compiler_params=pltpu.CompilerParams(vmem_limit_bytes=32 * 1024 * 1024),
        name="second_products",
    )(first, *operands)


def by_products(own, nodes, width):
    sections, shards = lax.axis_size("section"), lax.axis_size("shard")

    def move(value, mask, to_section, to_shard):
        pairs = []
        for section in range(sections):
            if section ^ mask != sections - 1:
                pairs += [(section * shards + i, to_section(section) * shards + to_shard(i)) for i in range(shards)]
        return lax.ppermute(value, ("section", "shard"), pairs)

    def same(index):
        return index

    def along_section(value, mask):
        return move(value, 0, lambda section: section ^ mask, same)

    def across_cores(value, mask):
        return move(value, mask, same, lambda i: i ^ 1)

    def along_z(value, mask):
        steps = range(2, shards, 2)
        return jnp.stack([value] + [move(value, mask, same, lambda i, step=step: i ^ step) for step in steps])

    ahead = {mask: along_section(own, mask) for mask in range(1, sections) if mask & (mask - 1)}
    mine, ahead = lax.optimization_barrier((along_z(own, 0), ahead))
    gathered = [mine]
    for mask in range(1, sections):
        gathered.append(along_z(ahead[mask], mask) if mask in ahead else along_section(mine, mask))
    pairs = [(here, across_cores(here, mask)) for mask, here in enumerate(gathered)]
    first = first_products(own, pairs, nodes, sections)
    return second_products(first, pairs, width, sections)


def by_hops(features, own):
    sections = lax.axis_size("section")
    part = features.shape[1] // sections
    piece = lax.dynamic_slice_in_dim(features, lax.axis_index("section") * part, part, axis=1)
    relations = lax.all_gather(own, "section", axis=0, tiled=False)
    pieces = []
    for hop in range(sections):
        slab = lax.all_gather(piece, "shard", axis=0, tiled=True)
        piece = jnp.dot(relations[hop], slab, preferred_element_type=jnp.float32).astype(jnp.bfloat16)
        pieces.append(piece)
    mine = lax.all_to_all(jnp.stack(pieces), "section", split_axis=0, concat_axis=0, tiled=True)
    return jnp.swapaxes(mine, 0, 1).reshape(features.shape)


def per_device(features, tile_cols, live_tiles, tile_values, degrees):
    row_count, width = features.shape
    sections, shards = lax.axis_size("section"), lax.axis_size("shard")
    nodes = row_count * shards
    doubles = shards >= 2 and shards & (shards - 1) == 0 and sections & (sections - 1) == 0
    products = doubles and nodes <= width and width % (sections - 1) == 0
    share = width // (sections - 1) if products else 0
    own = dense_rows(tile_cols, live_tiles, tile_values[0], degrees, features, share)
    out = by_products(own, nodes, width) if products else by_hops(features, own)
    return out[None]


def solution(mesh):
    in_specs = (
        P("shard", None),
        P("section", None, None),
        P("section", None),
        P("section", "shard", None, None),
        P("section", "shard"),
    )
    out_specs = P("section", "shard", None)
    return jax.shard_map(
        per_device, mesh=mesh, in_specs=in_specs, out_specs=out_specs, check_vma=False
    )
```

```python
import functools

import jax
import jax.numpy as jnp
from jax import lax
from jax.experimental import pallas as pl
from jax.experimental.pallas import tpu as pltpu
from jax.sharding import PartitionSpec as P


def dense_rows_kernel(cols_ref, live_ref, tiles_ref, degrees_ref, features_ref, rows_ref, *sent_refs):
    row_count, slots, tile_size = tiles_ref.shape
    nodes = rows_ref.shape[1]
    blocks = nodes // tile_size
    block_row = lax.axis_index("shard") * row_count // tile_size
    live = live_ref[0, block_row]
    wide = row_count * slots
    slot = lax.rem(lax.broadcasted_iota(jnp.int32, (1, wide), 1), slots)
    column = jnp.full((1, wide), -1, jnp.int32)
    for k in range(slots):
        column = jnp.where(slot == k, jnp.where(k < live, cols_ref[0, block_row, k], -1), column)
    owner = lax.div(lax.broadcasted_iota(jnp.int32, (row_count, wide), 1), slots)
    mine = lax.broadcasted_iota(jnp.int32, (row_count, wide), 0) == owner
    column = jnp.where(mine, jnp.broadcast_to(column, (row_count, wide)), -1)
    tiles = tiles_ref[...].reshape(wide, tile_size)
    degree = jnp.broadcast_to(degrees_ref[...].astype(jnp.float32), (row_count, row_count))
    diagonal = lax.broadcasted_iota(jnp.int32, (row_count, row_count), 0) == lax.broadcasted_iota(
        jnp.int32, (row_count, row_count), 1
    )
    scale = lax.rsqrt(jnp.sum(jnp.where(diagonal, degree, 0.0), axis=1, keepdims=True))
    for b in range(blocks):
        pick = (column == b).astype(jnp.bfloat16)
        summed = jnp.dot(pick, tiles, preferred_element_type=jnp.float32)
        rows_ref[:, b * tile_size : (b + 1) * tile_size] = (summed * scale).astype(jnp.bfloat16)
    for sent_ref in sent_refs:
        sections, section = lax.axis_size("section"), lax.axis_index("section")
        bulk, share = sent_ref.shape[1], sent_ref.shape[1] - nodes
        shares = (features_ref.shape[1] - bulk) // share

        @pl.when(section == sections - 1)
        def _():
            sent_ref[...] = features_ref[:, :bulk]

        @pl.when(section < sections - 1)
        def _():
            first = pl.multiple_of(bulk + jnp.minimum(section, shares - 1) * share, 128)
            sent_ref[:, :nodes] = rows_ref[...]
            sent_ref[:, nodes:] = features_ref[:, pl.ds(first, share)]


def dense_rows(tile_cols, live_tiles, tile_rows, degrees, features, sent_width):
    row_count = tile_rows.shape[0]
    nodes = row_count * lax.axis_size("shard")
    widths = [nodes, sent_width] if sent_width else [nodes]
    return pl.pallas_call(
        dense_rows_kernel,
        out_shape=[pltpu.VMEM((row_count, columns), jnp.bfloat16) for columns in widths],
        in_specs=[
            pl.BlockSpec(memory_space=pltpu.SMEM),
            pl.BlockSpec(memory_space=pltpu.SMEM),
            pl.BlockSpec(memory_space=pltpu.VMEM),
            pl.BlockSpec(memory_space=pltpu.VMEM),
            pl.BlockSpec(memory_space=pltpu.VMEM),
        ],
        out_specs=[pl.BlockSpec(memory_space=pltpu.VMEM)] * len(widths),
        name="dense_rows",
    )(tile_cols, live_tiles, tile_rows, degrees, features)


def split_chain(section):
    masks = [section ^ earlier for earlier in reversed(range(section))]
    count = next((i for i, mask in enumerate(masks) if mask & (mask - 1)), len(masks))
    return masks[:count], masks[count:]


def times(halves, pair_refs, mask, columns):
    row_count = halves.shape[0] // 2
    shard = lax.axis_index("shard")
    chip, first_core = lax.div(shard, 2), lax.rem(shard, 2) == 0
    here_ref, there_ref = pair_refs[mask]
    left, right = [], []
    for piece in range(here_ref.shape[0]):
        source = lax.bitwise_xor(chip, piece)
        left.append(halves[:, pl.ds(pl.multiple_of(source * 2 * row_count, 128), 2 * row_count)])
        here, there = here_ref[piece, :, columns], there_ref[piece, :, columns]
        right += [jnp.where(first_core, here, there), jnp.where(first_core, there, here)]
    left, right = jnp.concatenate(left, axis=1), jnp.concatenate(right, axis=0)
    both = jnp.dot(left, right, preferred_element_type=jnp.float32)
    return both[:row_count] + both[row_count:]


def multiply_through(halves, pair_refs, masks):
    row_count, nodes = halves.shape[0] // 2, halves.shape[1]
    for mask in masks:
        product = times(halves, pair_refs, mask, slice(0, nodes))
        high = product.astype(jnp.bfloat16)
        halves[:row_count] = high
        halves[row_count:] = (product - high.astype(jnp.float32)).astype(jnp.bfloat16)


def first_kernel(masks, sections, own_ref, *refs):
    pair_refs, halves = dict(zip(masks, zip(refs[:-1:2], refs[1:-1:2]))), refs[-1]
    row_count, nodes = own_ref.shape[0], halves.shape[1]
    halves[:row_count] = own_ref[...]
    halves[row_count:] = jnp.zeros((row_count, nodes), jnp.bfloat16)
    for at in range(sections):
        near, _ = split_chain(at)
        if near:
            pl.when(lax.axis_index("section") == at)(functools.partial(multiply_through, halves, pair_refs, near))


def second_kernel(sections, first_ref, *refs):
    pair_refs, out_ref, halves = list(zip(refs[:-2:2], refs[1:-2:2])), refs[-2], refs[-1]
    nodes, bulk = halves.shape[1], pair_refs[0][0].shape[2]
    share = bulk - nodes
    halves[...] = first_ref[...]
    for at in range(sections):

        @pl.when(lax.axis_index("section") == at)
        def _(at=at):
            multiply_through(halves, pair_refs, split_chain(at)[1])
            product = times(halves, pair_refs, at ^ (sections - 1), slice(0, bulk))
            out_ref[:, :bulk] = product.astype(jnp.bfloat16)
            for giver in range((out_ref.shape[1] - bulk) // share):
                product = times(halves, pair_refs, at ^ giver, slice(nodes, bulk))
                first = bulk + giver * share
                out_ref[:, first : first + share] = product.astype(jnp.bfloat16)


def first_products(own, pairs, nodes, sections):
    masks = [mask for mask in range(1, sections) if not mask & (mask - 1)]
    operands = [array for mask in masks for array in pairs[mask]]
    return pl.pallas_call(
        functools.partial(first_kernel, masks, sections),
        out_shape=pltpu.VMEM((2 * own.shape[0], nodes), jnp.bfloat16),
        in_specs=[pl.BlockSpec(memory_space=pltpu.VMEM)] * (1 + len(operands)),
        out_specs=pl.BlockSpec(memory_space=pltpu.VMEM),
        compiler_params=pltpu.CompilerParams(vmem_limit_bytes=32 * 1024 * 1024),
        name="first_products",
    )(own, *operands)


def second_products(first, pairs, width, sections):
    operands = [array for pair in pairs for array in pair]
    return pl.pallas_call(
        functools.partial(second_kernel, sections),
        out_shape=jax.ShapeDtypeStruct((first.shape[0] // 2, width), jnp.bfloat16),
        in_specs=[pl.BlockSpec(memory_space=pltpu.VMEM)] * (1 + len(operands)),
        out_specs=pl.BlockSpec(memory_space=pltpu.VMEM),
        scratch_shapes=[pltpu.VMEM(first.shape, jnp.bfloat16)],
        compiler_params=pltpu.CompilerParams(vmem_limit_bytes=32 * 1024 * 1024),
        name="second_products",
    )(first, *operands)


def by_products(own, sent, width):
    sections, shards = lax.axis_size("section"), lax.axis_size("shard")

    def along_shard(value, mask):
        return lax.ppermute(value, "shard", [(i, i ^ mask) for i in range(shards)])

    def along_section(value, mask):
        return lax.ppermute(value, "section", [(i, i ^ mask) for i in range(sections)])

    def along_z(value):
        return jnp.stack([value] + [along_shard(value, 2 * mask) for mask in range(1, shards // 2)])

    ahead = {mask: along_section(sent, mask) for mask in range(1, sections) if mask & (mask - 1)}
    mine, ahead = lax.optimization_barrier((along_z(sent), ahead))
    gathered = [mine]
    for mask in range(1, sections):
        gathered.append(along_z(ahead[mask]) if mask in ahead else along_section(mine, mask))
    pairs = [(here, along_shard(here, 1)) for here in gathered]
    first = first_products(own, pairs, own.shape[1], sections)
    return second_products(first, pairs, width, sections)


def by_hops(features, own):
    sections = lax.axis_size("section")
    part = features.shape[1] // sections
    piece = lax.dynamic_slice_in_dim(features, lax.axis_index("section") * part, part, axis=1)
    relations = lax.all_gather(own, "section", axis=0, tiled=False)
    pieces = []
    for hop in range(sections):
        slab = lax.all_gather(piece, "shard", axis=0, tiled=True)
        piece = jnp.dot(relations[hop], slab, preferred_element_type=jnp.float32).astype(jnp.bfloat16)
        pieces.append(piece)
    mine = lax.all_to_all(jnp.stack(pieces), "section", split_axis=0, concat_axis=0, tiled=True)
    return jnp.swapaxes(mine, 0, 1).reshape(features.shape)


def per_device(features, tile_cols, live_tiles, tile_values, degrees):
    row_count, width = features.shape
    sections, shards = lax.axis_size("section"), lax.axis_size("shard")
    nodes = row_count * shards
    sent_width = pl.cdiv((sections - 1) * nodes + width, sections * 128) * 128
    even = shards >= 2 and shards & (shards - 1) == 0 and sections > 1 and sections & (sections - 1) == 0
    parts = nodes < sent_width < width and (width - sent_width) % (sent_width - nodes) == 0
    if even and parts:
        own, sent = dense_rows(tile_cols, live_tiles, tile_values[0], degrees, features, sent_width)
        return by_products(own, sent, width)[None]
    (own,) = dense_rows(tile_cols, live_tiles, tile_values[0], degrees, features, 0)
    return by_hops(features, own)[None]


def solution(mesh):
    in_specs = (
        P("shard", None),
        P("section", None, None),
        P("section", None),
        P("section", "shard", None, None),
        P("section", "shard"),
    )
    out_specs = P("section", "shard", None)
    return jax.shard_map(
        per_device, mesh=mesh, in_specs=in_specs, out_specs=out_specs, check_vma=False
    )
```

```python
import functools

import jax
import jax.numpy as jnp
from jax import lax
from jax.experimental import pallas as pl
from jax.experimental.pallas import tpu as pltpu
from jax.sharding import PartitionSpec as P


def dense_rows_kernel(cols_ref, live_ref, tiles_ref, degrees_ref, features_ref, rows_ref, *sent_refs):
    row_count, slots, tile_size = tiles_ref.shape
    nodes = rows_ref.shape[1]
    blocks = nodes // tile_size
    block_row = lax.axis_index("shard") * row_count // tile_size
    live = live_ref[0, block_row]
    wide = row_count * slots
    slot = lax.rem(lax.broadcasted_iota(jnp.int32, (1, wide), 1), slots)
    column = jnp.full((1, wide), -1, jnp.int32)
    for k in range(slots):
        column = jnp.where(slot == k, jnp.where(k < live, cols_ref[0, block_row, k], -1), column)
    owner = lax.div(lax.broadcasted_iota(jnp.int32, (row_count, wide), 1), slots)
    mine = lax.broadcasted_iota(jnp.int32, (row_count, wide), 0) == owner
    column = jnp.where(mine, jnp.broadcast_to(column, (row_count, wide)), -1)
    tiles = tiles_ref[...].reshape(wide, tile_size)
    degree = jnp.broadcast_to(degrees_ref[...].astype(jnp.float32), (row_count, row_count))
    diagonal = lax.broadcasted_iota(jnp.int32, (row_count, row_count), 0) == lax.broadcasted_iota(
        jnp.int32, (row_count, row_count), 1
    )
    scale = lax.rsqrt(jnp.sum(jnp.where(diagonal, degree, 0.0), axis=1, keepdims=True))
    for b in range(blocks):
        pick = (column == b).astype(jnp.bfloat16)
        summed = jnp.dot(pick, tiles, preferred_element_type=jnp.float32)
        rows_ref[:, b * tile_size : (b + 1) * tile_size] = (summed * scale).astype(jnp.bfloat16)
    for sent_ref in sent_refs:
        sections, section = lax.axis_size("section"), lax.axis_index("section")
        bulk, share = sent_ref.shape[1], sent_ref.shape[1] - nodes
        shares = (features_ref.shape[1] - bulk) // share

        @pl.when(section == sections - 1)
        def _():
            sent_ref[...] = features_ref[:, :bulk]

        @pl.when(section < sections - 1)
        def _():
            first = pl.multiple_of(bulk + jnp.minimum(section, shares - 1) * share, 128)
            sent_ref[:, :nodes] = rows_ref[...]
            sent_ref[:, nodes:] = features_ref[:, pl.ds(first, share)]


def dense_rows(tile_cols, live_tiles, tile_rows, degrees, features, sent_width):
    row_count = tile_rows.shape[0]
    nodes = row_count * lax.axis_size("shard")
    widths = [nodes, sent_width] if sent_width else [nodes]
    return pl.pallas_call(
        dense_rows_kernel,
        out_shape=[pltpu.VMEM((row_count, columns), jnp.bfloat16) for columns in widths],
        in_specs=[
            pl.BlockSpec(memory_space=pltpu.SMEM),
            pl.BlockSpec(memory_space=pltpu.SMEM),
            pl.BlockSpec(memory_space=pltpu.VMEM),
            pl.BlockSpec(memory_space=pltpu.VMEM),
            pl.BlockSpec(memory_space=pltpu.VMEM),
        ],
        out_specs=[pl.BlockSpec(memory_space=pltpu.VMEM)] * len(widths),
        name="dense_rows",
    )(tile_cols, live_tiles, tile_rows, degrees, features)


def split_chain(section):
    masks = [section ^ earlier for earlier in reversed(range(section))]
    count = next((i for i, mask in enumerate(masks) if mask & (mask - 1)), len(masks))
    return masks[:count], masks[count:]


def times(halves, pieces, mask, columns):
    row_count = halves.shape[0] // 2
    shard = lax.axis_index("shard")
    chip, first_core = lax.div(shard, 2), lax.rem(shard, 2) == 0
    left, right = [], []
    for piece, (here_ref, there_ref) in enumerate(pieces[mask]):
        source = lax.bitwise_xor(chip, piece)
        left.append(halves[:, pl.ds(pl.multiple_of(source * 2 * row_count, 128), 2 * row_count)])
        here, there = here_ref[:, columns], there_ref[:, columns]
        right += [jnp.where(first_core, here, there), jnp.where(first_core, there, here)]
    left, right = jnp.concatenate(left, axis=1), jnp.concatenate(right, axis=0)
    both = jnp.dot(left, right, preferred_element_type=jnp.float32)
    return both[:row_count] + both[row_count:]


def pieces_of(refs, kinds):
    pieces, at = {}, 0
    for mask, count in kinds:
        here, there = refs[at : at + count], refs[at + count : at + 2 * count]
        if count == 1:
            here, there = ([ref.at[piece] for piece in range(ref.shape[0])] for ref in (here[0], there[0]))
        pieces[mask], at = list(zip(here, there)), at + 2 * count
    return pieces


def multiply_through(halves, pieces, masks):
    row_count, nodes = halves.shape[0] // 2, halves.shape[1]
    for mask in masks:
        product = times(halves, pieces, mask, slice(0, nodes))
        high = product.astype(jnp.bfloat16)
        halves[:row_count] = high
        halves[row_count:] = (product - high.astype(jnp.float32)).astype(jnp.bfloat16)


def first_kernel(kinds, sections, own_ref, *refs):
    pieces, halves = pieces_of(refs[:-1], kinds), refs[-1]
    row_count, nodes = own_ref.shape[0], halves.shape[1]
    halves[:row_count] = own_ref[...]
    halves[row_count:] = jnp.zeros((row_count, nodes), jnp.bfloat16)
    for at in range(sections):
        near, _ = split_chain(at)
        if near:
            pl.when(lax.axis_index("section") == at)(functools.partial(multiply_through, halves, pieces, near))


def second_kernel(kinds, sections, first_ref, *refs):
    pieces, out_ref, halves = pieces_of(refs[:-2], kinds), refs[-2], refs[-1]
    nodes, bulk = halves.shape[1], refs[0].shape[-1]
    share = bulk - nodes
    halves[...] = first_ref[...]
    for at in range(sections):

        @pl.when(lax.axis_index("section") == at)
        def _(at=at):
            multiply_through(halves, pieces, split_chain(at)[1])
            product = times(halves, pieces, at ^ (sections - 1), slice(0, bulk))
            out_ref[:, :bulk] = product.astype(jnp.bfloat16)
            for giver in range((out_ref.shape[1] - bulk) // share):
                product = times(halves, pieces, at ^ giver, slice(nodes, bulk))
                first = bulk + giver * share
                out_ref[:, first : first + share] = product.astype(jnp.bfloat16)


def flat(arrived, masks):
    kinds = [(mask, len(arrived[mask][0])) for mask in masks]
    return kinds, [array for mask in masks for side in arrived[mask] for array in side]


def first_products(own, arrived, sections):
    kinds, operands = flat(arrived, [mask for mask in range(1, sections) if not mask & (mask - 1)])
    return pl.pallas_call(
        functools.partial(first_kernel, kinds, sections),
        out_shape=pltpu.VMEM((2 * own.shape[0], own.shape[1]), jnp.bfloat16),
        in_specs=[pl.BlockSpec(memory_space=pltpu.VMEM)] * (1 + len(operands)),
        out_specs=pl.BlockSpec(memory_space=pltpu.VMEM),
        compiler_params=pltpu.CompilerParams(vmem_limit_bytes=32 * 1024 * 1024),
        name="first_products",
    )(own, *operands)


def second_products(first, arrived, width, sections):
    kinds, operands = flat(arrived, list(range(sections)))
    return pl.pallas_call(
        functools.partial(second_kernel, kinds, sections),
        out_shape=jax.ShapeDtypeStruct((first.shape[0] // 2, width), jnp.bfloat16),
        in_specs=[pl.BlockSpec(memory_space=pltpu.VMEM)] * (1 + len(operands)),
        out_specs=pl.BlockSpec(memory_space=pltpu.VMEM),
        scratch_shapes=[pltpu.VMEM(first.shape, jnp.bfloat16)],
        compiler_params=pltpu.CompilerParams(vmem_limit_bytes=32 * 1024 * 1024),
        name="second_products",
    )(first, *operands)


def by_products(own, sent, width):
    sections, shards = lax.axis_size("section"), lax.axis_size("shard")

    def along_shard(value, mask):
        return lax.ppermute(value, "shard", [(i, i ^ mask) for i in range(shards)])

    def along_section(value, mask):
        return lax.ppermute(value, "section", [(i, i ^ mask) for i in range(sections)])

    def along_z(value):
        return [value] + [along_shard(value, 2 * mask) for mask in range(1, shards // 2)]

    ahead = {mask: along_section(sent, mask) for mask in range(1, sections) if mask & (mask - 1)}
    mine, ahead = lax.optimization_barrier((jnp.stack(along_z(sent)), ahead))
    arrived = [[mine]]
    for mask in range(1, sections):
        arrived.append(along_z(ahead[mask]) if mask in ahead else [along_section(mine, mask)])
    arrived = [(here, [along_shard(array, 1) for array in here]) for here in arrived]
    first = first_products(own, arrived, sections)
    return second_products(first, arrived, width, sections)


def by_hops(features, own):
    sections = lax.axis_size("section")
    part = features.shape[1] // sections
    piece = lax.dynamic_slice_in_dim(features, lax.axis_index("section") * part, part, axis=1)
    relations = lax.all_gather(own, "section", axis=0, tiled=False)
    pieces = []
    for hop in range(sections):
        slab = lax.all_gather(piece, "shard", axis=0, tiled=True)
        piece = jnp.dot(relations[hop], slab, preferred_element_type=jnp.float32).astype(jnp.bfloat16)
        pieces.append(piece)
    mine = lax.all_to_all(jnp.stack(pieces), "section", split_axis=0, concat_axis=0, tiled=True)
    return jnp.swapaxes(mine, 0, 1).reshape(features.shape)


def per_device(features, tile_cols, live_tiles, tile_values, degrees):
    row_count, width = features.shape
    sections, shards = lax.axis_size("section"), lax.axis_size("shard")
    nodes = row_count * shards
    sent_width = pl.cdiv((sections - 1) * nodes + width, sections * 128) * 128
    even = shards >= 2 and shards & (shards - 1) == 0 and sections > 1 and sections & (sections - 1) == 0
    parts = nodes < sent_width < width and (width - sent_width) % (sent_width - nodes) == 0
    if even and parts:
        own, sent = dense_rows(tile_cols, live_tiles, tile_values[0], degrees, features, sent_width)
        return by_products(own, sent, width)[None]
    (own,) = dense_rows(tile_cols, live_tiles, tile_values[0], degrees, features, 0)
    return by_hops(features, own)[None]


def solution(mesh):
    in_specs = (
        P("shard", None),
        P("section", None, None),
        P("section", None),
        P("section", "shard", None, None),
        P("section", "shard"),
    )
    out_specs = P("section", "shard", None)
    return jax.shard_map(
        per_device, mesh=mesh, in_specs=in_specs, out_specs=out_specs, check_vma=False
    )
```

```python
import functools

import jax
import jax.numpy as jnp
from jax import lax
from jax.experimental import pallas as pl
from jax.experimental.pallas import tpu as pltpu
from jax.sharding import PartitionSpec as P


def dense_rows_kernel(cols_ref, live_ref, tiles_ref, degrees_ref, features_ref, rows_ref, *sent_refs):
    row_count, slots, tile_size = tiles_ref.shape
    nodes = rows_ref.shape[1]
    blocks = nodes // tile_size
    block_row = lax.axis_index("shard") * row_count // tile_size
    live = live_ref[0, block_row]
    wide = row_count * slots
    slot = lax.rem(lax.broadcasted_iota(jnp.int32, (1, wide), 1), slots)
    column = jnp.full((1, wide), -1, jnp.int32)
    for k in range(slots):
        column = jnp.where(slot == k, jnp.where(k < live, cols_ref[0, block_row, k], -1), column)
    owner = lax.div(lax.broadcasted_iota(jnp.int32, (row_count, wide), 1), slots)
    mine = lax.broadcasted_iota(jnp.int32, (row_count, wide), 0) == owner
    column = jnp.where(mine, jnp.broadcast_to(column, (row_count, wide)), -1)
    tiles = tiles_ref[...].reshape(wide, tile_size)
    degree = jnp.broadcast_to(degrees_ref[...].astype(jnp.float32), (row_count, row_count))
    diagonal = lax.broadcasted_iota(jnp.int32, (row_count, row_count), 0) == lax.broadcasted_iota(
        jnp.int32, (row_count, row_count), 1
    )
    scale = lax.rsqrt(jnp.sum(jnp.where(diagonal, degree, 0.0), axis=1, keepdims=True))
    for b in range(blocks):
        pick = (column == b).astype(jnp.bfloat16)
        summed = jnp.dot(pick, tiles, preferred_element_type=jnp.float32)
        rows_ref[:, b * tile_size : (b + 1) * tile_size] = (summed * scale).astype(jnp.bfloat16)
    for sent_ref in sent_refs:
        sections, section = lax.axis_size("section"), lax.axis_index("section")
        part = sent_ref.shape[0] - blocks * row_count
        for at in range(sections):

            @pl.when(section == at)
            def _(at=at):
                source = features_ref if at == sections - 1 else rows_ref
                for b in range(blocks):
                    rows = slice(b * row_count, (b + 1) * row_count)
                    sent_ref[rows] = source[:, b * tile_size : (b + 1) * tile_size]
                column, row = nodes + at * part // row_count * tile_size, at * part % row_count
                sent_ref[blocks * row_count :] = features_ref[row : row + part, column : column + tile_size]


def dense_rows(tile_cols, live_tiles, tile_rows, degrees, features, sent_rows):
    row_count = tile_rows.shape[0]
    nodes = row_count * lax.axis_size("shard")
    shapes = [(row_count, nodes)] + ([(sent_rows, tile_rows.shape[2])] if sent_rows else [])
    return pl.pallas_call(
        dense_rows_kernel,
        out_shape=[pltpu.VMEM(shape, jnp.bfloat16) for shape in shapes],
        in_specs=[
            pl.BlockSpec(memory_space=pltpu.SMEM),
            pl.BlockSpec(memory_space=pltpu.SMEM),
            pl.BlockSpec(memory_space=pltpu.VMEM),
            pl.BlockSpec(memory_space=pltpu.VMEM),
            pl.BlockSpec(memory_space=pltpu.VMEM),
        ],
        out_specs=[pl.BlockSpec(memory_space=pltpu.VMEM)] * len(shapes),
        name="dense_rows",
    )(tile_cols, live_tiles, tile_rows, degrees, features)


def split_chain(section):
    masks = [section ^ earlier for earlier in reversed(range(section))]
    count = next((i for i, mask in enumerate(masks) if mask & (mask - 1)), len(masks))
    return masks[:count], masks[count:]


def gathered_rows(pair_refs, mask, first, count):
    first_core = lax.rem(lax.axis_index("shard"), 2) == 0
    here_ref, there_ref = pair_refs[mask]
    found = []
    for piece in range(here_ref.shape[0]):
        here, there = here_ref[piece, first : first + count], there_ref[piece, first : first + count]
        found += [jnp.where(first_core, here, there), jnp.where(first_core, there, here)]
    return found


def times(halves, matrix):
    row_count = halves.shape[0] // 2
    chip, chips = lax.div(lax.axis_index("shard"), 2), len(matrix[0]) // 2
    left = []
    for piece in range(chips):
        source = lax.bitwise_xor(chip, piece)
        left.append(halves[:, pl.ds(pl.multiple_of(source * 2 * row_count, 128), 2 * row_count)])
    left = jnp.concatenate(left, axis=1)
    right = jnp.concatenate([jnp.concatenate(tile, axis=0) for tile in matrix], axis=1)
    both = jnp.dot(left, right, preferred_element_type=jnp.float32)
    return both[:row_count] + both[row_count:]


def stacked_tiles(pair_refs, mask, row_count, tiles):
    return [gathered_rows(pair_refs, mask, tile * row_count, row_count) for tile in range(tiles)]


def multiply_through(halves, pair_refs, masks):
    row_count, tiles = halves.shape[0] // 2, halves.shape[1] // 128
    for mask in masks:
        product = times(halves, stacked_tiles(pair_refs, mask, row_count, tiles))
        high = product.astype(jnp.bfloat16)
        halves[:row_count] = high
        halves[row_count:] = (product - high.astype(jnp.float32)).astype(jnp.bfloat16)


def first_kernel(masks, sections, own_ref, *refs):
    pair_refs, halves = dict(zip(masks, zip(refs[:-1:2], refs[1:-1:2]))), refs[-1]
    row_count, nodes = own_ref.shape[0], halves.shape[1]
    halves[:row_count] = own_ref[...]
    halves[row_count:] = jnp.zeros((row_count, nodes), jnp.bfloat16)
    for at in range(sections):
        near, _ = split_chain(at)
        if near:
            pl.when(lax.axis_index("section") == at)(functools.partial(multiply_through, halves, pair_refs, near))


def second_kernel(sections, first_ref, *refs):
    pair_refs, out_ref, halves = list(zip(refs[:-2:2], refs[1:-2:2])), refs[-2], refs[-1]
    row_count, nodes = halves.shape[0] // 2, halves.shape[1]
    tiles = nodes // 128
    stacked = tiles * row_count
    part = pair_refs[0][0].shape[1] - stacked
    halves[...] = first_ref[...]
    for at in range(sections):

        @pl.when(lax.axis_index("section") == at)
        def _(at=at):
            multiply_through(halves, pair_refs, split_chain(at)[1])
            bulk = stacked_tiles(pair_refs, at ^ (sections - 1), row_count, tiles)
            out_ref[:, :nodes] = times(halves, bulk).astype(jnp.bfloat16)
            parts = [gathered_rows(pair_refs, at ^ giver, stacked, part) for giver in range(sections)]
            each = row_count // part
            rest = [
                [jnp.concatenate(rows, axis=0) for rows in zip(*parts[tile : tile + each])]
                for tile in range(0, sections, each)
            ]
            out_ref[:, nodes:] = times(halves, rest).astype(jnp.bfloat16)


def first_products(own, pairs, nodes, sections):
    masks = [mask for mask in range(1, sections) if not mask & (mask - 1)]
    operands = [array for mask in masks for array in pairs[mask]]
    return pl.pallas_call(
        functools.partial(first_kernel, masks, sections),
        out_shape=pltpu.VMEM((2 * own.shape[0], nodes), jnp.bfloat16),
        in_specs=[pl.BlockSpec(memory_space=pltpu.VMEM)] * (1 + len(operands)),
        out_specs=pl.BlockSpec(memory_space=pltpu.VMEM),
        compiler_params=pltpu.CompilerParams(vmem_limit_bytes=32 * 1024 * 1024),
        name="first_products",
    )(own, *operands)


def second_products(first, pairs, width, sections):
    operands = [array for pair in pairs for array in pair]
    return pl.pallas_call(
        functools.partial(second_kernel, sections),
        out_shape=jax.ShapeDtypeStruct((first.shape[0] // 2, width), jnp.bfloat16),
        in_specs=[pl.BlockSpec(memory_space=pltpu.VMEM)] * (1 + len(operands)),
        out_specs=pl.BlockSpec(memory_space=pltpu.VMEM),
        scratch_shapes=[pltpu.VMEM(first.shape, jnp.bfloat16)],
        compiler_params=pltpu.CompilerParams(vmem_limit_bytes=32 * 1024 * 1024),
        name="second_products",
    )(first, *operands)


def by_products(own, sent, width):
    sections, shards = lax.axis_size("section"), lax.axis_size("shard")

    def along_shard(value, mask):
        return lax.ppermute(value, "shard", [(i, i ^ mask) for i in range(shards)])

    def along_section(value, mask):
        return lax.ppermute(value, "section", [(i, i ^ mask) for i in range(sections)])

    def along_z(value):
        return jnp.stack([value] + [along_shard(value, 2 * mask) for mask in range(1, shards // 2)])

    ahead = {mask: along_section(sent, mask) for mask in range(1, sections) if mask & (mask - 1)}
    mine, ahead = lax.optimization_barrier((along_z(sent), ahead))
    gathered = [mine]
    for mask in range(1, sections):
        gathered.append(along_z(ahead[mask]) if mask in ahead else along_section(mine, mask))
    pairs = [(here, along_shard(here, 1)) for here in gathered]
    first = first_products(own, pairs, own.shape[1], sections)
    return second_products(first, pairs, width, sections)


def by_hops(features, own):
    sections = lax.axis_size("section")
    part = features.shape[1] // sections
    piece = lax.dynamic_slice_in_dim(features, lax.axis_index("section") * part, part, axis=1)
    relations = lax.all_gather(own, "section", axis=0, tiled=False)
    pieces = []
    for hop in range(sections):
        slab = lax.all_gather(piece, "shard", axis=0, tiled=True)
        piece = jnp.dot(relations[hop], slab, preferred_element_type=jnp.float32).astype(jnp.bfloat16)
        pieces.append(piece)
    mine = lax.all_to_all(jnp.stack(pieces), "section", split_axis=0, concat_axis=0, tiled=True)
    return jnp.swapaxes(mine, 0, 1).reshape(features.shape)


def per_device(features, tile_cols, live_tiles, tile_values, degrees):
    row_count, width = features.shape
    sections, shards = lax.axis_size("section"), lax.axis_size("shard")
    nodes = row_count * shards
    tile_size = tile_values.shape[3]
    part = max(width - nodes, 0) // tile_size * row_count // sections
    sent_rows = nodes // tile_size * row_count + part
    even = shards >= 2 and shards & (shards - 1) == 0 and sections > 1 and sections & (sections - 1) == 0
    parts = part >= 16 and part % 16 == 0 and row_count % part == 0 and tile_size == 128
    whole = part * sections * tile_size == (width - nodes) * row_count
    if even and parts and whole:
        own, sent = dense_rows(tile_cols, live_tiles, tile_values[0], degrees, features, sent_rows)
        return by_products(own, sent, width)[None]
    (own,) = dense_rows(tile_cols, live_tiles, tile_values[0], degrees, features, 0)
    return by_hops(features, own)[None]


def solution(mesh):
    in_specs = (
        P("shard", None),
        P("section", None, None),
        P("section", None),
        P("section", "shard", None, None),
        P("section", "shard"),
    )
    out_specs = P("section", "shard", None)
    return jax.shard_map(
        per_device, mesh=mesh, in_specs=in_specs, out_specs=out_specs, check_vma=False
    )
```

```python
import functools

import jax
import jax.numpy as jnp
from jax import lax
from jax.experimental import pallas as pl
from jax.experimental.pallas import tpu as pltpu
from jax.sharding import PartitionSpec as P


def dense_rows_kernel(cols_ref, live_ref, tiles_ref, degrees_ref, features_ref, rows_ref, *sent_refs):
    row_count, slots, tile_size = tiles_ref.shape
    nodes = rows_ref.shape[1]
    blocks = nodes // tile_size
    block_row = lax.axis_index("shard") * row_count // tile_size
    live = live_ref[0, block_row]
    wide = row_count * slots
    slot = lax.rem(lax.broadcasted_iota(jnp.int32, (1, wide), 1), slots)
    column = jnp.full((1, wide), -1, jnp.int32)
    for k in range(slots):
        column = jnp.where(slot == k, jnp.where(k < live, cols_ref[0, block_row, k], -1), column)
    owner = lax.div(lax.broadcasted_iota(jnp.int32, (row_count, wide), 1), slots)
    mine = lax.broadcasted_iota(jnp.int32, (row_count, wide), 0) == owner
    column = jnp.where(mine, jnp.broadcast_to(column, (row_count, wide)), -1)
    tiles = tiles_ref[...].reshape(wide, tile_size)
    degree = jnp.broadcast_to(degrees_ref[...].astype(jnp.float32), (row_count, row_count))
    diagonal = lax.broadcasted_iota(jnp.int32, (row_count, row_count), 0) == lax.broadcasted_iota(
        jnp.int32, (row_count, row_count), 1
    )
    scale = lax.rsqrt(jnp.sum(jnp.where(diagonal, degree, 0.0), axis=1, keepdims=True))
    for start in range(0, blocks, 4):
        group = range(start, min(start + 4, blocks))
        pick = jnp.concatenate([(column == b).astype(jnp.bfloat16) for b in group], axis=0)
        summed = jnp.dot(pick, tiles, preferred_element_type=jnp.float32)
        for at, b in enumerate(group):
            block = summed[at * row_count : (at + 1) * row_count] * scale
            rows_ref[:, b * tile_size : (b + 1) * tile_size] = block.astype(jnp.bfloat16)
    for sent_ref in sent_refs:
        sections, section = lax.axis_size("section"), lax.axis_index("section")
        part = sent_ref.shape[0] - blocks * row_count
        for at in range(sections):

            @pl.when(section == at)
            def _(at=at):
                source = features_ref if at == sections - 1 else rows_ref
                for b in range(blocks):
                    rows = slice(b * row_count, (b + 1) * row_count)
                    sent_ref[rows] = source[:, b * tile_size : (b + 1) * tile_size]
                column, row = nodes + at * part // row_count * tile_size, at * part % row_count
                sent_ref[blocks * row_count :] = features_ref[row : row + part, column : column + tile_size]


def dense_rows(tile_cols, live_tiles, tile_rows, degrees, features, sent_rows):
    row_count = tile_rows.shape[0]
    nodes = row_count * lax.axis_size("shard")
    shapes = [(row_count, nodes)] + ([(sent_rows, tile_rows.shape[2])] if sent_rows else [])
    return pl.pallas_call(
        dense_rows_kernel,
        out_shape=[pltpu.VMEM(shape, jnp.bfloat16) for shape in shapes],
        in_specs=[
            pl.BlockSpec(memory_space=pltpu.SMEM),
            pl.BlockSpec(memory_space=pltpu.SMEM),
            pl.BlockSpec(memory_space=pltpu.VMEM),
            pl.BlockSpec(memory_space=pltpu.VMEM),
            pl.BlockSpec(memory_space=pltpu.VMEM),
        ],
        out_specs=[pl.BlockSpec(memory_space=pltpu.VMEM)] * len(shapes),
        name="dense_rows",
    )(tile_cols, live_tiles, tile_rows, degrees, features)


def split_chain(section):
    masks = [section ^ earlier for earlier in reversed(range(section))]
    count = next((i for i, mask in enumerate(masks) if mask & (mask - 1)), len(masks))
    return masks[:count], masks[count:]


def gathered_rows(pair_refs, mask, first, count):
    first_core = lax.rem(lax.axis_index("shard"), 2) == 0
    here_ref, there_ref = pair_refs[mask]
    found = []
    for piece in range(here_ref.shape[0]):
        here, there = here_ref[piece, first : first + count], there_ref[piece, first : first + count]
        found += [jnp.where(first_core, here, there), jnp.where(first_core, there, here)]
    return found


def times(halves, matrix):
    row_count = halves.shape[0] // 2
    chip, chips = lax.div(lax.axis_index("shard"), 2), len(matrix[0]) // 2
    left = []
    for piece in range(chips):
        source = lax.bitwise_xor(chip, piece)
        left.append(halves[:, pl.ds(pl.multiple_of(source * 2 * row_count, 128), 2 * row_count)])
    left = jnp.concatenate(left, axis=1)
    right = jnp.concatenate([jnp.concatenate(tile, axis=0) for tile in matrix], axis=1)
    both = jnp.dot(left, right, preferred_element_type=jnp.float32)
    return both[:row_count] + both[row_count:]


def stacked_tiles(pair_refs, mask, row_count, tiles):
    return [gathered_rows(pair_refs, mask, tile * row_count, row_count) for tile in range(tiles)]


def multiply_through(halves, pair_refs, masks):
    row_count, tiles = halves.shape[0] // 2, halves.shape[1] // 128
    for mask in masks:
        product = times(halves, stacked_tiles(pair_refs, mask, row_count, tiles))
        high = product.astype(jnp.bfloat16)
        halves[:row_count] = high
        halves[row_count:] = (product - high.astype(jnp.float32)).astype(jnp.bfloat16)


def first_kernel(masks, sections, own_ref, *refs):
    pair_refs, halves = dict(zip(masks, zip(refs[:-1:2], refs[1:-1:2]))), refs[-1]
    row_count, nodes = own_ref.shape[0], halves.shape[1]
    halves[:row_count] = own_ref[...]
    halves[row_count:] = jnp.zeros((row_count, nodes), jnp.bfloat16)
    for at in range(sections):
        near, _ = split_chain(at)
        if near:
            pl.when(lax.axis_index("section") == at)(functools.partial(multiply_through, halves, pair_refs, near))


def second_kernel(sections, first_ref, *refs):
    pair_refs, out_ref, halves = list(zip(refs[:-2:2], refs[1:-2:2])), refs[-2], refs[-1]
    row_count, nodes = halves.shape[0] // 2, halves.shape[1]
    tiles = nodes // 128
    stacked = tiles * row_count
    part = pair_refs[0][0].shape[1] - stacked
    halves[...] = first_ref[...]
    for at in range(sections):

        @pl.when(lax.axis_index("section") == at)
        def _(at=at):
            multiply_through(halves, pair_refs, split_chain(at)[1])
            bulk = stacked_tiles(pair_refs, at ^ (sections - 1), row_count, tiles)
            out_ref[:, :nodes] = times(halves, bulk).astype(jnp.bfloat16)
            parts = [gathered_rows(pair_refs, at ^ giver, stacked, part) for giver in range(sections)]
            each = row_count // part
            rest = [
                [jnp.concatenate(rows, axis=0) for rows in zip(*parts[tile : tile + each])]
                for tile in range(0, sections, each)
            ]
            out_ref[:, nodes:] = times(halves, rest).astype(jnp.bfloat16)


def first_products(own, pairs, nodes, sections):
    masks = [mask for mask in range(1, sections) if not mask & (mask - 1)]
    operands = [array for mask in masks for array in pairs[mask]]
    return pl.pallas_call(
        functools.partial(first_kernel, masks, sections),
        out_shape=pltpu.VMEM((2 * own.shape[0], nodes), jnp.bfloat16),
        in_specs=[pl.BlockSpec(memory_space=pltpu.VMEM)] * (1 + len(operands)),
        out_specs=pl.BlockSpec(memory_space=pltpu.VMEM),
        compiler_params=pltpu.CompilerParams(vmem_limit_bytes=32 * 1024 * 1024),
        name="first_products",
    )(own, *operands)


def second_products(first, pairs, width, sections):
    operands = [array for pair in pairs for array in pair]
    return pl.pallas_call(
        functools.partial(second_kernel, sections),
        out_shape=jax.ShapeDtypeStruct((first.shape[0] // 2, width), jnp.bfloat16),
        in_specs=[pl.BlockSpec(memory_space=pltpu.VMEM)] * (1 + len(operands)),
        out_specs=pl.BlockSpec(memory_space=pltpu.VMEM),
        scratch_shapes=[pltpu.VMEM(first.shape, jnp.bfloat16)],
        compiler_params=pltpu.CompilerParams(vmem_limit_bytes=32 * 1024 * 1024),
        name="second_products",
    )(first, *operands)


def by_products(own, sent, width):
    sections, shards = lax.axis_size("section"), lax.axis_size("shard")

    def along_shard(value, mask):
        return lax.ppermute(value, "shard", [(i, i ^ mask) for i in range(shards)])

    def along_section(value, mask):
        return lax.ppermute(value, "section", [(i, i ^ mask) for i in range(sections)])

    def along_z(value):
        return jnp.stack([value] + [along_shard(value, 2 * mask) for mask in range(1, shards // 2)])

    ahead = {mask: along_section(sent, mask) for mask in range(1, sections) if mask & (mask - 1)}
    mine, ahead = lax.optimization_barrier((along_z(sent), ahead))
    gathered = [mine]
    for mask in range(1, sections):
        gathered.append(along_z(ahead[mask]) if mask in ahead else along_section(mine, mask))
    pairs = [(here, along_shard(here, 1)) for here in gathered]
    first = first_products(own, pairs, own.shape[1], sections)
    return second_products(first, pairs, width, sections)


def by_hops(features, own):
    sections = lax.axis_size("section")
    part = features.shape[1] // sections
    piece = lax.dynamic_slice_in_dim(features, lax.axis_index("section") * part, part, axis=1)
    relations = lax.all_gather(own, "section", axis=0, tiled=False)
    pieces = []
    for hop in range(sections):
        slab = lax.all_gather(piece, "shard", axis=0, tiled=True)
        piece = jnp.dot(relations[hop], slab, preferred_element_type=jnp.float32).astype(jnp.bfloat16)
        pieces.append(piece)
    mine = lax.all_to_all(jnp.stack(pieces), "section", split_axis=0, concat_axis=0, tiled=True)
    return jnp.swapaxes(mine, 0, 1).reshape(features.shape)


def per_device(features, tile_cols, live_tiles, tile_values, degrees):
    row_count, width = features.shape
    sections, shards = lax.axis_size("section"), lax.axis_size("shard")
    nodes = row_count * shards
    tile_size = tile_values.shape[3]
    part = max(width - nodes, 0) // tile_size * row_count // sections
    sent_rows = nodes // tile_size * row_count + part
    even = shards >= 2 and shards & (shards - 1) == 0 and sections > 1 and sections & (sections - 1) == 0
    parts = part >= 16 and part % 16 == 0 and row_count % part == 0 and tile_size == 128
    whole = part * sections * tile_size == (width - nodes) * row_count
    if even and parts and whole:
        own, sent = dense_rows(tile_cols, live_tiles, tile_values[0], degrees, features, sent_rows)
        return by_products(own, sent, width)[None]
    (own,) = dense_rows(tile_cols, live_tiles, tile_values[0], degrees, features, 0)
    return by_hops(features, own)[None]


def solution(mesh):
    in_specs = (
        P("shard", None),
        P("section", None, None),
        P("section", None),
        P("section", "shard", None, None),
        P("section", "shard"),
    )
    out_specs = P("section", "shard", None)
    return jax.shard_map(
        per_device, mesh=mesh, in_specs=in_specs, out_specs=out_specs, check_vma=False
    )
```

```python
import functools

import jax
import jax.numpy as jnp
from jax import lax
from jax.experimental import pallas as pl
from jax.experimental.pallas import tpu as pltpu
from jax.sharding import PartitionSpec as P


def dense_rows_kernel(cols_ref, live_ref, tiles_ref, degrees_ref, features_ref, rows_ref, *sent_refs):
    row_count, slots, tile_size = tiles_ref.shape
    nodes = rows_ref.shape[1]
    blocks = nodes // tile_size
    block_row = lax.axis_index("shard") * row_count // tile_size
    live = live_ref[0, block_row]
    wide = row_count * slots
    slot = lax.rem(lax.broadcasted_iota(jnp.int32, (1, wide), 1), slots)
    column = jnp.full((1, wide), -1, jnp.int32)
    for k in range(slots):
        column = jnp.where(slot == k, jnp.where(k < live, cols_ref[0, block_row, k], -1), column)
    owner = lax.div(lax.broadcasted_iota(jnp.int32, (row_count, wide), 1), slots)
    mine = lax.broadcasted_iota(jnp.int32, (row_count, wide), 0) == owner
    column = jnp.where(mine, jnp.broadcast_to(column, (row_count, wide)), -1)
    tiles = tiles_ref[...].reshape(wide, tile_size)
    degree = jnp.broadcast_to(degrees_ref[...].astype(jnp.float32), (row_count, row_count))
    diagonal = lax.broadcasted_iota(jnp.int32, (row_count, row_count), 0) == lax.broadcasted_iota(
        jnp.int32, (row_count, row_count), 1
    )
    scale = lax.rsqrt(jnp.sum(jnp.where(diagonal, degree, 0.0), axis=1, keepdims=True))
    for b in range(blocks):
        pick = (column == b).astype(jnp.bfloat16)
        summed = jnp.dot(pick, tiles, preferred_element_type=jnp.float32)
        rows_ref[:, b * tile_size : (b + 1) * tile_size] = (summed * scale).astype(jnp.bfloat16)
    for sent_ref in sent_refs:
        sections, section = lax.axis_size("section"), lax.axis_index("section")
        part = sent_ref.shape[0] - blocks * row_count
        for at in range(sections):

            @pl.when(section == at)
            def _(at=at):
                source = features_ref if at == sections - 1 else rows_ref
                for b in range(blocks):
                    rows = slice(b * row_count, (b + 1) * row_count)
                    sent_ref[rows] = source[:, b * tile_size : (b + 1) * tile_size]
                column, row = nodes + at * part // row_count * tile_size, at * part % row_count
                sent_ref[blocks * row_count :] = features_ref[row : row + part, column : column + tile_size]


def dense_rows(tile_cols, live_tiles, tile_rows, degrees, features, sent_rows):
    row_count = tile_rows.shape[0]
    nodes = row_count * lax.axis_size("shard")
    shapes = [(row_count, nodes)] + ([(sent_rows, tile_rows.shape[2])] if sent_rows else [])
    return pl.pallas_call(
        dense_rows_kernel,
        out_shape=[pltpu.VMEM(shape, jnp.bfloat16) for shape in shapes],
        in_specs=[
            pl.BlockSpec(memory_space=pltpu.SMEM),
            pl.BlockSpec(memory_space=pltpu.SMEM),
            pl.BlockSpec(memory_space=pltpu.VMEM),
            pl.BlockSpec(memory_space=pltpu.VMEM),
            pl.BlockSpec(memory_space=pltpu.VMEM),
        ],
        out_specs=[pl.BlockSpec(memory_space=pltpu.VMEM)] * len(shapes),
        name="dense_rows",
    )(tile_cols, live_tiles, tile_rows, degrees, features)


def split_chain(section):
    masks = [section ^ earlier for earlier in reversed(range(section))]
    count = next((i for i, mask in enumerate(masks) if mask & (mask - 1)), len(masks))
    return masks[:count], masks[count:]


def gathered_rows(pair_refs, mask, first, count):
    first_core = lax.rem(lax.axis_index("shard"), 2) == 0
    found = {}
    for here_ref, there_ref, order in pair_refs[mask]:
        for piece, source in enumerate(order):
            here, there = here_ref[piece, first : first + count], there_ref[piece, first : first + count]
            found[source] = [jnp.where(first_core, here, there), jnp.where(first_core, there, here)]
    return [rows for source in sorted(found) for rows in found[source]]


def times(halves, matrix):
    row_count = halves.shape[0] // 2
    chip, chips = lax.div(lax.axis_index("shard"), 2), len(matrix[0]) // 2
    left = []
    for piece in range(chips):
        source = lax.bitwise_xor(chip, piece)
        left.append(halves[:, pl.ds(pl.multiple_of(source * 2 * row_count, 128), 2 * row_count)])
    left = jnp.concatenate(left, axis=1)
    right = jnp.concatenate([jnp.concatenate(tile, axis=0) for tile in matrix], axis=1)
    both = jnp.dot(left, right, preferred_element_type=jnp.float32)
    return both[:row_count] + both[row_count:]


def by_mask(refs, orders):
    refs = iter(refs)
    return {mask: [(next(refs), next(refs), order) for order in groups] for mask, groups in orders}


def stacked_tiles(pair_refs, mask, row_count, tiles):
    return [gathered_rows(pair_refs, mask, tile * row_count, row_count) for tile in range(tiles)]


def multiply_through(halves, pair_refs, masks):
    row_count, tiles = halves.shape[0] // 2, halves.shape[1] // 128
    for mask in masks:
        product = times(halves, stacked_tiles(pair_refs, mask, row_count, tiles))
        high = product.astype(jnp.bfloat16)
        halves[:row_count] = high
        halves[row_count:] = (product - high.astype(jnp.float32)).astype(jnp.bfloat16)


def first_kernel(orders, sections, own_ref, *refs):
    pair_refs, halves = by_mask(refs[:-1], orders), refs[-1]
    row_count, nodes = own_ref.shape[0], halves.shape[1]
    halves[:row_count] = own_ref[...]
    halves[row_count:] = jnp.zeros((row_count, nodes), jnp.bfloat16)
    for at in range(sections):
        near, _ = split_chain(at)
        if near:
            pl.when(lax.axis_index("section") == at)(functools.partial(multiply_through, halves, pair_refs, near))


def second_kernel(orders, sections, first_ref, *refs):
    pair_refs, out_ref, halves = by_mask(refs[:-2], orders), refs[-2], refs[-1]
    row_count, nodes = halves.shape[0] // 2, halves.shape[1]
    tiles = nodes // 128
    stacked = tiles * row_count
    part = refs[0].shape[1] - stacked
    halves[...] = first_ref[...]
    for at in range(sections):

        @pl.when(lax.axis_index("section") == at)
        def _(at=at):
            multiply_through(halves, pair_refs, split_chain(at)[1])
            bulk = stacked_tiles(pair_refs, at ^ (sections - 1), row_count, tiles)
            out_ref[:, :nodes] = times(halves, bulk).astype(jnp.bfloat16)
            parts = [gathered_rows(pair_refs, at ^ giver, stacked, part) for giver in range(sections)]
            each = row_count // part
            rest = [
                [jnp.concatenate(rows, axis=0) for rows in zip(*parts[tile : tile + each])]
                for tile in range(0, sections, each)
            ]
            out_ref[:, nodes:] = times(halves, rest).astype(jnp.bfloat16)


def flat(pairs, masks):
    orders = [(mask, [order for order, _ in pairs[mask]]) for mask in masks]
    return orders, [array for mask in masks for _, pair in pairs[mask] for array in pair]


def first_products(own, pairs, nodes, sections):
    orders, operands = flat(pairs, [mask for mask in range(1, sections) if not mask & (mask - 1)])
    return pl.pallas_call(
        functools.partial(first_kernel, orders, sections),
        out_shape=pltpu.VMEM((2 * own.shape[0], nodes), jnp.bfloat16),
        in_specs=[pl.BlockSpec(memory_space=pltpu.VMEM)] * (1 + len(operands)),
        out_specs=pl.BlockSpec(memory_space=pltpu.VMEM),
        compiler_params=pltpu.CompilerParams(vmem_limit_bytes=32 * 1024 * 1024),
        name="first_products",
    )(own, *operands)


def second_products(first, pairs, width, sections):
    orders, operands = flat(pairs, list(range(sections)))
    return pl.pallas_call(
        functools.partial(second_kernel, orders, sections),
        out_shape=jax.ShapeDtypeStruct((first.shape[0] // 2, width), jnp.bfloat16),
        in_specs=[pl.BlockSpec(memory_space=pltpu.VMEM)] * (1 + len(operands)),
        out_specs=pl.BlockSpec(memory_space=pltpu.VMEM),
        scratch_shapes=[pltpu.VMEM(first.shape, jnp.bfloat16)],
        compiler_params=pltpu.CompilerParams(vmem_limit_bytes=32 * 1024 * 1024),
        name="second_products",
    )(first, *operands)


def by_products(own, sent, width):
    sections, shards = lax.axis_size("section"), lax.axis_size("shard")

    def along_shard(value, mask):
        return lax.ppermute(value, "shard", [(i, i ^ mask) for i in range(shards)])

    def along_section(value, mask):
        return lax.ppermute(value, "section", [(i, i ^ mask) for i in range(sections)])

    def along_z(value, groups):
        came = [value] + [along_shard(value, 2 * mask) for mask in range(1, shards // 2)]
        return [jnp.stack([came[mask] for mask in order]) for order in groups]

    whole = [list(range(shards // 2))]
    last_first = [0] + whole[0][:0:-1]
    in_two = [last_first[: shards // 4], last_first[shards // 4 :]]

    ahead = {mask: along_section(sent, mask) for mask in range(1, sections) if mask & (mask - 1)}
    mine, ahead = lax.optimization_barrier((along_z(sent, whole)[0], ahead))
    arrived = [(whole, [mine])]
    for mask in range(1, sections):
        if mask in ahead:
            arrived.append((in_two, along_z(ahead[mask], in_two)))
        else:
            arrived.append((whole, [along_section(mine, mask)]))
    pairs = [[(order, (here, along_shard(here, 1))) for order, here in zip(*group)] for group in arrived]
    first = first_products(own, pairs, own.shape[1], sections)
    return second_products(first, pairs, width, sections)


def by_hops(features, own):
    sections = lax.axis_size("section")
    part = features.shape[1] // sections
    piece = lax.dynamic_slice_in_dim(features, lax.axis_index("section") * part, part, axis=1)
    relations = lax.all_gather(own, "section", axis=0, tiled=False)
    pieces = []
    for hop in range(sections):
        slab = lax.all_gather(piece, "shard", axis=0, tiled=True)
        piece = jnp.dot(relations[hop], slab, preferred_element_type=jnp.float32).astype(jnp.bfloat16)
        pieces.append(piece)
    mine = lax.all_to_all(jnp.stack(pieces), "section", split_axis=0, concat_axis=0, tiled=True)
    return jnp.swapaxes(mine, 0, 1).reshape(features.shape)


def per_device(features, tile_cols, live_tiles, tile_values, degrees):
    row_count, width = features.shape
    sections, shards = lax.axis_size("section"), lax.axis_size("shard")
    nodes = row_count * shards
    tile_size = tile_values.shape[3]
    part = max(width - nodes, 0) // tile_size * row_count // sections
    sent_rows = nodes // tile_size * row_count + part
    even = shards >= 4 and shards & (shards - 1) == 0 and sections > 1 and sections & (sections - 1) == 0
    parts = part >= 16 and part % 16 == 0 and row_count % part == 0 and tile_size == 128
    whole = part * sections * tile_size == (width - nodes) * row_count
    if even and parts and whole:
        own, sent = dense_rows(tile_cols, live_tiles, tile_values[0], degrees, features, sent_rows)
        return by_products(own, sent, width)[None]
    (own,) = dense_rows(tile_cols, live_tiles, tile_values[0], degrees, features, 0)
    return by_hops(features, own)[None]


def solution(mesh):
    in_specs = (
        P("shard", None),
        P("section", None, None),
        P("section", None),
        P("section", "shard", None, None),
        P("section", "shard"),
    )
    out_specs = P("section", "shard", None)
    return jax.shard_map(
        per_device, mesh=mesh, in_specs=in_specs, out_specs=out_specs, check_vma=False
    )
```

```python
import functools

import jax
import jax.numpy as jnp
from jax import lax
from jax.experimental import pallas as pl
from jax.experimental.pallas import tpu as pltpu
from jax.sharding import PartitionSpec as P


def dense_rows_kernel(cols_ref, live_ref, tiles_ref, degrees_ref, features_ref, rows_ref, *rest):
    *sent_refs, arrived, arrival = rest
    copy = pltpu.make_async_copy(tiles_ref, arrived, arrival)
    copy.start()
    row_count, slots, tile_size = tiles_ref.shape
    nodes = rows_ref.shape[1]
    blocks = nodes // tile_size
    block_row = lax.axis_index("shard") * row_count // tile_size
    live = live_ref[0, block_row]
    wide = row_count * slots
    slot = lax.rem(lax.broadcasted_iota(jnp.int32, (1, wide), 1), slots)
    column = jnp.full((1, wide), -1, jnp.int32)
    for k in range(slots):
        column = jnp.where(slot == k, jnp.where(k < live, cols_ref[0, block_row, k], -1), column)
    owner = lax.div(lax.broadcasted_iota(jnp.int32, (row_count, wide), 1), slots)
    mine = lax.broadcasted_iota(jnp.int32, (row_count, wide), 0) == owner
    column = jnp.where(mine, jnp.broadcast_to(column, (row_count, wide)), -1)
    degree = jnp.broadcast_to(degrees_ref[...].astype(jnp.float32), (row_count, row_count))
    diagonal = lax.broadcasted_iota(jnp.int32, (row_count, row_count), 0) == lax.broadcasted_iota(
        jnp.int32, (row_count, row_count), 1
    )
    scale = lax.rsqrt(jnp.sum(jnp.where(diagonal, degree, 0.0), axis=1, keepdims=True))
    copy.wait()
    tiles = arrived[...].reshape(wide, tile_size)
    for b in range(blocks):
        pick = (column == b).astype(jnp.bfloat16)
        summed = jnp.dot(pick, tiles, preferred_element_type=jnp.float32)
        rows_ref[:, b * tile_size : (b + 1) * tile_size] = (summed * scale).astype(jnp.bfloat16)
    for sent_ref in sent_refs:
        sections, section = lax.axis_size("section"), lax.axis_index("section")
        part = sent_ref.shape[0] - blocks * row_count
        for at in range(sections):

            @pl.when(section == at)
            def _(at=at):
                source = features_ref if at == sections - 1 else rows_ref
                for b in range(blocks):
                    rows = slice(b * row_count, (b + 1) * row_count)
                    sent_ref[rows] = source[:, b * tile_size : (b + 1) * tile_size]
                column, row = nodes + at * part // row_count * tile_size, at * part % row_count
                sent_ref[blocks * row_count :] = features_ref[row : row + part, column : column + tile_size]


def dense_rows(tile_cols, live_tiles, tile_rows, degrees, features, sent_rows):
    row_count = tile_rows.shape[0]
    nodes = row_count * lax.axis_size("shard")
    shapes = [(row_count, nodes)] + ([(sent_rows, tile_rows.shape[2])] if sent_rows else [])
    return pl.pallas_call(
        dense_rows_kernel,
        out_shape=[pltpu.VMEM(shape, jnp.bfloat16) for shape in shapes],
        in_specs=[
            pl.BlockSpec(memory_space=pltpu.SMEM),
            pl.BlockSpec(memory_space=pltpu.SMEM),
            pl.BlockSpec(memory_space=pl.ANY),
            pl.BlockSpec(memory_space=pltpu.VMEM),
            pl.BlockSpec(memory_space=pltpu.VMEM),
        ],
        out_specs=[pl.BlockSpec(memory_space=pltpu.VMEM)] * len(shapes),
        scratch_shapes=[pltpu.VMEM(tile_rows.shape, tile_rows.dtype), pltpu.SemaphoreType.DMA],
        name="dense_rows",
    )(tile_cols, live_tiles, tile_rows, degrees, features)


def split_chain(section):
    masks = [section ^ earlier for earlier in reversed(range(section))]
    count = next((i for i, mask in enumerate(masks) if mask & (mask - 1)), len(masks))
    return masks[:count], masks[count:]


def gathered_rows(pair_refs, mask, first, count):
    first_core = lax.rem(lax.axis_index("shard"), 2) == 0
    found = {}
    for here_ref, there_ref, order in pair_refs[mask]:
        for piece, source in enumerate(order):
            here, there = here_ref[piece, first : first + count], there_ref[piece, first : first + count]
            found[source] = [jnp.where(first_core, here, there), jnp.where(first_core, there, here)]
    return [rows for source in sorted(found) for rows in found[source]]


def times(halves, matrix):
    row_count = halves.shape[0] // 2
    chip, chips = lax.div(lax.axis_index("shard"), 2), len(matrix[0]) // 2
    left = []
    for piece in range(chips):
        source = lax.bitwise_xor(chip, piece)
        left.append(halves[:, pl.ds(pl.multiple_of(source * 2 * row_count, 128), 2 * row_count)])
    left = jnp.concatenate(left, axis=1)
    right = jnp.concatenate([jnp.concatenate(tile, axis=0) for tile in matrix], axis=1)
    both = jnp.dot(left, right, preferred_element_type=jnp.float32)
    return both[:row_count] + both[row_count:]


def by_mask(refs, orders):
    refs = iter(refs)
    return {mask: [(next(refs), next(refs), order) for order in groups] for mask, groups in orders}


def stacked_tiles(pair_refs, mask, row_count, tiles):
    return [gathered_rows(pair_refs, mask, tile * row_count, row_count) for tile in range(tiles)]


def multiply_through(halves, pair_refs, masks):
    row_count, tiles = halves.shape[0] // 2, halves.shape[1] // 128
    for mask in masks:
        product = times(halves, stacked_tiles(pair_refs, mask, row_count, tiles))
        high = product.astype(jnp.bfloat16)
        halves[:row_count] = high
        halves[row_count:] = (product - high.astype(jnp.float32)).astype(jnp.bfloat16)


def first_kernel(orders, sections, own_ref, *refs):
    pair_refs, halves = by_mask(refs[:-1], orders), refs[-1]
    row_count, nodes = own_ref.shape[0], halves.shape[1]
    halves[:row_count] = own_ref[...]
    halves[row_count:] = jnp.zeros((row_count, nodes), jnp.bfloat16)
    for at in range(sections):
        near, _ = split_chain(at)
        if near:
            pl.when(lax.axis_index("section") == at)(functools.partial(multiply_through, halves, pair_refs, near))


def second_kernel(orders, sections, first_ref, *refs):
    pair_refs, out_ref, halves = by_mask(refs[:-2], orders), refs[-2], refs[-1]
    row_count, nodes = halves.shape[0] // 2, halves.shape[1]
    tiles = nodes // 128
    stacked = tiles * row_count
    part = refs[0].shape[1] - stacked
    halves[...] = first_ref[...]
    for at in range(sections):

        @pl.when(lax.axis_index("section") == at)
        def _(at=at):
            multiply_through(halves, pair_refs, split_chain(at)[1])
            bulk = stacked_tiles(pair_refs, at ^ (sections - 1), row_count, tiles)
            out_ref[:, :nodes] = times(halves, bulk).astype(jnp.bfloat16)
            parts = [gathered_rows(pair_refs, at ^ giver, stacked, part) for giver in range(sections)]
            each = row_count // part
            rest = [
                [jnp.concatenate(rows, axis=0) for rows in zip(*parts[tile : tile + each])]
                for tile in range(0, sections, each)
            ]
            out_ref[:, nodes:] = times(halves, rest).astype(jnp.bfloat16)


def flat(pairs, masks):
    orders = [(mask, [order for order, _ in pairs[mask]]) for mask in masks]
    return orders, [array for mask in masks for _, pair in pairs[mask] for array in pair]


def first_products(own, pairs, nodes, sections):
    orders, operands = flat(pairs, [mask for mask in range(1, sections) if not mask & (mask - 1)])
    return pl.pallas_call(
        functools.partial(first_kernel, orders, sections),
        out_shape=pltpu.VMEM((2 * own.shape[0], nodes), jnp.bfloat16),
        in_specs=[pl.BlockSpec(memory_space=pltpu.VMEM)] * (1 + len(operands)),
        out_specs=pl.BlockSpec(memory_space=pltpu.VMEM),
        compiler_params=pltpu.CompilerParams(vmem_limit_bytes=32 * 1024 * 1024),
        name="first_products",
    )(own, *operands)


def second_products(first, pairs, width, sections):
    orders, operands = flat(pairs, list(range(sections)))
    return pl.pallas_call(
        functools.partial(second_kernel, orders, sections),
        out_shape=jax.ShapeDtypeStruct((first.shape[0] // 2, width), jnp.bfloat16),
        in_specs=[pl.BlockSpec(memory_space=pltpu.VMEM)] * (1 + len(operands)),
        out_specs=pl.BlockSpec(memory_space=pltpu.VMEM),
        scratch_shapes=[pltpu.VMEM(first.shape, jnp.bfloat16)],
        compiler_params=pltpu.CompilerParams(vmem_limit_bytes=32 * 1024 * 1024),
        name="second_products",
    )(first, *operands)


def by_products(own, sent, width):
    sections, shards = lax.axis_size("section"), lax.axis_size("shard")

    def along_shard(value, mask):
        return lax.ppermute(value, "shard", [(i, i ^ mask) for i in range(shards)])

    def along_section(value, mask):
        return lax.ppermute(value, "section", [(i, i ^ mask) for i in range(sections)])

    def along_z(value, groups):
        came = [value] + [along_shard(value, 2 * mask) for mask in range(1, shards // 2)]
        return [jnp.stack([came[mask] for mask in order]) for order in groups]

    whole = [list(range(shards // 2))]
    last_first = [0] + whole[0][:0:-1]
    in_two = [last_first[: shards // 4], last_first[shards // 4 :]]

    ahead = {mask: along_section(sent, mask) for mask in range(1, sections) if mask & (mask - 1)}
    mine, ahead = lax.optimization_barrier((along_z(sent, whole)[0], ahead))
    arrived = [(whole, [mine])]
    for mask in range(1, sections):
        if mask in ahead:
            arrived.append((in_two, along_z(ahead[mask], in_two)))
        else:
            arrived.append((whole, [along_section(mine, mask)]))
    pairs = [[(order, (here, along_shard(here, 1))) for order, here in zip(*group)] for group in arrived]
    first = first_products(own, pairs, own.shape[1], sections)
    return second_products(first, pairs, width, sections)


def by_hops(features, own):
    sections = lax.axis_size("section")
    part = features.shape[1] // sections
    piece = lax.dynamic_slice_in_dim(features, lax.axis_index("section") * part, part, axis=1)
    relations = lax.all_gather(own, "section", axis=0, tiled=False)
    pieces = []
    for hop in range(sections):
        slab = lax.all_gather(piece, "shard", axis=0, tiled=True)
        piece = jnp.dot(relations[hop], slab, preferred_element_type=jnp.float32).astype(jnp.bfloat16)
        pieces.append(piece)
    mine = lax.all_to_all(jnp.stack(pieces), "section", split_axis=0, concat_axis=0, tiled=True)
    return jnp.swapaxes(mine, 0, 1).reshape(features.shape)


def per_device(features, tile_cols, live_tiles, tile_values, degrees):
    row_count, width = features.shape
    sections, shards = lax.axis_size("section"), lax.axis_size("shard")
    nodes = row_count * shards
    tile_size = tile_values.shape[3]
    part = max(width - nodes, 0) // tile_size * row_count // sections
    sent_rows = nodes // tile_size * row_count + part
    even = shards >= 4 and shards & (shards - 1) == 0 and sections > 1 and sections & (sections - 1) == 0
    parts = part >= 16 and part % 16 == 0 and row_count % part == 0 and tile_size == 128
    whole = part * sections * tile_size == (width - nodes) * row_count
    if even and parts and whole:
        own, sent = dense_rows(tile_cols, live_tiles, tile_values[0], degrees, features, sent_rows)
        return by_products(own, sent, width)[None]
    (own,) = dense_rows(tile_cols, live_tiles, tile_values[0], degrees, features, 0)
    return by_hops(features, own)[None]


def solution(mesh):
    in_specs = (
        P("shard", None),
        P("section", None, None),
        P("section", None),
        P("section", "shard", None, None),
        P("section", "shard"),
    )
    out_specs = P("section", "shard", None)
    return jax.shard_map(
        per_device, mesh=mesh, in_specs=in_specs, out_specs=out_specs, check_vma=False
    )
```

```python
import functools

import jax
import jax.numpy as jnp
from jax import lax
from jax.experimental import pallas as pl
from jax.experimental.pallas import tpu as pltpu
from jax.sharding import PartitionSpec as P


def dense_rows_kernel(cols_ref, live_ref, tiles_ref, degrees_ref, features_ref, rows_ref, *sent_refs):
    row_count, slots, tile_size = tiles_ref.shape
    nodes = rows_ref.shape[1]
    blocks = nodes // tile_size
    block_row = lax.axis_index("shard") * row_count // tile_size
    live = live_ref[0, block_row]
    wide = row_count * slots
    slot = lax.rem(lax.broadcasted_iota(jnp.int32, (1, wide), 1), slots)
    column = jnp.full((1, wide), -1, jnp.int32)
    for k in range(slots):
        column = jnp.where(slot == k, jnp.where(k < live, cols_ref[0, block_row, k], -1), column)
    owner = lax.div(lax.broadcasted_iota(jnp.int32, (row_count, wide), 1), slots)
    mine = lax.broadcasted_iota(jnp.int32, (row_count, wide), 0) == owner
    column = jnp.where(mine, jnp.broadcast_to(column, (row_count, wide)), -1)
    tiles = tiles_ref[...].reshape(wide, tile_size)
    degree = jnp.broadcast_to(degrees_ref[...].astype(jnp.float32), (row_count, row_count))
    diagonal = lax.broadcasted_iota(jnp.int32, (row_count, row_count), 0) == lax.broadcasted_iota(
        jnp.int32, (row_count, row_count), 1
    )
    scale = lax.rsqrt(jnp.sum(jnp.where(diagonal, degree, 0.0), axis=1, keepdims=True))
    for b in range(blocks):
        pick = (column == b).astype(jnp.bfloat16)
        summed = jnp.dot(pick, tiles, preferred_element_type=jnp.float32)
        rows_ref[:, b * tile_size : (b + 1) * tile_size] = (summed * scale).astype(jnp.bfloat16)
    for sent_ref in sent_refs:
        sections, section = lax.axis_size("section"), lax.axis_index("section")
        part = sent_ref.shape[0] - blocks * row_count
        for at in range(sections):

            @pl.when(section == at)
            def _(at=at):
                source = features_ref if at == sections - 1 else rows_ref
                for b in range(blocks):
                    rows = slice(b * row_count, (b + 1) * row_count)
                    sent_ref[rows] = source[:, b * tile_size : (b + 1) * tile_size]
                column, row = nodes + at * part // row_count * tile_size, at * part % row_count
                sent_ref[blocks * row_count :] = features_ref[row : row + part, column : column + tile_size]


def dense_rows(tile_cols, live_tiles, tile_rows, degrees, features, sent_rows):
    row_count = tile_rows.shape[0]
    nodes = row_count * lax.axis_size("shard")
    shapes = [(row_count, nodes)] + ([(sent_rows, tile_rows.shape[2])] if sent_rows else [])
    return pl.pallas_call(
        dense_rows_kernel,
        out_shape=[pltpu.VMEM(shape, jnp.bfloat16) for shape in shapes],
        in_specs=[
            pl.BlockSpec(memory_space=pltpu.SMEM),
            pl.BlockSpec(memory_space=pltpu.SMEM),
            pl.BlockSpec(memory_space=pltpu.VMEM),
            pl.BlockSpec(memory_space=pltpu.VMEM),
            pl.BlockSpec(memory_space=pltpu.VMEM),
        ],
        out_specs=[pl.BlockSpec(memory_space=pltpu.VMEM)] * len(shapes),
        name="dense_rows",
    )(tile_cols, live_tiles, tile_rows, degrees, features)


def split_chain(section):
    masks = [section ^ earlier for earlier in reversed(range(section))]
    count = next((i for i, mask in enumerate(masks) if mask & (mask - 1)), len(masks))
    return masks[:count], masks[count:]


def gathered_rows(pair_refs, mask, first, count):
    first_core = lax.rem(lax.axis_index("shard"), 2) == 0
    found = {}
    for here_ref, there_ref, order in pair_refs[mask]:
        for piece, source in enumerate(order):
            here, there = here_ref[piece, first : first + count], there_ref[piece, first : first + count]
            found[source] = [jnp.where(first_core, here, there), jnp.where(first_core, there, here)]
    return [rows for source in sorted(found) for rows in found[source]]


def times(halves, matrix):
    row_count = halves.shape[0] // 2
    chip, chips = lax.div(lax.axis_index("shard"), 2), len(matrix[0]) // 2
    left = []
    for piece in range(chips):
        source = lax.rem(chip - piece + chips, chips)
        left.append(halves[:, pl.ds(pl.multiple_of(source * 2 * row_count, 128), 2 * row_count)])
    left = jnp.concatenate(left, axis=1)
    right = jnp.concatenate([jnp.concatenate(tile, axis=0) for tile in matrix], axis=1)
    both = jnp.dot(left, right, preferred_element_type=jnp.float32)
    return both[:row_count] + both[row_count:]


def by_mask(refs, orders):
    refs = iter(refs)
    return {mask: [(next(refs), next(refs), order) for order in groups] for mask, groups in orders}


def stacked_tiles(pair_refs, mask, row_count, tiles):
    return [gathered_rows(pair_refs, mask, tile * row_count, row_count) for tile in range(tiles)]


def multiply_through(halves, pair_refs, masks):
    row_count, tiles = halves.shape[0] // 2, halves.shape[1] // 128
    for mask in masks:
        product = times(halves, stacked_tiles(pair_refs, mask, row_count, tiles))
        high = product.astype(jnp.bfloat16)
        halves[:row_count] = high
        halves[row_count:] = (product - high.astype(jnp.float32)).astype(jnp.bfloat16)


def first_kernel(orders, sections, own_ref, *refs):
    pair_refs, halves = by_mask(refs[:-1], orders), refs[-1]
    row_count, nodes = own_ref.shape[0], halves.shape[1]
    halves[:row_count] = own_ref[...]
    halves[row_count:] = jnp.zeros((row_count, nodes), jnp.bfloat16)
    for at in range(sections):
        near, _ = split_chain(at)
        if near:
            pl.when(lax.axis_index("section") == at)(functools.partial(multiply_through, halves, pair_refs, near))


def second_kernel(orders, sections, first_ref, *refs):
    pair_refs, out_ref, halves = by_mask(refs[:-2], orders), refs[-2], refs[-1]
    row_count, nodes = halves.shape[0] // 2, halves.shape[1]
    tiles = nodes // 128
    stacked = tiles * row_count
    part = refs[0].shape[1] - stacked
    halves[...] = first_ref[...]
    for at in range(sections):

        @pl.when(lax.axis_index("section") == at)
        def _(at=at):
            multiply_through(halves, pair_refs, split_chain(at)[1])
            bulk = stacked_tiles(pair_refs, at ^ (sections - 1), row_count, tiles)
            out_ref[:, :nodes] = times(halves, bulk).astype(jnp.bfloat16)
            parts = [gathered_rows(pair_refs, at ^ giver, stacked, part) for giver in range(sections)]
            each = row_count // part
            rest = [
                [jnp.concatenate(rows, axis=0) for rows in zip(*parts[tile : tile + each])]
                for tile in range(0, sections, each)
            ]
            out_ref[:, nodes:] = times(halves, rest).astype(jnp.bfloat16)


def flat(pairs, masks):
    orders = [(mask, [order for order, _ in pairs[mask]]) for mask in masks]
    return orders, [array for mask in masks for _, pair in pairs[mask] for array in pair]


def first_products(own, pairs, nodes, sections):
    orders, operands = flat(pairs, [mask for mask in range(1, sections) if not mask & (mask - 1)])
    return pl.pallas_call(
        functools.partial(first_kernel, orders, sections),
        out_shape=pltpu.VMEM((2 * own.shape[0], nodes), jnp.bfloat16),
        in_specs=[pl.BlockSpec(memory_space=pltpu.VMEM)] * (1 + len(operands)),
        out_specs=pl.BlockSpec(memory_space=pltpu.VMEM),
        compiler_params=pltpu.CompilerParams(vmem_limit_bytes=32 * 1024 * 1024),
        name="first_products",
    )(own, *operands)


def second_products(first, pairs, width, sections):
    orders, operands = flat(pairs, list(range(sections)))
    return pl.pallas_call(
        functools.partial(second_kernel, orders, sections),
        out_shape=jax.ShapeDtypeStruct((first.shape[0] // 2, width), jnp.bfloat16),
        in_specs=[pl.BlockSpec(memory_space=pltpu.VMEM)] * (1 + len(operands)),
        out_specs=pl.BlockSpec(memory_space=pltpu.VMEM),
        scratch_shapes=[pltpu.VMEM(first.shape, jnp.bfloat16)],
        compiler_params=pltpu.CompilerParams(vmem_limit_bytes=32 * 1024 * 1024),
        name="second_products",
    )(first, *operands)


def by_products(own, sent, width):
    sections, shards = lax.axis_size("section"), lax.axis_size("shard")

    def along_shard(value, mask):
        return lax.ppermute(value, "shard", [(i, i ^ mask) for i in range(shards)])

    def along_section(value, mask):
        return lax.ppermute(value, "section", [(i, i ^ mask) for i in range(sections)])

    def along_z(value, groups):
        turns = [[(i, (i + 2 * back) % shards) for i in range(shards)] for back in range(1, shards // 2)]
        came = [value] + [lax.ppermute(value, "shard", turn) for turn in turns]
        return [jnp.stack([came[back] for back in order]) for order in groups]

    whole = [list(range(shards // 2))]
    last_first = [0] + whole[0][:0:-1]
    in_two = [last_first[: shards // 4], last_first[shards // 4 :]]

    ahead = {mask: along_section(sent, mask) for mask in range(1, sections) if mask & (mask - 1)}
    mine, ahead = lax.optimization_barrier((along_z(sent, whole)[0], ahead))
    arrived = [(whole, [mine])]
    for mask in range(1, sections):
        if mask in ahead:
            arrived.append((in_two, along_z(ahead[mask], in_two)))
        else:
            arrived.append((whole, [along_section(mine, mask)]))
    pairs = [[(order, (here, along_shard(here, 1))) for order, here in zip(*group)] for group in arrived]
    first = first_products(own, pairs, own.shape[1], sections)
    return second_products(first, pairs, width, sections)


def by_hops(features, own):
    sections = lax.axis_size("section")
    part = features.shape[1] // sections
    piece = lax.dynamic_slice_in_dim(features, lax.axis_index("section") * part, part, axis=1)
    relations = lax.all_gather(own, "section", axis=0, tiled=False)
    pieces = []
    for hop in range(sections):
        slab = lax.all_gather(piece, "shard", axis=0, tiled=True)
        piece = jnp.dot(relations[hop], slab, preferred_element_type=jnp.float32).astype(jnp.bfloat16)
        pieces.append(piece)
    mine = lax.all_to_all(jnp.stack(pieces), "section", split_axis=0, concat_axis=0, tiled=True)
    return jnp.swapaxes(mine, 0, 1).reshape(features.shape)


def per_device(features, tile_cols, live_tiles, tile_values, degrees):
    row_count, width = features.shape
    sections, shards = lax.axis_size("section"), lax.axis_size("shard")
    nodes = row_count * shards
    tile_size = tile_values.shape[3]
    part = max(width - nodes, 0) // tile_size * row_count // sections
    sent_rows = nodes // tile_size * row_count + part
    even = shards >= 4 and shards & (shards - 1) == 0 and sections > 1 and sections & (sections - 1) == 0
    parts = part >= 16 and part % 16 == 0 and row_count % part == 0 and tile_size == 128
    whole = part * sections * tile_size == (width - nodes) * row_count
    if even and parts and whole:
        own, sent = dense_rows(tile_cols, live_tiles, tile_values[0], degrees, features, sent_rows)
        return by_products(own, sent, width)[None]
    (own,) = dense_rows(tile_cols, live_tiles, tile_values[0], degrees, features, 0)
    return by_hops(features, own)[None]


def solution(mesh):
    in_specs = (
        P("shard", None),
        P("section", None, None),
        P("section", None),
        P("section", "shard", None, None),
        P("section", "shard"),
    )
    out_specs = P("section", "shard", None)
    return jax.shard_map(
        per_device, mesh=mesh, in_specs=in_specs, out_specs=out_specs, check_vma=False
    )
```

```python
import functools

import jax
import jax.numpy as jnp
from jax import lax
from jax.experimental import pallas as pl
from jax.experimental.pallas import tpu as pltpu
from jax.sharding import PartitionSpec as P


def dense_rows_kernel(cols_ref, live_ref, tiles_ref, degrees_ref, features_ref, rows_ref, *sent_refs):
    row_count, slots, tile_size = tiles_ref.shape
    nodes = rows_ref.shape[1]
    blocks = nodes // tile_size
    block_row = lax.axis_index("shard") * row_count // tile_size
    live = live_ref[0, block_row]
    wide = row_count * slots
    slot = lax.rem(lax.broadcasted_iota(jnp.int32, (1, wide), 1), slots)
    column = jnp.full((1, wide), -1, jnp.int32)
    for k in range(slots):
        column = jnp.where(slot == k, jnp.where(k < live, cols_ref[0, block_row, k], -1), column)
    owner = lax.div(lax.broadcasted_iota(jnp.int32, (row_count, wide), 1), slots)
    mine = lax.broadcasted_iota(jnp.int32, (row_count, wide), 0) == owner
    column = jnp.where(mine, jnp.broadcast_to(column, (row_count, wide)), -1)
    tiles = tiles_ref[...].reshape(wide, tile_size)
    degree = jnp.broadcast_to(degrees_ref[...].astype(jnp.float32), (row_count, row_count))
    diagonal = lax.broadcasted_iota(jnp.int32, (row_count, row_count), 0) == lax.broadcasted_iota(
        jnp.int32, (row_count, row_count), 1
    )
    scale = lax.rsqrt(jnp.sum(jnp.where(diagonal, degree, 0.0), axis=1, keepdims=True))
    for b in range(blocks):
        pick = (column == b).astype(jnp.bfloat16)
        summed = jnp.dot(pick, tiles, preferred_element_type=jnp.float32)
        rows_ref[:, b * tile_size : (b + 1) * tile_size] = (summed * scale).astype(jnp.bfloat16)
    for sent_ref in sent_refs:
        sections, section = lax.axis_size("section"), lax.axis_index("section")
        part = sent_ref.shape[0] - blocks * row_count
        for at in range(sections):

            @pl.when(section == at)
            def _(at=at):
                source = features_ref if at == sections - 1 else rows_ref
                for b in range(blocks):
                    rows = slice(b * row_count, (b + 1) * row_count)
                    sent_ref[rows] = source[:, b * tile_size : (b + 1) * tile_size]
                column, row = nodes + at * part // row_count * tile_size, at * part % row_count
                sent_ref[blocks * row_count :] = features_ref[row : row + part, column : column + tile_size]


def dense_rows(tile_cols, live_tiles, tile_rows, degrees, features, sent_rows):
    row_count = tile_rows.shape[0]
    nodes = row_count * lax.axis_size("shard")
    shapes = [(row_count, nodes)] + ([(sent_rows, tile_rows.shape[2])] if sent_rows else [])
    return pl.pallas_call(
        dense_rows_kernel,
        out_shape=[pltpu.VMEM(shape, jnp.bfloat16) for shape in shapes],
        in_specs=[
            pl.BlockSpec(memory_space=pltpu.SMEM),
            pl.BlockSpec(memory_space=pltpu.SMEM),
            pl.BlockSpec(memory_space=pltpu.VMEM),
            pl.BlockSpec(memory_space=pltpu.VMEM),
            pl.BlockSpec(memory_space=pltpu.VMEM),
        ],
        out_specs=[pl.BlockSpec(memory_space=pltpu.VMEM)] * len(shapes),
        name="dense_rows",
    )(tile_cols, live_tiles, tile_rows, degrees, features)


def split_chain(section):
    masks = [section ^ earlier for earlier in reversed(range(section))]
    count = next((i for i, mask in enumerate(masks) if mask & (mask - 1)), len(masks))
    return masks[:count], masks[count:]


def gathered_rows(pair_refs, mask, first, count):
    first_core = lax.rem(lax.axis_index("shard"), 2) == 0
    found = {}
    for here_ref, there_ref, order in pair_refs[mask]:
        for piece, source in enumerate(order):
            here, there = here_ref[piece, first : first + count], there_ref[piece, first : first + count]
            found[source] = [jnp.where(first_core, here, there), jnp.where(first_core, there, here)]
    return [rows for source in sorted(found) for rows in found[source]]


def times(halves, matrix):
    row_count = halves.shape[0] // 2
    chip, chips = lax.div(lax.axis_index("shard"), 2), len(matrix[0]) // 2
    left = []
    for piece in range(chips):
        source = lax.bitwise_xor(chip, piece)
        left.append(halves[:, pl.ds(pl.multiple_of(source * 2 * row_count, 128), 2 * row_count)])
    left = jnp.concatenate(left, axis=1)
    right = jnp.concatenate([jnp.concatenate(tile, axis=0) for tile in matrix], axis=1)
    both = jnp.dot(left, right, preferred_element_type=jnp.float32)
    return both[:row_count] + both[row_count:]


def by_mask(refs, orders):
    refs = iter(refs)
    return {mask: [(next(refs), next(refs), order) for order in groups] for mask, groups in orders}


def stacked_tiles(pair_refs, mask, row_count, tiles):
    return [gathered_rows(pair_refs, mask, tile * row_count, row_count) for tile in range(tiles)]


def multiply_through(halves, pair_refs, masks):
    row_count, tiles = halves.shape[0] // 2, halves.shape[1] // 128
    for mask in masks:
        product = times(halves, stacked_tiles(pair_refs, mask, row_count, tiles))
        high = product.astype(jnp.bfloat16)
        halves[:row_count] = high
        halves[row_count:] = (product - high.astype(jnp.float32)).astype(jnp.bfloat16)


def first_kernel(orders, sections, own_ref, *refs):
    pair_refs, halves = by_mask(refs[:-1], orders), refs[-1]
    row_count, nodes = own_ref.shape[0], halves.shape[1]
    halves[:row_count] = own_ref[...]
    halves[row_count:] = jnp.zeros((row_count, nodes), jnp.bfloat16)
    for at in range(sections):
        near, _ = split_chain(at)
        if near:
            pl.when(lax.axis_index("section") == at)(functools.partial(multiply_through, halves, pair_refs, near))


def second_kernel(orders, sections, first_ref, *refs):
    pair_refs, out_ref, halves = by_mask(refs[:-2], orders), refs[-2], refs[-1]
    row_count, nodes = halves.shape[0] // 2, halves.shape[1]
    tiles = nodes // 128
    stacked = tiles * row_count
    part = refs[0].shape[1] - stacked
    halves[...] = first_ref[...]
    for at in range(sections):

        @pl.when(lax.axis_index("section") == at)
        def _(at=at):
            multiply_through(halves, pair_refs, split_chain(at)[1])
            bulk = stacked_tiles(pair_refs, at ^ (sections - 1), row_count, tiles)
            out_ref[:, :nodes] = times(halves, bulk).astype(jnp.bfloat16)
            parts = [gathered_rows(pair_refs, at ^ giver, stacked, part) for giver in range(sections)]
            each = row_count // part
            rest = [
                [jnp.concatenate(rows, axis=0) for rows in zip(*parts[tile : tile + each])]
                for tile in range(0, sections, each)
            ]
            out_ref[:, nodes:] = times(halves, rest).astype(jnp.bfloat16)


def flat(pairs, masks):
    orders = [(mask, [order for order, _ in pairs[mask]]) for mask in masks]
    return orders, [array for mask in masks for _, pair in pairs[mask] for array in pair]


def first_products(own, pairs, nodes, sections):
    orders, operands = flat(pairs, [mask for mask in range(1, sections) if not mask & (mask - 1)])
    return pl.pallas_call(
        functools.partial(first_kernel, orders, sections),
        out_shape=pltpu.VMEM((2 * own.shape[0], nodes), jnp.bfloat16),
        in_specs=[pl.BlockSpec(memory_space=pltpu.VMEM)] * (1 + len(operands)),
        out_specs=pl.BlockSpec(memory_space=pltpu.VMEM),
        compiler_params=pltpu.CompilerParams(vmem_limit_bytes=32 * 1024 * 1024),
        name="first_products",
    )(own, *operands)


def second_products(first, pairs, width, sections):
    orders, operands = flat(pairs, list(range(sections)))
    return pl.pallas_call(
        functools.partial(second_kernel, orders, sections),
        out_shape=jax.ShapeDtypeStruct((first.shape[0] // 2, width), jnp.bfloat16),
        in_specs=[pl.BlockSpec(memory_space=pltpu.VMEM)] * (1 + len(operands)),
        out_specs=pl.BlockSpec(memory_space=pltpu.VMEM),
        scratch_shapes=[pltpu.VMEM(first.shape, jnp.bfloat16)],
        compiler_params=pltpu.CompilerParams(vmem_limit_bytes=32 * 1024 * 1024),
        name="second_products",
    )(first, *operands)


def by_products(own, sent, width):
    sections, shards = lax.axis_size("section"), lax.axis_size("shard")

    def along_shard(value, mask):
        return lax.ppermute(value, "shard", [(i, i ^ mask) for i in range(shards)])

    def along_section(value, mask):
        return lax.ppermute(value, "section", [(i, i ^ mask) for i in range(sections)])

    def along_z(value, groups):
        came = [value] + [along_shard(value, 2 * mask) for mask in range(1, shards // 2)]
        return [jnp.stack([came[mask] for mask in order]) for order in groups]

    whole = [list(range(shards // 2))]
    last_first = [0] + whole[0][:0:-1]
    in_two = [last_first[:-1], last_first[-1:]]

    ahead = {mask: along_section(sent, mask) for mask in range(1, sections) if mask & (mask - 1)}
    mine, ahead = lax.optimization_barrier((along_z(sent, whole)[0], ahead))
    arrived = [(whole, [mine])]
    for mask in range(1, sections):
        if mask in ahead:
            arrived.append((in_two, along_z(ahead[mask], in_two)))
        else:
            arrived.append((whole, [along_section(mine, mask)]))
    pairs = [[(order, (here, along_shard(here, 1))) for order, here in zip(*group)] for group in arrived]
    first = first_products(own, pairs, own.shape[1], sections)
    return second_products(first, pairs, width, sections)


def by_hops(features, own):
    sections = lax.axis_size("section")
    part = features.shape[1] // sections
    piece = lax.dynamic_slice_in_dim(features, lax.axis_index("section") * part, part, axis=1)
    relations = lax.all_gather(own, "section", axis=0, tiled=False)
    pieces = []
    for hop in range(sections):
        slab = lax.all_gather(piece, "shard", axis=0, tiled=True)
        piece = jnp.dot(relations[hop], slab, preferred_element_type=jnp.float32).astype(jnp.bfloat16)
        pieces.append(piece)
    mine = lax.all_to_all(jnp.stack(pieces), "section", split_axis=0, concat_axis=0, tiled=True)
    return jnp.swapaxes(mine, 0, 1).reshape(features.shape)


def per_device(features, tile_cols, live_tiles, tile_values, degrees):
    row_count, width = features.shape
    sections, shards = lax.axis_size("section"), lax.axis_size("shard")
    nodes = row_count * shards
    tile_size = tile_values.shape[3]
    part = max(width - nodes, 0) // tile_size * row_count // sections
    sent_rows = nodes // tile_size * row_count + part
    even = shards >= 4 and shards & (shards - 1) == 0 and sections > 1 and sections & (sections - 1) == 0
    parts = part >= 16 and part % 16 == 0 and row_count % part == 0 and tile_size == 128
    whole = part * sections * tile_size == (width - nodes) * row_count
    if even and parts and whole:
        own, sent = dense_rows(tile_cols, live_tiles, tile_values[0], degrees, features, sent_rows)
        return by_products(own, sent, width)[None]
    (own,) = dense_rows(tile_cols, live_tiles, tile_values[0], degrees, features, 0)
    return by_hops(features, own)[None]


def solution(mesh):
    in_specs = (
        P("shard", None),
        P("section", None, None),
        P("section", None),
        P("section", "shard", None, None),
        P("section", "shard"),
    )
    out_specs = P("section", "shard", None)
    return jax.shard_map(
        per_device, mesh=mesh, in_specs=in_specs, out_specs=out_specs, check_vma=False
    )
```

```python
import functools

import jax
import jax.numpy as jnp
from jax import lax
from jax.experimental import pallas as pl
from jax.experimental.pallas import tpu as pltpu
from jax.sharding import PartitionSpec as P


def dense_rows_kernel(cols_ref, live_ref, tiles_ref, degrees_ref, features_ref, rows_ref, *sent_refs):
    row_count, slots, tile_size = tiles_ref.shape
    nodes = rows_ref.shape[1]
    blocks = nodes // tile_size
    block_row = lax.axis_index("shard") * row_count // tile_size
    live = live_ref[0, block_row]
    wide = row_count * slots
    slot = lax.rem(lax.broadcasted_iota(jnp.int32, (1, wide), 1), slots)
    column = jnp.full((1, wide), -1, jnp.int32)
    for k in range(slots):
        column = jnp.where(slot == k, jnp.where(k < live, cols_ref[0, block_row, k], -1), column)
    owner = lax.div(lax.broadcasted_iota(jnp.int32, (row_count, wide), 1), slots)
    mine = lax.broadcasted_iota(jnp.int32, (row_count, wide), 0) == owner
    column = jnp.where(mine, jnp.broadcast_to(column, (row_count, wide)), -1)
    tiles = tiles_ref[...].reshape(wide, tile_size)
    degree = jnp.broadcast_to(degrees_ref[...].astype(jnp.float32), (row_count, row_count))
    diagonal = lax.broadcasted_iota(jnp.int32, (row_count, row_count), 0) == lax.broadcasted_iota(
        jnp.int32, (row_count, row_count), 1
    )
    scale = lax.rsqrt(jnp.sum(jnp.where(diagonal, degree, 0.0), axis=1, keepdims=True))
    for b in range(blocks):
        pick = (column == b).astype(jnp.bfloat16)
        summed = jnp.dot(pick, tiles, preferred_element_type=jnp.float32)
        rows_ref[:, b * tile_size : (b + 1) * tile_size] = (summed * scale).astype(jnp.bfloat16)
    for sent_ref in sent_refs:
        sections, section = lax.axis_size("section"), lax.axis_index("section")
        part = sent_ref.shape[0] - blocks * row_count
        for at in range(sections):

            @pl.when(section == at)
            def _(at=at):
                source = features_ref if at == sections - 1 else rows_ref
                for b in range(blocks):
                    rows = slice(b * row_count, (b + 1) * row_count)
                    sent_ref[rows] = source[:, b * tile_size : (b + 1) * tile_size]
                column, row = nodes + at * part // row_count * tile_size, at * part % row_count
                sent_ref[blocks * row_count :] = features_ref[row : row + part, column : column + tile_size]


def dense_rows(tile_cols, live_tiles, tile_rows, degrees, features, sent_rows):
    row_count = tile_rows.shape[0]
    nodes = row_count * lax.axis_size("shard")
    shapes = [(row_count, nodes)] + ([(sent_rows, tile_rows.shape[2])] if sent_rows else [])
    return pl.pallas_call(
        dense_rows_kernel,
        out_shape=[pltpu.VMEM(shape, jnp.bfloat16) for shape in shapes],
        in_specs=[
            pl.BlockSpec(memory_space=pltpu.SMEM),
            pl.BlockSpec(memory_space=pltpu.SMEM),
            pl.BlockSpec(memory_space=pltpu.VMEM),
            pl.BlockSpec(memory_space=pltpu.VMEM),
            pl.BlockSpec(memory_space=pltpu.VMEM),
        ],
        out_specs=[pl.BlockSpec(memory_space=pltpu.VMEM)] * len(shapes),
        name="dense_rows",
    )(tile_cols, live_tiles, tile_rows, degrees, features)


def split_chain(section):
    masks = [section ^ earlier for earlier in reversed(range(section))]
    count = next((i for i, mask in enumerate(masks) if mask & (mask - 1)), len(masks))
    return masks[:count], masks[count:]


def gathered_rows(pair_refs, mask, first, count):
    first_core = lax.rem(lax.axis_index("shard"), 2) == 0
    found = {}
    for here_ref, there_ref, order in pair_refs[mask]:
        for piece, source in enumerate(order):
            here, there = here_ref[piece, first : first + count], there_ref[piece, first : first + count]
            found[source] = [jnp.where(first_core, here, there), jnp.where(first_core, there, here)]
    return [rows for source in sorted(found) for rows in found[source]]


def times(halves, matrix):
    row_count = halves.shape[0] // 2
    chip, chips = lax.div(lax.axis_index("shard"), 2), len(matrix[0]) // 2
    left = []
    for piece in range(chips):
        source = lax.bitwise_xor(chip, piece)
        left.append(halves[:, pl.ds(pl.multiple_of(source * 2 * row_count, 128), 2 * row_count)])
    left = jnp.concatenate(left, axis=1)
    right = jnp.concatenate([jnp.concatenate(tile, axis=0) for tile in matrix], axis=1)
    both = jnp.dot(left, right, preferred_element_type=jnp.float32)
    return both[:row_count] + both[row_count:]


def by_mask(refs, orders):
    refs = iter(refs)
    return {mask: [(next(refs), next(refs), order) for order in groups] for mask, groups in orders}


def stacked_tiles(pair_refs, mask, row_count, tiles):
    return [gathered_rows(pair_refs, mask, tile * row_count, row_count) for tile in range(tiles)]


def multiply_through(halves, pair_refs, masks):
    row_count, tiles = halves.shape[0] // 2, halves.shape[1] // 128
    for mask in masks:
        product = times(halves, stacked_tiles(pair_refs, mask, row_count, tiles))
        high = product.astype(jnp.bfloat16)
        halves[:row_count] = high
        halves[row_count:] = (product - high.astype(jnp.float32)).astype(jnp.bfloat16)


def first_kernel(orders, sections, own_ref, *refs):
    pair_refs, halves = by_mask(refs[:-1], orders), refs[-1]
    row_count, nodes = own_ref.shape[0], halves.shape[1]
    halves[:row_count] = own_ref[...]
    halves[row_count:] = jnp.zeros((row_count, nodes), jnp.bfloat16)
    for at in range(sections):
        near, _ = split_chain(at)
        if near:
            pl.when(lax.axis_index("section") == at)(functools.partial(multiply_through, halves, pair_refs, near))


def second_kernel(orders, sections, first_ref, *refs):
    pair_refs, out_ref, halves = by_mask(refs[:-2], orders), refs[-2], refs[-1]
    row_count, nodes = halves.shape[0] // 2, halves.shape[1]
    tiles = nodes // 128
    stacked = tiles * row_count
    part = refs[0].shape[1] - stacked
    halves[...] = first_ref[...]
    for at in range(sections):

        @pl.when(lax.axis_index("section") == at)
        def _(at=at):
            multiply_through(halves, pair_refs, split_chain(at)[1])
            bulk = stacked_tiles(pair_refs, at ^ (sections - 1), row_count, tiles)
            out_ref[:, :nodes] = times(halves, bulk).astype(jnp.bfloat16)
            parts = [gathered_rows(pair_refs, at ^ giver, stacked, part) for giver in range(sections)]
            each = row_count // part
            rest = [
                [jnp.concatenate(rows, axis=0) for rows in zip(*parts[tile : tile + each])]
                for tile in range(0, sections, each)
            ]
            out_ref[:, nodes:] = times(halves, rest).astype(jnp.bfloat16)


def flat(pairs, masks):
    orders = [(mask, [order for order, _ in pairs[mask]]) for mask in masks]
    return orders, [array for mask in masks for _, pair in pairs[mask] for array in pair]


def first_products(own, pairs, nodes, sections):
    orders, operands = flat(pairs, [mask for mask in range(1, sections) if not mask & (mask - 1)])
    return pl.pallas_call(
        functools.partial(first_kernel, orders, sections),
        out_shape=pltpu.VMEM((2 * own.shape[0], nodes), jnp.bfloat16),
        in_specs=[pl.BlockSpec(memory_space=pltpu.VMEM)] * (1 + len(operands)),
        out_specs=pl.BlockSpec(memory_space=pltpu.VMEM),
        compiler_params=pltpu.CompilerParams(vmem_limit_bytes=32 * 1024 * 1024),
        name="first_products",
    )(own, *operands)


def second_products(first, pairs, width, sections):
    orders, operands = flat(pairs, list(range(sections)))
    return pl.pallas_call(
        functools.partial(second_kernel, orders, sections),
        out_shape=jax.ShapeDtypeStruct((first.shape[0] // 2, width), jnp.bfloat16),
        in_specs=[pl.BlockSpec(memory_space=pltpu.VMEM)] * (1 + len(operands)),
        out_specs=pl.BlockSpec(memory_space=pltpu.VMEM),
        scratch_shapes=[pltpu.VMEM(first.shape, jnp.bfloat16)],
        compiler_params=pltpu.CompilerParams(vmem_limit_bytes=32 * 1024 * 1024),
        name="second_products",
    )(first, *operands)


def by_products(own, sent, width):
    sections, shards = lax.axis_size("section"), lax.axis_size("shard")

    def along_shard(value, mask):
        return lax.ppermute(value, "shard", [(i, i ^ mask) for i in range(shards)])

    def along_section(value, mask):
        return lax.ppermute(value, "section", [(i, i ^ mask) for i in range(sections)])

    def along_z(value, groups):
        came = [value] + [along_shard(value, 2 * mask) for mask in range(1, shards // 2)]
        return [jnp.stack([came[mask] for mask in order]) for order in groups]

    whole = [list(range(shards // 2))]
    last_first = [0] + whole[0][:0:-1]
    in_two = [last_first[: shards // 4], last_first[shards // 4 :]]

    ahead = {mask: along_section(sent, mask) for mask in range(1, sections) if mask & (mask - 1)}
    mine, ahead = lax.optimization_barrier((along_z(sent, whole)[0], ahead))
    arrived = {0: (whole, [mine])}
    for mask in reversed(range(1, sections)):
        if mask in ahead:
            arrived[mask] = (in_two, along_z(ahead[mask], in_two))
        else:
            arrived[mask] = (whole, [along_section(mine, mask)])
    arrived = [arrived[mask] for mask in range(sections)]
    pairs = [[(order, (here, along_shard(here, 1))) for order, here in zip(*group)] for group in arrived]
    first = first_products(own, pairs, own.shape[1], sections)
    return second_products(first, pairs, width, sections)


def by_hops(features, own):
    sections = lax.axis_size("section")
    part = features.shape[1] // sections
    piece = lax.dynamic_slice_in_dim(features, lax.axis_index("section") * part, part, axis=1)
    relations = lax.all_gather(own, "section", axis=0, tiled=False)
    pieces = []
    for hop in range(sections):
        slab = lax.all_gather(piece, "shard", axis=0, tiled=True)
        piece = jnp.dot(relations[hop], slab, preferred_element_type=jnp.float32).astype(jnp.bfloat16)
        pieces.append(piece)
    mine = lax.all_to_all(jnp.stack(pieces), "section", split_axis=0, concat_axis=0, tiled=True)
    return jnp.swapaxes(mine, 0, 1).reshape(features.shape)


def per_device(features, tile_cols, live_tiles, tile_values, degrees):
    row_count, width = features.shape
    sections, shards = lax.axis_size("section"), lax.axis_size("shard")
    nodes = row_count * shards
    tile_size = tile_values.shape[3]
    part = max(width - nodes, 0) // tile_size * row_count // sections
    sent_rows = nodes // tile_size * row_count + part
    even = shards >= 4 and shards & (shards - 1) == 0 and sections > 1 and sections & (sections - 1) == 0
    parts = part >= 16 and part % 16 == 0 and row_count % part == 0 and tile_size == 128
    whole = part * sections * tile_size == (width - nodes) * row_count
    if even and parts and whole:
        own, sent = dense_rows(tile_cols, live_tiles, tile_values[0], degrees, features, sent_rows)
        return by_products(own, sent, width)[None]
    (own,) = dense_rows(tile_cols, live_tiles, tile_values[0], degrees, features, 0)
    return by_hops(features, own)[None]


def solution(mesh):
    in_specs = (
        P("shard", None),
        P("section", None, None),
        P("section", None),
        P("section", "shard", None, None),
        P("section", "shard"),
    )
    out_specs = P("section", "shard", None)
    return jax.shard_map(
        per_device, mesh=mesh, in_specs=in_specs, out_specs=out_specs, check_vma=False
    )
```
